32 devices in a mesh: serve: 8 (over y, x, core), tensor: 4 (over z).
Axes of the slice: x: 2, y: 2, z: 4, core: 2. Of those that a mesh axis runs over, the one named last changes fastest.
Arguments:
- queries: bfloat16 [8192, 4096], P('serve', 'tensor'), may hold values from -8 to 8
- kv_cache: bfloat16 [8, 6400, 256], P('serve', 'tensor'), may hold values from -6 to 6
- question_slot: int32 [256], P('serve'), may hold values from 0 to 3, as said below
- question_len: int32 [256], P('serve'), may hold values from 1 to 32, 5120 in all
- out_weight: bfloat16 [4096, 8192], P(None, 'tensor'), may hold values from -0.375 to 0.375
Outputs:
- answers: bfloat16 [8192, 8192], P('serve', 'tensor')
The draws below stay inside these ranges and needn't reach their ends.
Inputs may be any that keep to these rules, and one draw needn't show every extreme that they name: Question q of serving group g asks about the image held by serving group (g - question_slot[q]) mod 8; among one serving group's 32 questions every value 0 to 3 occurs exactly 32 / 4 times.
All inputs are finite; a program needn't handle non-finite values. No bound on the sum of `question_len` on one device may be relied on, other than what follows from the above.
Results may differ from the reference program's by a relative error of at most 0.0058.
Values may be sent and summed in bfloat16 or wider, within the bound.
No kernel may reach another device: no remote copies, remote signals or barrier semaphores. Data moves between devices by JAX's collectives and lax.ppermute only.
A program may use at most 128 MiB of HBM per device.

```python
import math
import jax
import jax.numpy as jnp
import numpy as np
from jax import lax

D = 8192
HEADS = 32
KVH = 4
HEAD_DIM = 128
P_SIZE = 1600
Q_GRP = 32
QLEN = 32
NEED = 4
IMAGES = 8
QUESTIONS = 256
ROWS = 8192
N_SERVE = 8


def slot_values(key):
    group_keys = jax.random.split(jax.random.fold_in(key, 17), IMAGES)
    base_slots = (jnp.arange(Q_GRP, dtype=jnp.int32) % NEED).astype(jnp.int32)
    shuffled = jax.vmap(lambda one_key: jax.random.permutation(one_key, base_slots))(group_keys)
    return shuffled.reshape(QUESTIONS).astype(jnp.int32)


def draw_question_slot(key, part):
    return slot_values(key)


def draw_queries(key, part):
    base = 2.0 * jax.random.normal(jax.random.fold_in(key, 23), (ROWS, HEADS * HEAD_DIM), jnp.float32)
    base = jnp.clip(base, -8.0, 8.0)
    return base.astype(jnp.bfloat16)


def draw_kv_cache(key, part):
    base = jax.random.normal(jax.random.fold_in(key, 29), (IMAGES, KVH, P_SIZE, 2 * HEAD_DIM), jnp.float32)
    base = jnp.clip(base, -6.0, 6.0)
    return base.reshape(IMAGES, KVH * P_SIZE, 2 * HEAD_DIM).astype(jnp.bfloat16)


def block_scale(rng, dims, shards, low, top_value):
    level = 1.0
    for dim, parts in shards:
        draws = jax.random.uniform(jax.random.fold_in(jax.random.fold_in(rng, 6), dim), (parts,), jnp.float32, low / len(shards), top_value / len(shards))
        level = level * jnp.repeat(jnp.exp(draws), dims[dim] // parts).reshape((-1,) + (1,) * (len(dims) - 1 - dim))
    return level


def profile(amount, total, limit, skew):
    portions = [(1 << 20) // math.isqrt(standing ** skew) + 1 for standing in range(2, amount + 1)]
    spare, counts = total - limit - (amount - 1), [1] * (amount - 1)
    while spare > 0:
        movable = [i for i in range(amount - 1) if counts[i] < limit]
        pool, budget = sum([portions[i] for i in movable]), spare
        for i in movable:
            addition = min(limit - counts[i], max(1, budget * portions[i] // pool), spare)
            counts[i] = counts[i] + addition
            spare = spare - addition
    return np.array([limit] + counts)


def ragged_sizes(stream_key, count, total, most, lean):
    if count == 2:
        one = jax.random.randint(stream_key, (), max(1, total - most), min(most, total - 1) + 1)
        return jnp.stack([one, total - one])
    lengths = jnp.asarray(profile(count, total, most, lean), jnp.int32)
    twos = (count - 1) // 2
    source_of, taker = lengths[1:1 + 2 * twos:2], lengths[2:2 + 2 * twos:2]
    room = jnp.minimum(source_of - 1, most - taker)
    shifted = jax.random.randint(jax.random.fold_in(stream_key, 1), (twos,), 0, 1 << 20) % (room + 1)
    lengths = lengths.at[1:1 + 2 * twos:2].set(source_of - shifted).at[2:2 + 2 * twos:2].set(taker + shifted)
    return lengths[jax.random.permutation(jax.random.fold_in(stream_key, 2), count)]


def bell_draw(own_key, extent, width, limit, cuts=(), kind=jnp.bfloat16):
    values = jax.random.normal(own_key, extent, jnp.float32) * width
    if len(cuts) > 0:
        values = block_scale(own_key, extent, cuts, -0.22, 0.18) * values
    return jnp.clip(values, min=-limit, max=limit).astype(kind)


def setup_inputs(seed: int = 0) -> dict:
    arg_keys = jax.random.split(jax.random.key(seed), 6)
    queries = draw_queries(jax.random.fold_in(arg_keys[5], 71), 0)
    kv_cache = draw_kv_cache(jax.random.fold_in(arg_keys[5], 71), 0)
    question_slot = draw_question_slot(jax.random.fold_in(arg_keys[5], 71), 0)
    question_len = ragged_sizes(arg_keys[3], QUESTIONS, QUESTIONS * QLEN * 5 // 8, QLEN, 2).astype(jnp.int32)
    out_weight = bell_draw(arg_keys[4], (HEADS * HEAD_DIM, D), (HEADS * HEAD_DIM // 16) ** -0.5, 0.375, ((1, 4),))
    return {"queries": queries, "kv_cache": kv_cache, "question_slot": question_slot, "question_len": question_len, "out_weight": out_weight}


def attend_one(query_rows, key_value):
    head_dim = key_value.shape[2] // 2
    grouped = query_rows.reshape(query_rows.shape[0], key_value.shape[0], -1, head_dim)
    key_part = key_value[:, :, :head_dim]
    value_part = key_value[:, :, head_dim:]
    scores = jnp.einsum("rkgd,kpd->kgrp", grouped, key_part, precision=lax.Precision.HIGHEST) * (head_dim ** -0.5)
    row_max = jnp.max(scores, axis=3, keepdims=True)
    exp_scores = jnp.exp(scores - row_max)
    sum_exp = jnp.sum(exp_scores, axis=3, keepdims=True)
    weights = lax.optimization_barrier((exp_scores / sum_exp).astype(jnp.bfloat16)).astype(jnp.float32)
    blended = jnp.einsum("kgrp,kpd->rkgd", weights, value_part, precision=lax.Precision.HIGHEST)
    return blended.reshape(query_rows.shape[0], -1)


def reference(queries, kv_cache, question_slot, question_len, out_weight):
    row_count = queries.shape[0]
    question_count = row_count // QLEN
    owner_group = (jnp.arange(question_count, dtype=jnp.int32) // Q_GRP - question_slot) % N_SERVE
    owner_group = owner_group.astype(jnp.int32)
    per_question = queries.reshape(question_count, QLEN, queries.shape[1])

    def one_question(packed):
        query_rows, image_index, length = packed
        key_value = lax.dynamic_index_in_dim(kv_cache, image_index, 0, keepdims=False)
        key_value = key_value.reshape(KVH, -1, key_value.shape[1]).astype(jnp.float32)
        blended = attend_one(query_rows.astype(jnp.float32), key_value)
        live_rows = jnp.arange(QLEN, dtype=jnp.int32) < length
        return jnp.where(live_rows[:, None], blended, jnp.float32(0.0)).astype(jnp.bfloat16)

    attended = lax.map(one_question, (per_question, owner_group, question_len))
    attended = attended.reshape(row_count, queries.shape[1])
    return jnp.dot(attended, out_weight, preferred_element_type=jnp.float32).astype(jnp.bfloat16)
```

```python
import functools

import jax
import jax.numpy as jnp
from jax import lax
from jax.experimental import pallas as pl
from jax.experimental.pallas import tpu as pltpu
from jax.sharding import PartitionSpec as P

KVH = 4
P_SIZE = 1600
QLEN = 32
NEED = 4
LOG2E = 1.4426950408889634
MIB = 1 << 20
F32 = jnp.float32
BF16 = jnp.bfloat16


def swapped(shard, axis, bit):
    return lax.ppermute(shard, axis, [(i, i ^ 1 << bit) for i in range(lax.axis_size(axis))])


def shifted(value, axis, steps):
    count = lax.axis_size(axis)
    pairs = [(source, (source + steps) % count) for source in range(count)]
    return lax.ppermute(value, axis, pairs)


def attend(query_rows, key_value):
    row_count = query_rows.shape[0]
    head_count = key_value.shape[0]
    head_dim = key_value.shape[2] // 2
    grouped = query_rows.reshape(row_count, head_count, -1, head_dim)
    key_part = key_value[:, :, :head_dim]
    value_part = key_value[:, :, head_dim:]
    scores = jnp.einsum(
        "rkgd,kpd->kgrp", grouped, key_part, preferred_element_type=jnp.float32
    ) * head_dim ** (-0.5)
    row_max = jnp.max(scores, axis=3, keepdims=True)
    exp_scores = jnp.exp(scores - row_max)
    sum_exp = jnp.sum(exp_scores, axis=3, keepdims=True)
    weights = (exp_scores / sum_exp).astype(jnp.bfloat16)
    blended = jnp.einsum("kgrp,kpd->rkgd", weights, value_part, preferred_element_type=jnp.float32)
    return blended.reshape(row_count, -1)


def on_device_general(queries, kv_cache, question_slot, question_len, out_weight):
    row_count, col_count = queries.shape
    head_dim = kv_cache.shape[2] // 2
    question_count = row_count // QLEN
    per_slot = question_count // NEED
    head_piece = kv_cache[0]
    sharing = lax.axis_size("tensor") // KVH
    if sharing > 1:
        for bit_number in range(sharing.bit_length() - 1):
            partner_piece = swapped(head_piece, "tensor", bit_number)
            upper_member = lax.axis_index("tensor") // 2**bit_number % 2 == 1
            head_piece = jnp.where(
                upper_member,
                jnp.concatenate([partner_piece, head_piece], axis=0),
                jnp.concatenate([head_piece, partner_piece], axis=0),
            )
    key_value = head_piece.reshape(-1, P_SIZE, 2 * head_dim)
    ordering = jnp.argsort(question_slot, stable=True)
    inverse_order = jnp.argsort(ordering, stable=True)
    sorted_rows = queries.reshape(question_count, QLEN, col_count)[ordering]
    sorted_rows = sorted_rows.reshape(NEED, per_slot * QLEN, col_count)
    results = []
    for offset_back in range(NEED):
        if offset_back == 0:
            remote = key_value
        else:
            remote = shifted(key_value, "serve", offset_back)
        results.append(attend(sorted_rows[offset_back], remote))
    sorted_out = jnp.stack(results).reshape(question_count, QLEN, col_count)
    blended = sorted_out[inverse_order].reshape(row_count, col_count)
    token_pos = jnp.arange(row_count, dtype=jnp.int32) % QLEN
    live_rows = token_pos < jnp.repeat(question_len, QLEN, total_repeat_length=row_count)
    attended = jnp.where(live_rows[:, None], blended, 0.0).astype(jnp.bfloat16)
    zero_sum = jnp.zeros((row_count, out_weight.shape[1]), jnp.float32)
    gathered_cols = lax.all_gather(attended, "tensor", axis=1, tiled=True)
    weight_rows = lax.slice_in_dim(out_weight, 0, gathered_cols.shape[1], axis=0)
    answers = zero_sum + jnp.dot(gathered_cols, weight_rows, preferred_element_type=jnp.float32)
    return answers.astype(jnp.bfloat16)


def make_plan(info_ref, slot_ref, len_ref, plan_ref, work_ref):
    count = slot_ref.shape[0]
    per = count // NEED
    half = per * QLEN // 2
    odd = info_ref[1]
    for g in range(NEED):
        work_ref[g] = g * per
        work_ref[NEED + g] = 0

    def step(q, carry):
        slot = slot_ref[q]
        length = len_ref[q]
        last = jnp.where(slot == 1, 3 - odd, 2 + odd)
        seg = jnp.where(slot == 0, 0, jnp.where(slot == 2, 1, last))
        at = work_ref[seg]
        first = work_ref[NEED + seg]
        plan_ref[at] = q
        plan_ref[count + at] = first
        plan_ref[2 * count + at] = length
        work_ref[seg] = at + 1
        work_ref[NEED + seg] = first + length
        return carry

    lax.fori_loop(0, count, step, 0)
    begin = jnp.int32(0)
    for g in range(NEED):
        live = work_ref[NEED + g]
        plan_ref[3 * count + g] = live
        plan_ref[3 * count + NEED + g] = begin
        begin = begin + jnp.maximum(live - half, 0)
    plan_ref[3 * count + 2 * NEED] = begin


def segment_rows(q_ref, plan_ref, seg, low, rows):
    count = q_ref.shape[0] // QLEN
    per = count // NEED
    width = per * QLEN
    lane = lax.broadcasted_iota(jnp.int32, (1, width), 1)
    owner = lane // QLEN
    inner = lane % QLEN
    first = jnp.zeros((1, width), jnp.int32)
    length = jnp.zeros((1, width), jnp.int32)
    blocks = []
    for k in range(per):
        q = plan_ref[seg * per + k]
        blocks.append(q_ref[pl.ds(pl.multiple_of(q * QLEN, QLEN), QLEN), :])
        first = jnp.where(owner == k, plan_ref[count + seg * per + k], first)
        length = jnp.where(owner == k, plan_ref[2 * count + seg * per + k], length)
    target = jnp.where(inner < length, first + inner, -1)
    row = lax.broadcasted_iota(jnp.int32, (rows, width), 0) + low
    pick = jnp.where(row == target, 1.0, 0.0).astype(BF16)
    return jnp.dot(pick, jnp.concatenate(blocks, axis=0), preferred_element_type=F32).astype(BF16)


def attend_tiles(rows_ref, kv_ref, out_ref, base, live, rows):
    dim = kv_ref.shape[1] // 2
    heads = rows_ref.shape[1] // dim
    scale = LOG2E * dim ** (-0.5)
    for t in range(rows // QLEN):
        @pl.when(live > t * QLEN)
        def _():
            x = rows_ref[t * QLEN:(t + 1) * QLEN, :]
            x = jnp.concatenate([x[:, h * dim:(h + 1) * dim] for h in range(heads)], axis=0)
            s = lax.dot_general(x, kv_ref[:, :dim], (((1,), (1,)), ((), ())), preferred_element_type=F32)
            top = jnp.max(s, axis=1, keepdims=True)
            e = jnp.exp2((s - top) * scale)
            total = jnp.sum(e, axis=1, keepdims=True)
            o = jnp.dot(e.astype(BF16), kv_ref[:, dim:], preferred_element_type=F32) / total
            o = o.astype(BF16)
            for h in range(heads):
                out_ref[base + t * QLEN:base + (t + 1) * QLEN, h * dim:(h + 1) * dim] = o[h * QLEN:(h + 1) * QLEN, :]

        @pl.when(live <= t * QLEN)
        def _():
            out_ref[base + t * QLEN:base + (t + 1) * QLEN, :] = jnp.zeros((QLEN, out_ref.shape[1]), out_ref.dtype)


def first_kernel(info_ref, slot_ref, len_ref, q_ref, kv_ref, plan_ref, out_ref, work_ref, rows_ref):
    make_plan(info_ref, slot_ref, len_ref, plan_ref, work_ref)
    head_body(plan_ref, q_ref, kv_ref, out_ref, rows_ref, 0)


def head_body(plan_ref, q_ref, kv_ref, out_ref, rows_ref, seg):
    half = out_ref.shape[0]
    live = plan_ref[3 * (q_ref.shape[0] // QLEN) + seg]
    rows_ref[...] = segment_rows(q_ref, plan_ref, seg, 0, half)
    attend_tiles(rows_ref, kv_ref, out_ref, 0, live, half)


def head_kernel(seg, plan_ref, q_ref, kv_ref, out_ref, rows_ref):
    head_body(plan_ref, q_ref, kv_ref, out_ref, rows_ref, seg)


def tails_kernel(plan_ref, q_ref, kv0_ref, kv1_ref, kv2_ref, kv3_ref, out_ref, rows_ref, tails_ref):
    count = q_ref.shape[0] // QLEN
    half = rows_ref.shape[0]
    width = tails_ref.shape[0]
    lane = lax.broadcasted_iota(jnp.int32, (1, width), 1)
    target = jnp.full((1, width), -1, jnp.int32)
    for g, kv_ref in enumerate((kv0_ref, kv1_ref, kv2_ref, kv3_ref)):
        live = plan_ref[3 * count + g] - half
        begin = plan_ref[3 * count + NEED + g]

        @pl.when(live > 0)
        def _():
            rows_ref[...] = segment_rows(q_ref, plan_ref, g, half, half)

        attend_tiles(rows_ref, kv_ref, tails_ref, g * half, live, half)
        inner = lane - g * half
        target = jnp.where((inner >= 0) & (inner < live), begin + inner, target)
    row = lax.broadcasted_iota(jnp.int32, (out_ref.shape[0], width), 0)
    pick = jnp.where(row == target, 1.0, 0.0).astype(BF16)
    out_ref[...] = jnp.dot(pick, tails_ref[...], preferred_element_type=F32).astype(BF16)


def project_kernel(parts, info_ref, *refs):
    w_ref, out_ref = refs[5 * parts:]
    me = info_ref[0]
    depth = refs[0].shape[1]
    line = w_ref.shape[0] // depth
    total = None
    for k in range(line):
        pieces = []
        for c in range(parts):
            own, one, two, three, passed = refs[5 * c:5 * c + 5]
            if k == 0:
                pieces.append(own[...])
            elif k == 1:
                pieces.append(jnp.where(me == 0, passed[...], one[...]))
            elif k == 2:
                pieces.append(two[...])
            else:
                pieces.append(jnp.where(me == line - 1, passed[...], three[...]))
        x = pieces[0] if parts == 1 else jnp.concatenate(pieces, axis=0)
        at = lax.rem(me + line - k, line)
        w = w_ref[pl.ds(pl.multiple_of(at * depth, depth), depth), :]
        y = jnp.dot(x, w, preferred_element_type=F32)
        total = y if total is None else total + y
    out_ref[...] = total.astype(out_ref.dtype)


def place_kernel(plan_ref, *refs):
    *compact, out_ref, pick_ref = refs
    rows, width = pick_ref.shape
    count = rows // QLEN
    per = count // NEED
    half = per * QLEN // 2

    @pl.when(pl.program_id(0) == 0)
    def _():
        sub = lax.broadcasted_iota(jnp.int32, (QLEN, 1), 0)
        lane = lax.broadcasted_iota(jnp.int32, (QLEN, width), 1)
        for p in range(count):
            seg = p // per
            q = plan_ref[p]
            at = plan_ref[count + p] + sub
            tail = plan_ref[3 * count + NEED + seg] + (NEED - 1) * half
            at = jnp.where(at < half, seg * half + at, tail + at)
            at = jnp.where(sub < plan_ref[2 * count + p], at, -1)
            pick_ref[pl.ds(pl.multiple_of(q * QLEN, QLEN), QLEN), :] = jnp.where(lane == at, 1.0, 0.0).astype(BF16)

    total = None
    low = 0
    for c in compact:
        high = low + c.shape[0]
        y = jnp.dot(pick_ref[:, low:high], c[...], preferred_element_type=F32)
        total = y if total is None else total + y
        low = high
    out_ref[...] = total.astype(out_ref.dtype)


SMEM = pl.BlockSpec(memory_space=pltpu.SMEM)
VMEM = pl.BlockSpec(memory_space=pltpu.VMEM)


def on_device_line(queries, kv_cache, question_slot, question_len, out_weight):
    row_count, col_count = queries.shape
    count = row_count // QLEN
    seg_rows = row_count // NEED
    half = seg_rows // 2
    image = kv_cache[0]
    tokens, dim = image.shape[0], image.shape[1] // 2
    heads = col_count // dim
    out_cols = out_weight.shape[1]
    line = lax.axis_size("tensor")
    ring = lax.axis_size("serve")
    info = jnp.stack([lax.axis_index("tensor"), lax.axis_index("serve") % 2]).astype(jnp.int32)

    kv_two = lax.ppermute(image, "serve", [(i, (i + 2) % ring) for i in range(ring)])
    kv_mix = lax.ppermute(image, "serve", [(i, i + 1) if i % 2 == 0 else (i, (i + 3) % ring) for i in range(ring)])
    kv_swap = lax.ppermute(kv_two, "serve", [(i, i ^ 1) for i in range(ring)])

    def attend_cost(rows):
        return pl.CostEstimate(
            flops=8 * rows * heads * tokens * dim,
            bytes_accessed=2 * (image.size + queries.size + rows * col_count),
            transcendentals=rows * heads * tokens,
        )

    params = pltpu.CompilerParams(vmem_limit_bytes=40 * MIB)
    plan_size = 3 * count + 2 * NEED + 8
    head_shape = jax.ShapeDtypeStruct((half, col_count), BF16)
    plan, head0 = pl.pallas_call(
        first_kernel,
        out_shape=(jax.ShapeDtypeStruct((plan_size,), jnp.int32), head_shape),
        in_specs=[SMEM, SMEM, SMEM, VMEM, VMEM],
        out_specs=(SMEM, VMEM),
        scratch_shapes=[pltpu.SMEM((2 * NEED,), jnp.int32), pltpu.VMEM((half, col_count), BF16)],
        compiler_params=params,
        cost_estimate=attend_cost(half),
        name="first_head",
    )(info, question_slot, question_len, queries, image)

    def head(seg, key_value):
        return pl.pallas_call(
            functools.partial(head_kernel, seg),
            out_shape=head_shape,
            in_specs=[SMEM, VMEM, VMEM],
            out_specs=VMEM,
            scratch_shapes=[pltpu.VMEM((half, col_count), BF16)],
            compiler_params=params,
            cost_estimate=attend_cost(half),
            name="head",
        )(plan, queries, key_value)

    def gathered(chunk):
        two = lax.ppermute(chunk, "tensor", [(i, (i + 2) % line) for i in range(line)])
        one = lax.ppermute(chunk, "tensor", [(i, i + 1) for i in range(line - 1)])
        three = lax.ppermute(chunk, "tensor", [(i + 1, i) for i in range(line - 1)])
        passed = lax.ppermute(two, "tensor", [(line - 2, line - 1), (1, 0)])
        return chunk, one, two, three, passed

    def project(*chunks):
        rows = sum(c[0].shape[0] for c in chunks)
        tile = 512
        whole = [pl.BlockSpec(a.shape, lambda n: (0, 0)) for c in chunks for a in c]
        return pl.pallas_call(
            functools.partial(project_kernel, len(chunks)),
            out_shape=jax.ShapeDtypeStruct((rows, out_cols), BF16),
            grid=(out_cols // tile,),
            in_specs=[SMEM] + whole + [pl.BlockSpec((out_weight.shape[0], tile), lambda n: (0, n))],
            out_specs=pl.BlockSpec((rows, tile), lambda n: (0, n)),
            compiler_params=params,
            cost_estimate=pl.CostEstimate(
                flops=2 * rows * out_weight.size, bytes_accessed=2 * out_weight.size, transcendentals=0),
            name="project",
        )(info, *[a for c in chunks for a in c], out_weight)

    def place(*compact):
        tile = 512
        width = sum(c.shape[0] for c in compact)
        return pl.pallas_call(
            place_kernel,
            out_shape=jax.ShapeDtypeStruct((row_count, out_cols), BF16),
            grid=(out_cols // tile,),
            in_specs=[SMEM] + [pl.BlockSpec((c.shape[0], tile), lambda n: (0, n)) for c in compact],
            out_specs=pl.BlockSpec((row_count, tile), lambda n: (0, n)),
            scratch_shapes=[pltpu.VMEM((row_count, width), BF16)],
            compiler_params=params,
            cost_estimate=pl.CostEstimate(
                flops=2 * row_count * width * out_cols, bytes_accessed=2 * (row_count + width) * out_cols,
                transcendentals=0),
            name="place",
        )(plan, *compact)

    chunk0 = gathered(head0)
    chunk1 = gathered(head(1, kv_two))
    chunk2 = gathered(head(2, kv_mix))
    chunk3 = gathered(head(3, kv_swap))
    rest = pl.pallas_call(
        tails_kernel,
        out_shape=jax.ShapeDtypeStruct((NEED * half, col_count), BF16),
        in_specs=[SMEM] + [VMEM] * 5,
        out_specs=VMEM,
        scratch_shapes=[pltpu.VMEM((half, col_count), BF16), pltpu.VMEM((NEED * half, col_count), BF16)],
        compiler_params=params,
        cost_estimate=attend_cost(half),
        name="tails",
    )(plan, queries, image, kv_two, kv_mix, kv_swap)
    done01 = project(chunk0, chunk1)
    done23 = project(chunk2, chunk3)
    live_rest = plan[3 * count + 2 * NEED]

    sizes = [0] + [half * k // 2 for k in (1, 2, 3, 4, 8)]

    def finish(size, rest, done01, done23):
        if size == 0:
            return place(done01, done23)
        parts = [gathered(rest[k * size // 2:(k + 1) * size // 2]) for k in range(2)]
        return place(done01, done23, project(*parts))

    index = sum([(live_rest > s).astype(jnp.int32) for s in sizes[:-1]])
    return lax.switch(index, [functools.partial(finish, s) for s in sizes], rest, done01, done23)


def solution(mesh):
    plain = mesh.shape["tensor"] == KVH == 4 and mesh.shape["serve"] % 2 == 0 and NEED == 4
    return jax.shard_map(
        on_device_line if plain else on_device_general,
        mesh=mesh,
        in_specs=(
            P("serve", "tensor"),
            P("serve", "tensor", None),
            P("serve"),
            P("serve"),
            P(None, "tensor"),
        ),
        out_specs=P("serve", "tensor"),
        check_vma=False,
    )
```

```python
import functools

import jax
import jax.numpy as jnp
from jax import lax
from jax.experimental import pallas as pl
from jax.experimental.pallas import tpu as pltpu
from jax.sharding import PartitionSpec as P

KVH = 4
P_SIZE = 1600
QLEN = 32
NEED = 4
LOG2E = 1.4426950408889634
MIB = 1 << 20
F32 = jnp.float32
BF16 = jnp.bfloat16


def swapped(shard, axis, bit):
    return lax.ppermute(shard, axis, [(i, i ^ 1 << bit) for i in range(lax.axis_size(axis))])


def shifted(value, axis, steps):
    count = lax.axis_size(axis)
    pairs = [(source, (source + steps) % count) for source in range(count)]
    return lax.ppermute(value, axis, pairs)


def attend(query_rows, key_value):
    row_count = query_rows.shape[0]
    head_count = key_value.shape[0]
    head_dim = key_value.shape[2] // 2
    grouped = query_rows.reshape(row_count, head_count, -1, head_dim)
    key_part = key_value[:, :, :head_dim]
    value_part = key_value[:, :, head_dim:]
    scores = jnp.einsum(
        "rkgd,kpd->kgrp", grouped, key_part, preferred_element_type=jnp.float32
    ) * head_dim ** (-0.5)
    row_max = jnp.max(scores, axis=3, keepdims=True)
    exp_scores = jnp.exp(scores - row_max)
    sum_exp = jnp.sum(exp_scores, axis=3, keepdims=True)
    weights = (exp_scores / sum_exp).astype(jnp.bfloat16)
    blended = jnp.einsum("kgrp,kpd->rkgd", weights, value_part, preferred_element_type=jnp.float32)
    return blended.reshape(row_count, -1)


def on_device_general(queries, kv_cache, question_slot, question_len, out_weight):
    row_count, col_count = queries.shape
    head_dim = kv_cache.shape[2] // 2
    question_count = row_count // QLEN
    per_slot = question_count // NEED
    head_piece = kv_cache[0]
    sharing = lax.axis_size("tensor") // KVH
    if sharing > 1:
        for bit_number in range(sharing.bit_length() - 1):
            partner_piece = swapped(head_piece, "tensor", bit_number)
            upper_member = lax.axis_index("tensor") // 2**bit_number % 2 == 1
            head_piece = jnp.where(
                upper_member,
                jnp.concatenate([partner_piece, head_piece], axis=0),
                jnp.concatenate([head_piece, partner_piece], axis=0),
            )
    key_value = head_piece.reshape(-1, P_SIZE, 2 * head_dim)
    ordering = jnp.argsort(question_slot, stable=True)
    inverse_order = jnp.argsort(ordering, stable=True)
    sorted_rows = queries.reshape(question_count, QLEN, col_count)[ordering]
    sorted_rows = sorted_rows.reshape(NEED, per_slot * QLEN, col_count)
    results = []
    for offset_back in range(NEED):
        if offset_back == 0:
            remote = key_value
        else:
            remote = shifted(key_value, "serve", offset_back)
        results.append(attend(sorted_rows[offset_back], remote))
    sorted_out = jnp.stack(results).reshape(question_count, QLEN, col_count)
    blended = sorted_out[inverse_order].reshape(row_count, col_count)
    token_pos = jnp.arange(row_count, dtype=jnp.int32) % QLEN
    live_rows = token_pos < jnp.repeat(question_len, QLEN, total_repeat_length=row_count)
    attended = jnp.where(live_rows[:, None], blended, 0.0).astype(jnp.bfloat16)
    zero_sum = jnp.zeros((row_count, out_weight.shape[1]), jnp.float32)
    gathered_cols = lax.all_gather(attended, "tensor", axis=1, tiled=True)
    weight_rows = lax.slice_in_dim(out_weight, 0, gathered_cols.shape[1], axis=0)
    answers = zero_sum + jnp.dot(gathered_cols, weight_rows, preferred_element_type=jnp.float32)
    return answers.astype(jnp.bfloat16)


def make_plan(info_ref, slot_ref, len_ref, plan_ref, work_ref):
    count = slot_ref.shape[0]
    per = count // NEED
    half = per * QLEN // 2
    odd = info_ref[1]
    for g in range(NEED):
        work_ref[g] = g * per
        work_ref[NEED + g] = 0

    def step(q, carry):
        slot = slot_ref[q]
        length = len_ref[q]
        last = jnp.where(slot == 1, 3 - odd, 2 + odd)
        seg = jnp.where(slot == 0, 0, jnp.where(slot == 2, 1, last))
        at = work_ref[seg]
        first = work_ref[NEED + seg]
        plan_ref[at] = q
        plan_ref[count + at] = first
        plan_ref[2 * count + at] = length
        work_ref[seg] = at + 1
        work_ref[NEED + seg] = first + length
        return carry

    lax.fori_loop(0, count, step, 0)
    begin = jnp.int32(0)
    for g in range(NEED):
        live = work_ref[NEED + g]
        plan_ref[3 * count + g] = live
        plan_ref[3 * count + NEED + g] = begin
        begin = begin + jnp.maximum(live - half, 0)
    plan_ref[3 * count + 2 * NEED] = begin


def segment_rows(q_ref, plan_ref, seg, low, rows):
    count = q_ref.shape[0] // QLEN
    per = count // NEED
    width = per * QLEN
    lane = lax.broadcasted_iota(jnp.int32, (1, width), 1)
    owner = lane // QLEN
    inner = lane % QLEN
    first = jnp.zeros((1, width), jnp.int32)
    length = jnp.zeros((1, width), jnp.int32)
    blocks = []
    for k in range(per):
        q = plan_ref[seg * per + k]
        blocks.append(q_ref[pl.ds(pl.multiple_of(q * QLEN, QLEN), QLEN), :])
        first = jnp.where(owner == k, plan_ref[count + seg * per + k], first)
        length = jnp.where(owner == k, plan_ref[2 * count + seg * per + k], length)
    target = jnp.where(inner < length, first + inner, -1)
    row = lax.broadcasted_iota(jnp.int32, (rows, width), 0) + low
    pick = jnp.where(row == target, 1.0, 0.0).astype(BF16)
    return jnp.dot(pick, jnp.concatenate(blocks, axis=0), preferred_element_type=F32).astype(BF16)


def blend(x, kv_ref, ones_ref):
    dim = kv_ref.shape[1] // 2
    s = lax.dot_general(x, kv_ref[:, :dim], (((1,), (1,)), ((), ())), preferred_element_type=F32)
    top = jnp.max(s, axis=1, keepdims=True)
    e = jnp.exp2((s - top) * (LOG2E * dim ** (-0.5))).astype(BF16)
    o = jnp.dot(e, ones_ref[...], preferred_element_type=F32)
    return (o[:, :dim] / o[:, dim:]).astype(BF16)


def fill_ones(kv_ref, ones_ref):
    dim = kv_ref.shape[1] // 2
    ones_ref[:, :dim] = kv_ref[:, dim:]
    ones_ref[:, dim:] = jnp.ones((kv_ref.shape[0], dim), BF16)


def attend_tiles(rows_ref, kv_ref, ones_ref, out_ref, base, live, rows):
    dim = kv_ref.shape[1] // 2
    heads = rows_ref.shape[1] // dim
    for t in range(rows // QLEN):
        @pl.when(live > t * QLEN)
        def _():
            x = rows_ref[t * QLEN:(t + 1) * QLEN, :]
            x = jnp.concatenate([x[:, h * dim:(h + 1) * dim] for h in range(heads)], axis=0)
            o = blend(x, kv_ref, ones_ref)
            for h in range(heads):
                out_ref[base + t * QLEN:base + (t + 1) * QLEN, h * dim:(h + 1) * dim] = o[h * QLEN:(h + 1) * QLEN, :]

        @pl.when(live <= t * QLEN)
        def _():
            out_ref[base + t * QLEN:base + (t + 1) * QLEN, :] = jnp.zeros((QLEN, out_ref.shape[1]), out_ref.dtype)


def attend_heads(x, kv_ref, keys_ref, ones_ref, out_ref, base):
    dim = kv_ref.shape[1] // 2
    rows = x.shape[0]
    fill_ones(kv_ref, ones_ref)
    keys_ref[...] = kv_ref[:, :dim].T
    for h in range(0, x.shape[1] // dim, 2):
        pair = jnp.concatenate([x[:, h * dim:(h + 1) * dim], x[:, (h + 1) * dim:(h + 2) * dim]], axis=0)
        s = jnp.dot(pair, keys_ref[...], preferred_element_type=F32)
        top = jnp.max(s, axis=1, keepdims=True)
        e = jnp.exp2((s - top) * (LOG2E * dim ** (-0.5))).astype(BF16)
        o = jnp.dot(e, ones_ref[...], preferred_element_type=F32)
        o = (o[:, :dim] / o[:, dim:]).astype(BF16)
        out_ref[base:base + rows, h * dim:(h + 1) * dim] = o[:rows, :]
        out_ref[base:base + rows, (h + 1) * dim:(h + 2) * dim] = o[rows:, :]


def first_kernel(info_ref, slot_ref, len_ref, q_ref, kv_ref, plan_ref, out_ref, work_ref, keys_ref, ones_ref):
    make_plan(info_ref, slot_ref, len_ref, plan_ref, work_ref)
    x = segment_rows(q_ref, plan_ref, 0, 0, out_ref.shape[0])
    attend_heads(x, kv_ref, keys_ref, ones_ref, out_ref, 0)


def heads_kernel(segs, plan_ref, q_ref, *refs):
    kv_refs, (out_ref, keys_ref, ones_ref) = refs[:len(segs)], refs[len(segs):]
    half = out_ref.shape[0] // len(segs)
    for i, (seg, kv_ref) in enumerate(zip(segs, kv_refs)):
        x = segment_rows(q_ref, plan_ref, seg, 0, half)
        attend_heads(x, kv_ref, keys_ref, ones_ref, out_ref, i * half)


def tails_kernel(plan_ref, q_ref, kv0_ref, kv1_ref, kv2_ref, kv3_ref, out_ref, rows_ref, tails_ref, ones_ref):
    count = q_ref.shape[0] // QLEN
    half = rows_ref.shape[0]
    width = tails_ref.shape[0]
    lane = lax.broadcasted_iota(jnp.int32, (1, width), 1)
    target = jnp.full((1, width), -1, jnp.int32)
    for g, kv_ref in enumerate((kv0_ref, kv1_ref, kv2_ref, kv3_ref)):
        live = plan_ref[3 * count + g] - half
        begin = plan_ref[3 * count + NEED + g]

        @pl.when(live > 0)
        def _():
            rows_ref[...] = segment_rows(q_ref, plan_ref, g, half, half)
            fill_ones(kv_ref, ones_ref)

        attend_tiles(rows_ref, kv_ref, ones_ref, tails_ref, g * half, live, half)
        inner = lane - g * half
        target = jnp.where((inner >= 0) & (inner < live), begin + inner, target)
    row = lax.broadcasted_iota(jnp.int32, (out_ref.shape[0], width), 0)
    pick = jnp.where(row == target, 1.0, 0.0).astype(BF16)
    out_ref[...] = jnp.dot(pick, tails_ref[...], preferred_element_type=F32).astype(BF16)


def project_kernel(parts, info_ref, *refs):
    w_ref, out_ref = refs[4 * parts:]
    me = info_ref[0]
    depth = refs[0].shape[1]
    line = w_ref.shape[0] // depth
    upper = me >= line // 2
    end = (me == 0) | (me == line - 1)
    pair = jnp.where(upper, 5 - me, 1 - me)
    near = jnp.where(upper, 1, 2)
    far = jnp.where(upper, 0, 3)
    total = None
    for k, at in enumerate((me, pair, near, far)):
        pieces = []
        for c in range(parts):
            own, other, middle, ends = refs[4 * c:4 * c + 4]
            rows = own.shape[0]
            if k < 2:
                pieces.append((own, other)[k][...])
            else:
                part = pl.ds((k - 2) * rows, rows)
                pieces.append(jnp.where(end, ends[part, :], middle[part, :]))
        x = pieces[0] if parts == 1 else jnp.concatenate(pieces, axis=0)
        w = w_ref[pl.ds(pl.multiple_of(at * depth, depth), depth), :]
        y = jnp.dot(x, w, preferred_element_type=F32)
        total = y if total is None else total + y
    out_ref[...] = total.astype(out_ref.dtype)


def place_kernel(plan_ref, *refs):
    *compact, out_ref, pick_ref = refs
    rows, width = pick_ref.shape
    count = rows // QLEN
    per = count // NEED
    half = per * QLEN // 2

    @pl.when(pl.program_id(0) == 0)
    def _():
        sub = lax.broadcasted_iota(jnp.int32, (QLEN, 1), 0)
        lane = lax.broadcasted_iota(jnp.int32, (QLEN, width), 1)
        for p in range(count):
            seg = p // per
            q = plan_ref[p]
            at = plan_ref[count + p] + sub
            tail = plan_ref[3 * count + NEED + seg] + (NEED - 1) * half
            at = jnp.where(at < half, seg * half + at, tail + at)
            at = jnp.where(sub < plan_ref[2 * count + p], at, -1)
            pick_ref[pl.ds(pl.multiple_of(q * QLEN, QLEN), QLEN), :] = jnp.where(lane == at, 1.0, 0.0).astype(BF16)

    total = None
    low = 0
    for c in compact:
        high = low + c.shape[0]
        y = jnp.dot(pick_ref[:, low:high], c[...], preferred_element_type=F32)
        total = y if total is None else total + y
        low = high
    out_ref[...] = total.astype(out_ref.dtype)


SMEM = pl.BlockSpec(memory_space=pltpu.SMEM)
VMEM = pl.BlockSpec(memory_space=pltpu.VMEM)


def on_device_line(queries, kv_cache, question_slot, question_len, out_weight):
    row_count, col_count = queries.shape
    count = row_count // QLEN
    seg_rows = row_count // NEED
    half = seg_rows // 2
    image = kv_cache[0]
    tokens, dim = image.shape[0], image.shape[1] // 2
    heads = col_count // dim
    out_cols = out_weight.shape[1]
    line = lax.axis_size("tensor")
    ring = lax.axis_size("serve")
    info = jnp.stack([lax.axis_index("tensor"), lax.axis_index("serve") % 2]).astype(jnp.int32)

    kv_two = lax.ppermute(image, "serve", [(i, (i + 2) % ring) for i in range(ring)])
    kv_mix = lax.ppermute(image, "serve", [(i, i + 1) if i % 2 == 0 else (i, (i + 3) % ring) for i in range(ring)])
    params = pltpu.CompilerParams(vmem_limit_bytes=40 * MIB)
    plan_size = 3 * count + 2 * NEED + 8

    def cost(micros):
        return pl.CostEstimate(flops=int(micros * 1.1e9), bytes_accessed=image.size, transcendentals=0)

    scratch = [pltpu.VMEM((dim, tokens), BF16), pltpu.VMEM((tokens, 2 * dim), BF16)]
    plan, head0 = pl.pallas_call(
        first_kernel,
        out_shape=(
            jax.ShapeDtypeStruct((plan_size,), jnp.int32),
            jax.ShapeDtypeStruct((half, col_count), BF16),
        ),
        in_specs=[SMEM, SMEM, SMEM, VMEM, VMEM],
        out_specs=(SMEM, VMEM),
        scratch_shapes=[pltpu.SMEM((2 * NEED,), jnp.int32)] + scratch,
        compiler_params=params,
        cost_estimate=cost(5),
        name="first_head",
    )(info, question_slot, question_len, queries, image)

    def head(segs, *key_values):
        return pl.pallas_call(
            functools.partial(heads_kernel, segs),
            out_shape=jax.ShapeDtypeStruct((half * len(segs), col_count), BF16),
            in_specs=[SMEM, VMEM] + [VMEM] * len(segs),
            out_specs=VMEM,
            scratch_shapes=scratch,
            compiler_params=params,
            cost_estimate=cost(4 * len(segs)),
            name="heads",
        )(plan, queries, *key_values)

    def paired(chunk):
        return chunk, lax.ppermute(chunk, "tensor", [(i, i ^ 1) for i in range(line)])

    def crossed(chunk):
        both = jnp.concatenate(chunk, axis=0)
        return *chunk, lax.ppermute(both, "tensor", [(1, 2), (2, 1)])

    def ended(chunk):
        return *chunk, lax.ppermute(chunk[2], "tensor", [(1, 0), (2, 3)])

    def project(*chunks):
        rows = sum(c[0].shape[0] for c in chunks)
        tile = 512
        whole = [pl.BlockSpec(a.shape, lambda n: (0, 0)) for c in chunks for a in c]
        return pl.pallas_call(
            functools.partial(project_kernel, len(chunks)),
            out_shape=jax.ShapeDtypeStruct((rows, out_cols), BF16),
            grid=(out_cols // tile,),
            in_specs=[SMEM] + whole + [pl.BlockSpec((out_weight.shape[0], tile), lambda n: (0, n))],
            out_specs=pl.BlockSpec((rows, tile), lambda n: (0, n)),
            compiler_params=params,
            cost_estimate=cost(6 + rows / 100),
            name="project",
        )(info, *[a for c in chunks for a in c], out_weight)

    def place(*compact):
        tile = 512
        width = sum(c.shape[0] for c in compact)
        return pl.pallas_call(
            place_kernel,
            out_shape=jax.ShapeDtypeStruct((row_count, out_cols), BF16),
            grid=(out_cols // tile,),
            in_specs=[SMEM] + [pl.BlockSpec((c.shape[0], tile), lambda n: (0, n)) for c in compact],
            out_specs=pl.BlockSpec((row_count, tile), lambda n: (0, n)),
            scratch_shapes=[pltpu.VMEM((row_count, width), BF16)],
            compiler_params=params,
            cost_estimate=cost(5),
            name="place",
        )(plan, *compact)

    chunk0 = paired(head0)
    kv_two, chunk0 = lax.optimization_barrier((kv_two, chunk0))
    kv_swap = lax.ppermute(kv_two, "serve", [(i, i ^ 1) for i in range(ring)])
    chunk0 = ended(crossed(chunk0))
    chunk1 = ended(crossed(paired(head((1,), kv_two))))
    chunk2 = crossed(paired(head((2, 3), kv_mix, kv_swap)))
    rest = pl.pallas_call(
        tails_kernel,
        out_shape=jax.ShapeDtypeStruct((NEED * half, col_count), BF16),
        in_specs=[SMEM] + [VMEM] * 5,
        out_specs=VMEM,
        scratch_shapes=[
            pltpu.VMEM((half, col_count), BF16),
            pltpu.VMEM((NEED * half, col_count), BF16),
            pltpu.VMEM((tokens, 2 * dim), BF16),
        ],
        compiler_params=params,
        cost_estimate=cost(10),
        name="tails",
    )(plan, queries, image, kv_two, kv_mix, kv_swap)
    done01 = project(chunk0, chunk1)
    live_rest = plan[3 * count + 2 * NEED]

    sizes = [0] + [half * k // 2 for k in (1, 2, 3, 4, 8)]

    def finish(size, rest, done01, chunk2):
        chunk2 = ended(chunk2)
        if size == 0:
            return place(done01, project(chunk2))
        chunk3 = ended(crossed(paired(rest[:size])))
        return place(done01, project(chunk2), project(chunk3))

    index = sum([(live_rest > s).astype(jnp.int32) for s in sizes[:-1]])
    return lax.switch(index, [functools.partial(finish, s) for s in sizes], rest, done01, chunk2)


def solution(mesh):
    plain = mesh.shape["tensor"] == KVH == 4 and mesh.shape["serve"] % 2 == 0 and NEED == 4
    return jax.shard_map(
        on_device_line if plain else on_device_general,
        mesh=mesh,
        in_specs=(
            P("serve", "tensor"),
            P("serve", "tensor", None),
            P("serve"),
            P("serve"),
            P(None, "tensor"),
        ),
        out_specs=P("serve", "tensor"),
        check_vma=False,
    )
```

```python
import functools

import jax
import jax.numpy as jnp
from jax import lax
from jax.experimental import pallas as pl
from jax.experimental.pallas import tpu as pltpu
from jax.sharding import PartitionSpec as P

KVH = 4
P_SIZE = 1600
QLEN = 32
NEED = 4
LOG2E = 1.4426950408889634
MIB = 1 << 20
F32 = jnp.float32
BF16 = jnp.bfloat16


def swapped(shard, axis, bit):
    return lax.ppermute(shard, axis, [(i, i ^ 1 << bit) for i in range(lax.axis_size(axis))])


def shifted(value, axis, steps):
    count = lax.axis_size(axis)
    pairs = [(source, (source + steps) % count) for source in range(count)]
    return lax.ppermute(value, axis, pairs)


def attend(query_rows, key_value):
    row_count = query_rows.shape[0]
    head_count = key_value.shape[0]
    head_dim = key_value.shape[2] // 2
    grouped = query_rows.reshape(row_count, head_count, -1, head_dim)
    key_part = key_value[:, :, :head_dim]
    value_part = key_value[:, :, head_dim:]
    scores = jnp.einsum(
        "rkgd,kpd->kgrp", grouped, key_part, preferred_element_type=jnp.float32
    ) * head_dim ** (-0.5)
    row_max = jnp.max(scores, axis=3, keepdims=True)
    exp_scores = jnp.exp(scores - row_max)
    sum_exp = jnp.sum(exp_scores, axis=3, keepdims=True)
    weights = (exp_scores / sum_exp).astype(jnp.bfloat16)
    blended = jnp.einsum("kgrp,kpd->rkgd", weights, value_part, preferred_element_type=jnp.float32)
    return blended.reshape(row_count, -1)


def on_device_general(queries, kv_cache, question_slot, question_len, out_weight):
    row_count, col_count = queries.shape
    head_dim = kv_cache.shape[2] // 2
    question_count = row_count // QLEN
    per_slot = question_count // NEED
    head_piece = kv_cache[0]
    sharing = lax.axis_size("tensor") // KVH
    if sharing > 1:
        for bit_number in range(sharing.bit_length() - 1):
            partner_piece = swapped(head_piece, "tensor", bit_number)
            upper_member = lax.axis_index("tensor") // 2**bit_number % 2 == 1
            head_piece = jnp.where(
                upper_member,
                jnp.concatenate([partner_piece, head_piece], axis=0),
                jnp.concatenate([head_piece, partner_piece], axis=0),
            )
    key_value = head_piece.reshape(-1, P_SIZE, 2 * head_dim)
    ordering = jnp.argsort(question_slot, stable=True)
    inverse_order = jnp.argsort(ordering, stable=True)
    sorted_rows = queries.reshape(question_count, QLEN, col_count)[ordering]
    sorted_rows = sorted_rows.reshape(NEED, per_slot * QLEN, col_count)
    results = []
    for offset_back in range(NEED):
        if offset_back == 0:
            remote = key_value
        else:
            remote = shifted(key_value, "serve", offset_back)
        results.append(attend(sorted_rows[offset_back], remote))
    sorted_out = jnp.stack(results).reshape(question_count, QLEN, col_count)
    blended = sorted_out[inverse_order].reshape(row_count, col_count)
    token_pos = jnp.arange(row_count, dtype=jnp.int32) % QLEN
    live_rows = token_pos < jnp.repeat(question_len, QLEN, total_repeat_length=row_count)
    attended = jnp.where(live_rows[:, None], blended, 0.0).astype(jnp.bfloat16)
    zero_sum = jnp.zeros((row_count, out_weight.shape[1]), jnp.float32)
    gathered_cols = lax.all_gather(attended, "tensor", axis=1, tiled=True)
    weight_rows = lax.slice_in_dim(out_weight, 0, gathered_cols.shape[1], axis=0)
    answers = zero_sum + jnp.dot(gathered_cols, weight_rows, preferred_element_type=jnp.float32)
    return answers.astype(jnp.bfloat16)


def make_plan(info_ref, slot_ref, len_ref, plan_ref, work_ref):
    count = slot_ref.shape[0]
    per = count // NEED
    half = per * QLEN // 2
    odd = info_ref[1]
    for g in range(NEED):
        work_ref[g] = g * per
        work_ref[NEED + g] = 0

    def step(q, carry):
        slot = slot_ref[q]
        length = len_ref[q]
        last = jnp.where(slot == 1, 3 - odd, 2 + odd)
        seg = jnp.where(slot == 0, 0, jnp.where(slot == 2, 1, last))
        at = work_ref[seg]
        first = work_ref[NEED + seg]
        plan_ref[at] = q
        plan_ref[count + at] = first
        plan_ref[2 * count + at] = length
        work_ref[seg] = at + 1
        work_ref[NEED + seg] = first + length
        return carry

    lax.fori_loop(0, count, step, 0)
    begin = jnp.int32(0)
    for g in range(NEED):
        live = work_ref[NEED + g]
        plan_ref[3 * count + g] = live
        plan_ref[3 * count + NEED + g] = begin
        begin = begin + jnp.maximum(live - half, 0)
    plan_ref[3 * count + 2 * NEED] = begin


def segment_rows(q_ref, plan_ref, seg, low, rows):
    count = q_ref.shape[0] // QLEN
    per = count // NEED
    width = per * QLEN
    lane = lax.broadcasted_iota(jnp.int32, (1, width), 1)
    owner = lane // QLEN
    inner = lane % QLEN
    first = jnp.zeros((1, width), jnp.int32)
    length = jnp.zeros((1, width), jnp.int32)
    blocks = []
    for k in range(per):
        q = plan_ref[seg * per + k]
        blocks.append(q_ref[pl.ds(pl.multiple_of(q * QLEN, QLEN), QLEN), :])
        first = jnp.where(owner == k, plan_ref[count + seg * per + k], first)
        length = jnp.where(owner == k, plan_ref[2 * count + seg * per + k], length)
    target = jnp.where(inner < length, first + inner, -1)
    row = lax.broadcasted_iota(jnp.int32, (rows, width), 0) + low
    pick = jnp.where(row == target, 1.0, 0.0).astype(BF16)
    return jnp.dot(pick, jnp.concatenate(blocks, axis=0), preferred_element_type=F32).astype(BF16)


def load_image(kv_ref, keys_ref, ones_ref):
    dim = kv_ref.shape[1] // 2
    keys_ref[...] = kv_ref[:, :dim].T
    ones_ref[:, :dim] = kv_ref[:, dim:]
    ones_ref[:, dim:] = jnp.ones((kv_ref.shape[0], dim), BF16)


def attend_rows(x, keys_ref, ones_ref, out_ref, base):
    dim = keys_ref.shape[0]
    rows, cols = x.shape
    heads = cols // dim
    group = max(1, min(heads, 256 // rows))
    for low in range(0, heads, group):
        members = range(low, min(low + group, heads))
        q = [x[:, h * dim:(h + 1) * dim] for h in members]
        q = q[0] if len(q) == 1 else jnp.concatenate(q, axis=0)
        s = jnp.dot(q, keys_ref[...], preferred_element_type=F32)
        top = jnp.max(s, axis=1, keepdims=True)
        e = jnp.exp2((s - top) * (LOG2E * dim ** (-0.5))).astype(BF16)
        o = jnp.dot(e, ones_ref[...], preferred_element_type=F32)
        o = (o[:, :dim] / o[:, dim:]).astype(BF16)
        for i, h in enumerate(members):
            out_ref[base:base + rows, h * dim:(h + 1) * dim] = o[i * rows:(i + 1) * rows, :]


def first_kernel(info_ref, slot_ref, len_ref, q_ref, kv_ref, plan_ref, out_ref, work_ref, keys_ref, ones_ref):
    make_plan(info_ref, slot_ref, len_ref, plan_ref, work_ref)
    load_image(kv_ref, keys_ref, ones_ref)
    attend_rows(segment_rows(q_ref, plan_ref, 0, 0, out_ref.shape[0]), keys_ref, ones_ref, out_ref, 0)


def head_kernel(seg, plan_ref, q_ref, kv_ref, out_ref, keys_ref, ones_ref):
    load_image(kv_ref, keys_ref, ones_ref)
    attend_rows(segment_rows(q_ref, plan_ref, seg, 0, out_ref.shape[0]), keys_ref, ones_ref, out_ref, 0)


def tails_kernel(plan_ref, q_ref, kv0_ref, kv1_ref, kv2_ref, kv3_ref, out_ref, tails_ref, keys_ref, ones_ref):
    count = q_ref.shape[0] // QLEN
    width = tails_ref.shape[0]
    half = width // NEED
    lane = lax.broadcasted_iota(jnp.int32, (1, width), 1)
    target = jnp.full((1, width), -1, jnp.int32)
    tails_ref[...] = jnp.zeros(tails_ref.shape, tails_ref.dtype)
    for g, kv_ref in enumerate((kv0_ref, kv1_ref, kv2_ref, kv3_ref)):
        live = plan_ref[3 * count + g] - half
        begin = plan_ref[3 * count + NEED + g]

        @pl.when(live > 0)
        def _():
            load_image(kv_ref, keys_ref, ones_ref)

        for low, high in ((0, half // 4), (half // 4, half // 2), (half // 2, half)):
            @pl.when((live > low) & (live <= high))
            def _():
                x = segment_rows(q_ref, plan_ref, g, half, high)
                attend_rows(x, keys_ref, ones_ref, tails_ref, g * half)

        inner = lane - g * half
        target = jnp.where((inner >= 0) & (inner < live), begin + inner, target)
    row = lax.broadcasted_iota(jnp.int32, (out_ref.shape[0], width), 0)
    pick = jnp.where(row == target, 1.0, 0.0).astype(BF16)
    out_ref[...] = jnp.dot(pick, tails_ref[...], preferred_element_type=F32).astype(BF16)


def columns(info_ref, line):
    me = info_ref[0]
    upper = me >= line // 2
    pair = jnp.where(upper, 5 - me, 1 - me)
    return me, pair, jnp.where(upper, 1, 2), jnp.where(upper, 0, 3)


def weight_rows(w_ref, at, depth):
    return w_ref[pl.ds(pl.multiple_of(at * depth, depth), depth), :]


def from_afar(info_ref, line, middle_ref, ends_ref, k):
    me = info_ref[0]
    rows = middle_ref.shape[0] // 2
    part = pl.ds(k * rows, rows)
    return jnp.where((me == 0) | (me == line - 1), ends_ref[part, :], middle_ref[part, :])


def project_kernel(info_ref, *refs):
    *chunks, w_ref, out_ref = refs
    depth = chunks[0].shape[1]
    line = w_ref.shape[0] // depth
    total = None
    for k, at in enumerate(columns(info_ref, line)):
        if k < 2:
            pieces = [c[...] for c in chunks[k::4]]
        else:
            pieces = [from_afar(info_ref, line, m, e, k - 2) for m, e in zip(chunks[2::4], chunks[3::4])]
        x = pieces[0] if len(pieces) == 1 else jnp.concatenate(pieces, axis=0)
        y = jnp.dot(x, weight_rows(w_ref, at, depth), preferred_element_type=F32)
        total = y if total is None else total + y
    out_ref[...] = total.astype(out_ref.dtype)


def begin_kernel(info_ref, own_ref, other_ref, w_ref, out_ref):
    depth = own_ref.shape[1]
    at = columns(info_ref, w_ref.shape[0] // depth)
    y = jnp.dot(own_ref[...], weight_rows(w_ref, at[0], depth), preferred_element_type=F32)
    out_ref[...] = y + jnp.dot(other_ref[...], weight_rows(w_ref, at[1], depth), preferred_element_type=F32)


def pick_rows(plan_ref, pick_ref, tails):
    rows, width = pick_ref.shape
    count = rows // QLEN
    per = count // NEED
    half = per * QLEN // 2
    sub = lax.broadcasted_iota(jnp.int32, (QLEN, 1), 0)
    lane = lax.broadcasted_iota(jnp.int32, (QLEN, width), 1)
    for p in range(count):
        seg = p // per
        at = plan_ref[count + p] + sub
        here = at >= half if tails else at < half
        at = at - half + plan_ref[3 * count + NEED + seg] if tails else at + seg * half
        at = jnp.where(here & (sub < plan_ref[2 * count + p]), at, -1)
        block = pl.ds(pl.multiple_of(plan_ref[p] * QLEN, QLEN), QLEN)
        pick_ref[block, :] = jnp.where(lane == at, 1.0, 0.0).astype(BF16)


def place_kernel(plan_ref, *refs):
    *compact, out_ref, pick_ref = refs

    @pl.when(pl.program_id(0) == 0)
    def _():
        pick_rows(plan_ref, pick_ref, False)

    y = jnp.concatenate([c[...] for c in compact], axis=0)
    out_ref[...] = jnp.dot(pick_ref[...], y, preferred_element_type=F32).astype(out_ref.dtype)


def finish_kernel(info_ref, plan_ref, middle_ref, ends_ref, begun_ref, placed_ref, w_ref, out_ref, pick_ref):
    @pl.when(pl.program_id(0) == 0)
    def _():
        pick_rows(plan_ref, pick_ref, True)

    depth = middle_ref.shape[1]
    line = w_ref.shape[0] // depth
    y = begun_ref[...]
    for k, at in enumerate(columns(info_ref, line)[2:]):
        x = from_afar(info_ref, line, middle_ref, ends_ref, k)
        y = y + jnp.dot(x, weight_rows(w_ref, at, depth), preferred_element_type=F32)
    y = jnp.dot(pick_ref[...], y.astype(BF16), preferred_element_type=F32)
    out_ref[...] = (placed_ref[...].astype(F32) + y).astype(out_ref.dtype)


SMEM = pl.BlockSpec(memory_space=pltpu.SMEM)
VMEM = pl.BlockSpec(memory_space=pltpu.VMEM)


def on_device_line(queries, kv_cache, question_slot, question_len, out_weight):
    row_count, col_count = queries.shape
    count = row_count // QLEN
    seg_rows = row_count // NEED
    half = seg_rows // 2
    image = kv_cache[0]
    tokens, dim = image.shape[0], image.shape[1] // 2
    heads = col_count // dim
    out_cols = out_weight.shape[1]
    line = lax.axis_size("tensor")
    ring = lax.axis_size("serve")
    info = jnp.stack([lax.axis_index("tensor"), lax.axis_index("serve") % 2]).astype(jnp.int32)

    kv_two = lax.ppermute(image, "serve", [(i, (i + 2) % ring) for i in range(ring)])
    kv_mix = lax.ppermute(image, "serve", [(i, i + 1) if i % 2 == 0 else (i, (i + 3) % ring) for i in range(ring)])
    params = pltpu.CompilerParams(vmem_limit_bytes=40 * MIB)
    plan_size = 3 * count + 2 * NEED + 8

    def cost(micros):
        return pl.CostEstimate(flops=int(micros * 1.1e9), bytes_accessed=image.size, transcendentals=0)

    scratch = [pltpu.VMEM((dim, tokens), BF16), pltpu.VMEM((tokens, 2 * dim), BF16)]
    plan, head0 = pl.pallas_call(
        first_kernel,
        out_shape=(
            jax.ShapeDtypeStruct((plan_size,), jnp.int32),
            jax.ShapeDtypeStruct((half, col_count), BF16),
        ),
        in_specs=[SMEM, SMEM, SMEM, VMEM, VMEM],
        out_specs=(SMEM, VMEM),
        scratch_shapes=[pltpu.SMEM((2 * NEED,), jnp.int32)] + scratch,
        compiler_params=params,
        cost_estimate=cost(5),
        name="first_head",
    )(info, question_slot, question_len, queries, image)

    def head(seg, key_value):
        return pl.pallas_call(
            functools.partial(head_kernel, seg),
            out_shape=jax.ShapeDtypeStruct((half, col_count), BF16),
            in_specs=[SMEM, VMEM, VMEM],
            out_specs=VMEM,
            scratch_shapes=scratch,
            compiler_params=params,
            cost_estimate=cost(3),
            name="head",
        )(plan, queries, key_value)

    def tails(rows, *key_values):
        return pl.pallas_call(
            tails_kernel,
            out_shape=jax.ShapeDtypeStruct((rows, col_count), BF16),
            in_specs=[SMEM] + [VMEM] * 5,
            out_specs=VMEM,
            scratch_shapes=[pltpu.VMEM((NEED * half, col_count), BF16)] + scratch,
            compiler_params=params,
            cost_estimate=cost(8),
            name="tails",
        )(plan, queries, *key_values)

    def paired(chunk):
        return chunk, lax.ppermute(chunk, "tensor", [(i, i ^ 1) for i in range(line)])

    def crossed(chunk):
        both = jnp.concatenate(chunk, axis=0)
        return *chunk, lax.ppermute(both, "tensor", [(1, 2), (2, 1)])

    def ended(chunk):
        return *chunk, lax.ppermute(chunk[2], "tensor", [(1, 0), (2, 3)])

    tile = 512
    steps = (out_cols // tile,)
    w_spec = pl.BlockSpec((out_weight.shape[0], tile), lambda n: (0, n))

    def resident(*arrays):
        return [pl.BlockSpec(a.shape, lambda n: (0, 0)) for a in arrays]

    def tiled(rows):
        return pl.BlockSpec((rows, tile), lambda n: (0, n))

    def project(*chunks):
        arrays = [a for c in chunks for a in c]
        rows = sum(c[0].shape[0] for c in chunks)
        return pl.pallas_call(
            project_kernel,
            out_shape=jax.ShapeDtypeStruct((rows, out_cols), BF16),
            grid=steps,
            in_specs=[SMEM] + resident(*arrays) + [w_spec],
            out_specs=tiled(rows),
            compiler_params=params,
            cost_estimate=cost(8),
            name="project",
        )(info, *arrays, out_weight)

    def begin(own, other):
        rows = own.shape[0]
        return pl.pallas_call(
            begin_kernel,
            out_shape=jax.ShapeDtypeStruct((rows, out_cols), F32),
            grid=steps,
            in_specs=[SMEM] + resident(own, other) + [w_spec],
            out_specs=tiled(rows),
            compiler_params=params,
            cost_estimate=cost(5),
            name="begin",
        )(info, own, other, out_weight)

    def place(*compact):
        return pl.pallas_call(
            place_kernel,
            out_shape=jax.ShapeDtypeStruct((row_count, out_cols), BF16),
            grid=steps,
            in_specs=[SMEM] + [tiled(c.shape[0]) for c in compact],
            out_specs=tiled(row_count),
            scratch_shapes=[pltpu.VMEM((row_count, sum(c.shape[0] for c in compact)), BF16)],
            compiler_params=params,
            cost_estimate=cost(5),
            name="place",
        )(plan, *compact)

    def finish(middle, ends, begun, placed):
        rows = begun.shape[0]
        return pl.pallas_call(
            finish_kernel,
            out_shape=jax.ShapeDtypeStruct((row_count, out_cols), BF16),
            grid=steps,
            in_specs=[SMEM, SMEM] + resident(middle, ends) + [tiled(rows), tiled(row_count), w_spec],
            out_specs=tiled(row_count),
            scratch_shapes=[pltpu.VMEM((row_count, rows), BF16)],
            compiler_params=params,
            cost_estimate=cost(5),
            name="finish",
        )(info, plan, middle, ends, begun, placed, out_weight)

    chunk0 = paired(head0)
    kv_two, chunk0 = lax.optimization_barrier((kv_two, chunk0))
    kv_swap = lax.ppermute(kv_two, "serve", [(i, i ^ 1) for i in range(ring)])
    chunk0 = crossed(chunk0)
    chunk1 = paired(head(1, kv_two))
    kv_mix, chunk0 = lax.optimization_barrier((kv_mix, chunk0))
    chunk0 = ended(chunk0)
    chunk1 = crossed(chunk1)
    chunk0, chunk1 = lax.optimization_barrier((chunk0, chunk1))
    chunk1 = ended(chunk1)
    chunk2 = crossed(paired(head(2, kv_mix)))
    head3 = head(3, kv_swap)
    rest = tails(NEED * half, image, kv_two, kv_mix, kv_swap)
    done01 = project(chunk0, chunk1)
    live_rest = plan[3 * count + 2 * NEED]

    sizes = [0] + [half * k // 4 for k in (2, 3, 4, 5, 6, 7, 8, 9, 10, 16)]

    def branch(size, done01, chunk2, head3, rest):
        chunk2 = ended(chunk2)
        chunk3 = crossed(paired(head3))
        chunk2, chunk3 = lax.optimization_barrier((chunk2, chunk3))
        chunk3 = ended(chunk3)
        if size == 0:
            return place(done01, project(chunk2, chunk3))
        own, other, middle = crossed(paired(rest[:size]))
        own, other, middle, ends = ended((own, other, middle))
        begun = begin(own, other)
        return finish(middle, ends, begun, place(done01, project(chunk2, chunk3)))

    index = sum([(live_rest > s).astype(jnp.int32) for s in sizes[:-1]])
    return lax.switch(index, [functools.partial(branch, s) for s in sizes], done01, chunk2, head3, rest)


def solution(mesh):
    plain = mesh.shape["tensor"] == KVH == 4 and mesh.shape["serve"] % 2 == 0 and NEED == 4
    return jax.shard_map(
        on_device_line if plain else on_device_general,
        mesh=mesh,
        in_specs=(
            P("serve", "tensor"),
            P("serve", "tensor", None),
            P("serve"),
            P("serve"),
            P(None, "tensor"),
        ),
        out_specs=P("serve", "tensor"),
        check_vma=False,
    )
```

```python
import functools

import jax
import jax.numpy as jnp
from jax import lax
from jax.experimental import pallas as pl
from jax.experimental.pallas import tpu as pltpu
from jax.sharding import PartitionSpec as P

KVH = 4
P_SIZE = 1600
QLEN = 32
NEED = 4
LOG2E = 1.4426950408889634
MIB = 1 << 20
F32 = jnp.float32
BF16 = jnp.bfloat16


def swapped(shard, axis, bit):
    return lax.ppermute(shard, axis, [(i, i ^ 1 << bit) for i in range(lax.axis_size(axis))])


def shifted(value, axis, steps):
    count = lax.axis_size(axis)
    pairs = [(source, (source + steps) % count) for source in range(count)]
    return lax.ppermute(value, axis, pairs)


def attend(query_rows, key_value):
    row_count = query_rows.shape[0]
    head_count = key_value.shape[0]
    head_dim = key_value.shape[2] // 2
    grouped = query_rows.reshape(row_count, head_count, -1, head_dim)
    key_part = key_value[:, :, :head_dim]
    value_part = key_value[:, :, head_dim:]
    scores = jnp.einsum(
        "rkgd,kpd->kgrp", grouped, key_part, preferred_element_type=jnp.float32
    ) * head_dim ** (-0.5)
    row_max = jnp.max(scores, axis=3, keepdims=True)
    exp_scores = jnp.exp(scores - row_max)
    sum_exp = jnp.sum(exp_scores, axis=3, keepdims=True)
    weights = (exp_scores / sum_exp).astype(jnp.bfloat16)
    blended = jnp.einsum("kgrp,kpd->rkgd", weights, value_part, preferred_element_type=jnp.float32)
    return blended.reshape(row_count, -1)


def on_device_general(queries, kv_cache, question_slot, question_len, out_weight):
    row_count, col_count = queries.shape
    head_dim = kv_cache.shape[2] // 2
    question_count = row_count // QLEN
    per_slot = question_count // NEED
    head_piece = kv_cache[0]
    sharing = lax.axis_size("tensor") // KVH
    if sharing > 1:
        for bit_number in range(sharing.bit_length() - 1):
            partner_piece = swapped(head_piece, "tensor", bit_number)
            upper_member = lax.axis_index("tensor") // 2**bit_number % 2 == 1
            head_piece = jnp.where(
                upper_member,
                jnp.concatenate([partner_piece, head_piece], axis=0),
                jnp.concatenate([head_piece, partner_piece], axis=0),
            )
    key_value = head_piece.reshape(-1, P_SIZE, 2 * head_dim)
    ordering = jnp.argsort(question_slot, stable=True)
    inverse_order = jnp.argsort(ordering, stable=True)
    sorted_rows = queries.reshape(question_count, QLEN, col_count)[ordering]
    sorted_rows = sorted_rows.reshape(NEED, per_slot * QLEN, col_count)
    results = []
    for offset_back in range(NEED):
        if offset_back == 0:
            remote = key_value
        else:
            remote = shifted(key_value, "serve", offset_back)
        results.append(attend(sorted_rows[offset_back], remote))
    sorted_out = jnp.stack(results).reshape(question_count, QLEN, col_count)
    blended = sorted_out[inverse_order].reshape(row_count, col_count)
    token_pos = jnp.arange(row_count, dtype=jnp.int32) % QLEN
    live_rows = token_pos < jnp.repeat(question_len, QLEN, total_repeat_length=row_count)
    attended = jnp.where(live_rows[:, None], blended, 0.0).astype(jnp.bfloat16)
    zero_sum = jnp.zeros((row_count, out_weight.shape[1]), jnp.float32)
    gathered_cols = lax.all_gather(attended, "tensor", axis=1, tiled=True)
    weight_rows = lax.slice_in_dim(out_weight, 0, gathered_cols.shape[1], axis=0)
    answers = zero_sum + jnp.dot(gathered_cols, weight_rows, preferred_element_type=jnp.float32)
    return answers.astype(jnp.bfloat16)


def make_plan(info_ref, slot_ref, len_ref, plan_ref, work_ref):
    count = slot_ref.shape[0]
    per = count // NEED
    half = per * QLEN // 2
    odd = info_ref[1]
    for g in range(NEED):
        work_ref[g] = g * per
        work_ref[NEED + g] = 0

    def step(q, carry):
        slot = slot_ref[q]
        length = len_ref[q]
        last = jnp.where(slot == 1, 3 - odd, 2 + odd)
        seg = jnp.where(slot == 0, 0, jnp.where(slot == 2, 1, last))
        at = work_ref[seg]
        first = work_ref[NEED + seg]
        plan_ref[at] = q
        plan_ref[count + at] = first
        plan_ref[2 * count + at] = length
        work_ref[seg] = at + 1
        work_ref[NEED + seg] = first + length
        return carry

    lax.fori_loop(0, count, step, 0)
    begin = jnp.int32(0)
    for g in range(NEED):
        live = work_ref[NEED + g]
        plan_ref[3 * count + g] = live
        plan_ref[3 * count + NEED + g] = begin
        begin = begin + jnp.maximum(live - half, 0)
    plan_ref[3 * count + 2 * NEED] = begin


def segment_rows(q_ref, plan_ref, seg, low, rows):
    count = q_ref.shape[0] // QLEN
    per = count // NEED
    width = per * QLEN
    lane = lax.broadcasted_iota(jnp.int32, (1, width), 1)
    owner = lane // QLEN
    inner = lane % QLEN
    first = jnp.zeros((1, width), jnp.int32)
    length = jnp.zeros((1, width), jnp.int32)
    blocks = []
    for k in range(per):
        q = plan_ref[seg * per + k]
        blocks.append(q_ref[pl.ds(pl.multiple_of(q * QLEN, QLEN), QLEN), :])
        first = jnp.where(owner == k, plan_ref[count + seg * per + k], first)
        length = jnp.where(owner == k, plan_ref[2 * count + seg * per + k], length)
    target = jnp.where(inner < length, first + inner, -1)
    row = lax.broadcasted_iota(jnp.int32, (rows, width), 0) + low
    pick = jnp.where(row == target, 1.0, 0.0).astype(BF16)
    return jnp.dot(pick, jnp.concatenate(blocks, axis=0), preferred_element_type=F32).astype(BF16)


def load_image(kv_ref, keys_ref, ones_ref):
    dim = kv_ref.shape[1] // 2
    keys_ref[...] = kv_ref[:, :dim].T
    ones_ref[:, :dim] = kv_ref[:, dim:]
    ones_ref[:, dim:] = jnp.ones((kv_ref.shape[0], dim), BF16)


def attend_rows(x, keys_ref, ones_ref, out_ref, base):
    dim = keys_ref.shape[0]
    rows, cols = x.shape
    heads = cols // dim
    group = max(1, min(heads, 256 // rows))
    for low in range(0, heads, group):
        members = range(low, min(low + group, heads))
        q = [x[:, h * dim:(h + 1) * dim] for h in members]
        q = q[0] if len(q) == 1 else jnp.concatenate(q, axis=0)
        s = jnp.dot(q, keys_ref[...], preferred_element_type=F32)
        top = jnp.max(s, axis=1, keepdims=True)
        e = jnp.exp2((s - top) * (LOG2E * dim ** (-0.5))).astype(BF16)
        o = jnp.dot(e, ones_ref[...], preferred_element_type=F32)
        o = (o[:, :dim] / o[:, dim:]).astype(BF16)
        for i, h in enumerate(members):
            out_ref[pl.ds(base, rows), h * dim:(h + 1) * dim] = o[i * rows:(i + 1) * rows, :]


def first_kernel(info_ref, slot_ref, len_ref, q_ref, kv_ref, plan_ref, out_ref, work_ref, keys_ref, ones_ref):
    make_plan(info_ref, slot_ref, len_ref, plan_ref, work_ref)
    load_image(kv_ref, keys_ref, ones_ref)
    attend_rows(segment_rows(q_ref, plan_ref, 0, 0, out_ref.shape[0]), keys_ref, ones_ref, out_ref, 0)


def head_kernel(seg, plan_ref, q_ref, kv_ref, out_ref, keys_ref, ones_ref):
    load_image(kv_ref, keys_ref, ones_ref)
    attend_rows(segment_rows(q_ref, plan_ref, seg, 0, out_ref.shape[0]), keys_ref, ones_ref, out_ref, 0)


def tails_kernel(plan_ref, q_ref, kv0_ref, kv1_ref, kv2_ref, kv3_ref, out_ref, tails_ref, keys_ref, ones_ref):
    count = q_ref.shape[0] // QLEN
    width = tails_ref.shape[0]
    half = width // NEED
    seg = pl.program_id(0)
    live = plan_ref[3 * count + seg] - half

    @pl.when(seg == 0)
    def _():
        tails_ref[...] = jnp.zeros(tails_ref.shape, tails_ref.dtype)

    for g, kv_ref in enumerate((kv0_ref, kv1_ref, kv2_ref, kv3_ref)):
        @pl.when((seg == g) & (live > 0))
        def _():
            load_image(kv_ref, keys_ref, ones_ref)

    for low, high in ((0, half // 4), (half // 4, half // 2), (half // 2, half)):
        @pl.when((live > low) & (live <= high))
        def _():
            x = segment_rows(q_ref, plan_ref, seg, half, high)
            attend_rows(x, keys_ref, ones_ref, tails_ref, pl.multiple_of(seg * half, half))

    @pl.when(seg == NEED - 1)
    def _():
        lane = lax.broadcasted_iota(jnp.int32, (1, width), 1)
        target = jnp.full((1, width), -1, jnp.int32)
        for g in range(NEED):
            inner = lane - g * half
            here = (inner >= 0) & (inner < plan_ref[3 * count + g] - half)
            target = jnp.where(here, plan_ref[3 * count + NEED + g] + inner, target)
        row = lax.broadcasted_iota(jnp.int32, (out_ref.shape[0], width), 0)
        pick = jnp.where(row == target, 1.0, 0.0).astype(BF16)
        out_ref[...] = jnp.dot(pick, tails_ref[...], preferred_element_type=F32).astype(BF16)


def columns(info_ref, line):
    me = info_ref[0]
    upper = me >= line // 2
    pair = jnp.where(upper, 5 - me, 1 - me)
    return me, pair, jnp.where(upper, 1, 2), jnp.where(upper, 0, 3)


def weight_rows(w_ref, at, depth):
    return w_ref[pl.ds(pl.multiple_of(at * depth, depth), depth), :]


def from_afar(info_ref, line, middle_ref, ends_ref, k):
    me = info_ref[0]
    rows = middle_ref.shape[0] // 2
    part = pl.ds(k * rows, rows)
    return jnp.where((me == 0) | (me == line - 1), ends_ref[part, :], middle_ref[part, :])


def project_kernel(info_ref, *refs):
    *chunks, w_ref, out_ref = refs
    depth = chunks[0].shape[1]
    line = w_ref.shape[0] // depth
    total = None
    for k, at in enumerate(columns(info_ref, line)):
        if k < 2:
            pieces = [c[...] for c in chunks[k::4]]
        else:
            pieces = [from_afar(info_ref, line, m, e, k - 2) for m, e in zip(chunks[2::4], chunks[3::4])]
        x = pieces[0] if len(pieces) == 1 else jnp.concatenate(pieces, axis=0)
        y = jnp.dot(x, weight_rows(w_ref, at, depth), preferred_element_type=F32)
        total = y if total is None else total + y
    out_ref[...] = total.astype(out_ref.dtype)


def begin_kernel(info_ref, own_ref, other_ref, w_ref, out_ref):
    depth = own_ref.shape[1]
    upper = info_ref[0] % 2
    y = jnp.dot(own_ref[...], weight_rows(w_ref, upper, depth), preferred_element_type=F32)
    out_ref[...] = y + jnp.dot(other_ref[...], weight_rows(w_ref, 1 - upper, depth), preferred_element_type=F32)


def pick_rows(plan_ref, pick_ref, tails):
    rows, width = pick_ref.shape
    count = rows // QLEN
    per = count // NEED
    half = per * QLEN // 2
    sub = lax.broadcasted_iota(jnp.int32, (QLEN, 1), 0)
    lane = lax.broadcasted_iota(jnp.int32, (QLEN, width), 1)
    for p in range(count):
        seg = p // per
        at = plan_ref[count + p] + sub
        here = at >= half if tails else at < half
        at = at - half + plan_ref[3 * count + NEED + seg] if tails else at + seg * half
        at = jnp.where(here & (sub < plan_ref[2 * count + p]), at, -1)
        block = pl.ds(pl.multiple_of(plan_ref[p] * QLEN, QLEN), QLEN)
        pick_ref[block, :] = jnp.where(lane == at, 1.0, 0.0).astype(BF16)


def place_kernel(plan_ref, *refs):
    *compact, out_ref, pick_ref = refs

    @pl.when(pl.program_id(0) == 0)
    def _():
        pick_rows(plan_ref, pick_ref, False)

    y = jnp.concatenate([c[...] for c in compact], axis=0)
    out_ref[...] = jnp.dot(pick_ref[...], y, preferred_element_type=F32).astype(out_ref.dtype)


def finish_kernel(info_ref, plan_ref, middle_ref, ends_ref, begun_ref, placed_ref, w_ref, out_ref, pick_ref):
    @pl.when(pl.program_id(0) == 0)
    def _():
        pick_rows(plan_ref, pick_ref, True)

    depth = middle_ref.shape[1]
    line = 2 * (w_ref.shape[0] // depth)
    y = begun_ref[...]
    for k, at in enumerate(columns(info_ref, line)[2:]):
        x = from_afar(info_ref, line, middle_ref, ends_ref, k)
        y = y + jnp.dot(x, weight_rows(w_ref, at % 2, depth), preferred_element_type=F32)
    y = jnp.dot(pick_ref[...], y.astype(BF16), preferred_element_type=F32)
    out_ref[...] = (placed_ref[...].astype(F32) + y).astype(out_ref.dtype)


SMEM = pl.BlockSpec(memory_space=pltpu.SMEM)
VMEM = pl.BlockSpec(memory_space=pltpu.VMEM)


def on_device_line(queries, kv_cache, question_slot, question_len, out_weight):
    row_count, col_count = queries.shape
    count = row_count // QLEN
    seg_rows = row_count // NEED
    half = seg_rows // 2
    image = kv_cache[0]
    tokens, dim = image.shape[0], image.shape[1] // 2
    heads = col_count // dim
    out_cols = out_weight.shape[1]
    line = lax.axis_size("tensor")
    ring = lax.axis_size("serve")
    info = jnp.stack([lax.axis_index("tensor"), lax.axis_index("serve") % 2]).astype(jnp.int32)

    kv_two = lax.ppermute(image, "serve", [(i, (i + 2) % ring) for i in range(ring)])
    kv_mix = lax.ppermute(image, "serve", [(i, i + 1) if i % 2 == 0 else (i, (i + 3) % ring) for i in range(ring)])
    params = pltpu.CompilerParams(vmem_limit_bytes=40 * MIB)
    plan_size = 3 * count + 2 * NEED + 8

    def cost(micros):
        return pl.CostEstimate(flops=int(micros * 0.3e9), bytes_accessed=image.size, transcendentals=0)

    scratch = [pltpu.VMEM((dim, tokens), BF16), pltpu.VMEM((tokens, 2 * dim), BF16)]
    plan, head0 = pl.pallas_call(
        first_kernel,
        out_shape=(
            jax.ShapeDtypeStruct((plan_size,), jnp.int32),
            jax.ShapeDtypeStruct((half, col_count), BF16),
        ),
        in_specs=[SMEM, SMEM, SMEM, VMEM, VMEM],
        out_specs=(SMEM, VMEM),
        scratch_shapes=[pltpu.SMEM((2 * NEED,), jnp.int32)] + scratch,
        compiler_params=params,
        cost_estimate=cost(5),
        name="first_head",
    )(info, question_slot, question_len, queries, image)

    def resident(*arrays):
        return [pl.BlockSpec(a.shape, lambda n: (0, 0)) for a in arrays]

    def head(seg, key_value):
        return pl.pallas_call(
            functools.partial(head_kernel, seg),
            out_shape=jax.ShapeDtypeStruct((half, col_count), BF16),
            in_specs=[SMEM, VMEM, VMEM],
            out_specs=VMEM,
            scratch_shapes=scratch,
            compiler_params=params,
            cost_estimate=cost(3),
            name="head",
        )(plan, queries, key_value)

    def tails(rows, *key_values):
        return pl.pallas_call(
            tails_kernel,
            out_shape=jax.ShapeDtypeStruct((rows, col_count), BF16),
            grid=(NEED,),
            in_specs=[SMEM] + resident(queries, *key_values),
            out_specs=pl.BlockSpec((rows, col_count), lambda n: (0, 0)),
            scratch_shapes=[pltpu.VMEM((NEED * half, col_count), BF16)] + scratch,
            compiler_params=params,
            cost_estimate=cost(8),
            name="tails",
        )(plan, queries, *key_values)

    def paired(chunk):
        return chunk, lax.ppermute(chunk, "tensor", [(i, i ^ 1) for i in range(line)])

    def crossed(chunk):
        both = jnp.concatenate(chunk, axis=0)
        return *chunk, lax.ppermute(both, "tensor", [(1, 2), (2, 1)])

    def ended(chunk):
        return *chunk, lax.ppermute(chunk[2], "tensor", [(1, 0), (2, 3)])

    tile = 512
    steps = (out_cols // tile,)
    w_spec = pl.BlockSpec((out_weight.shape[0], tile), lambda n: (0, n))

    def tiled(rows):
        return pl.BlockSpec((rows, tile), lambda n: (0, n))

    def project(*chunks):
        arrays = [a for c in chunks for a in c]
        rows = sum(c[0].shape[0] for c in chunks)
        return pl.pallas_call(
            project_kernel,
            out_shape=jax.ShapeDtypeStruct((rows, out_cols), BF16),
            grid=steps,
            in_specs=[SMEM] + resident(*arrays) + [w_spec],
            out_specs=tiled(rows),
            compiler_params=params,
            cost_estimate=cost(10),
            name="project",
        )(info, *arrays, out_weight)

    def half_weight(far):
        def index(n, info_ref):
            upper = info_ref[0] // (line // 2)
            return 1 - upper if far else upper, n

        return pl.BlockSpec((out_weight.shape[0] // 2, tile), index)

    def with_info(in_specs, out_specs, scratch_shapes=()):
        return pltpu.PrefetchScalarGridSpec(
            num_scalar_prefetch=1, grid=steps, in_specs=in_specs, out_specs=out_specs, scratch_shapes=scratch_shapes)

    def fixed(*arrays):
        return [pl.BlockSpec(a.shape, lambda n, info_ref: (0, 0)) for a in arrays]

    def strip(rows):
        return pl.BlockSpec((rows, tile), lambda n, info_ref: (0, n))

    def begin(own, other):
        rows = own.shape[0]
        return pl.pallas_call(
            begin_kernel,
            out_shape=jax.ShapeDtypeStruct((rows, out_cols), F32),
            grid_spec=with_info(fixed(own, other) + [half_weight(False)], strip(rows)),
            compiler_params=params,
            cost_estimate=cost(4),
            name="begin",
        )(info, own, other, out_weight)

    def place(*compact):
        return pl.pallas_call(
            place_kernel,
            out_shape=jax.ShapeDtypeStruct((row_count, out_cols), BF16),
            grid=steps,
            in_specs=[SMEM] + [tiled(c.shape[0]) for c in compact],
            out_specs=tiled(row_count),
            scratch_shapes=[pltpu.VMEM((row_count, sum(c.shape[0] for c in compact)), BF16)],
            compiler_params=params,
            cost_estimate=cost(5),
            name="place",
        )(plan, *compact)

    def finish(middle, ends, begun, placed):
        rows = begun.shape[0]
        return pl.pallas_call(
            finish_kernel,
            out_shape=jax.ShapeDtypeStruct((row_count, out_cols), BF16),
            grid_spec=with_info(
                [SMEM] + fixed(middle, ends) + [strip(rows), strip(row_count), half_weight(True)],
                strip(row_count),
                [pltpu.VMEM((row_count, rows), BF16)],
            ),
            compiler_params=params,
            cost_estimate=cost(5),
            name="finish",
        )(info, plan, middle, ends, begun, placed, out_weight)

    def after(value, other):
        return lax.optimization_barrier((value, other))[0]

    chunk0 = paired(head0)
    kv_two = after(kv_two, chunk0[1])
    kv_swap = lax.ppermute(kv_two, "serve", [(i, i ^ 1) for i in range(ring)])
    chunk0 = crossed(chunk0)
    head1 = head(1, kv_two)
    chunk0 = ended((*chunk0[:2], after(chunk0[2], head1)))
    chunk1 = crossed(paired(head1))
    kv_mix = after(kv_mix, chunk1[1])
    chunk2 = crossed(paired(head(2, kv_mix)))
    chunk3 = paired(head(3, kv_swap))
    chunk1 = ended(chunk1)
    rest = tails(NEED * half, image, kv_two, after(kv_mix, chunk3[1]), kv_swap)
    live_rest = plan[3 * count + 2 * NEED]
    sizes = [half * k // 4 for k in (3, 5, 6, 7, 9, 16)]

    def branch(size, rest, chunk0, chunk1, chunk2, chunk3):
        chunk2 = ended(chunk2)
        chunk3 = ended(crossed(chunk3))
        own, other, middle, ends = ended(crossed(paired(rest[:size])))
        begun = begin(own, other)
        placed = place(project(chunk0, chunk1, chunk2, chunk3))
        return finish(middle, ends, begun, placed)

    index = sum([(live_rest > s).astype(jnp.int32) for s in sizes[:-1]])
    branches = [functools.partial(branch, s) for s in sizes]
    return lax.switch(index, branches, rest, chunk0, chunk1, chunk2, chunk3)


def solution(mesh):
    plain = mesh.shape["tensor"] == KVH == 4 and mesh.shape["serve"] % 2 == 0 and NEED == 4
    return jax.shard_map(
        on_device_line if plain else on_device_general,
        mesh=mesh,
        in_specs=(
            P("serve", "tensor"),
            P("serve", "tensor", None),
            P("serve"),
            P("serve"),
            P(None, "tensor"),
        ),
        out_specs=P("serve", "tensor"),
        check_vma=False,
    )
```

```python
import functools

import jax
import jax.numpy as jnp
from jax import lax
from jax.experimental import pallas as pl
from jax.experimental.pallas import tpu as pltpu
from jax.sharding import PartitionSpec as P

KVH = 4
P_SIZE = 1600
QLEN = 32
NEED = 4
LOG2E = 1.4426950408889634
MIB = 1 << 20
F32 = jnp.float32
BF16 = jnp.bfloat16


def swapped(shard, axis, bit):
    return lax.ppermute(shard, axis, [(i, i ^ 1 << bit) for i in range(lax.axis_size(axis))])


def shifted(value, axis, steps):
    count = lax.axis_size(axis)
    pairs = [(source, (source + steps) % count) for source in range(count)]
    return lax.ppermute(value, axis, pairs)


def attend(query_rows, key_value):
    row_count = query_rows.shape[0]
    head_count = key_value.shape[0]
    head_dim = key_value.shape[2] // 2
    grouped = query_rows.reshape(row_count, head_count, -1, head_dim)
    key_part = key_value[:, :, :head_dim]
    value_part = key_value[:, :, head_dim:]
    scores = jnp.einsum(
        "rkgd,kpd->kgrp", grouped, key_part, preferred_element_type=jnp.float32
    ) * head_dim ** (-0.5)
    row_max = jnp.max(scores, axis=3, keepdims=True)
    exp_scores = jnp.exp(scores - row_max)
    sum_exp = jnp.sum(exp_scores, axis=3, keepdims=True)
    weights = (exp_scores / sum_exp).astype(jnp.bfloat16)
    blended = jnp.einsum("kgrp,kpd->rkgd", weights, value_part, preferred_element_type=jnp.float32)
    return blended.reshape(row_count, -1)


def on_device_general(queries, kv_cache, question_slot, question_len, out_weight):
    row_count, col_count = queries.shape
    head_dim = kv_cache.shape[2] // 2
    question_count = row_count // QLEN
    per_slot = question_count // NEED
    head_piece = kv_cache[0]
    sharing = lax.axis_size("tensor") // KVH
    if sharing > 1:
        for bit_number in range(sharing.bit_length() - 1):
            partner_piece = swapped(head_piece, "tensor", bit_number)
            upper_member = lax.axis_index("tensor") // 2**bit_number % 2 == 1
            head_piece = jnp.where(
                upper_member,
                jnp.concatenate([partner_piece, head_piece], axis=0),
                jnp.concatenate([head_piece, partner_piece], axis=0),
            )
    key_value = head_piece.reshape(-1, P_SIZE, 2 * head_dim)
    ordering = jnp.argsort(question_slot, stable=True)
    inverse_order = jnp.argsort(ordering, stable=True)
    sorted_rows = queries.reshape(question_count, QLEN, col_count)[ordering]
    sorted_rows = sorted_rows.reshape(NEED, per_slot * QLEN, col_count)
    results = []
    for offset_back in range(NEED):
        if offset_back == 0:
            remote = key_value
        else:
            remote = shifted(key_value, "serve", offset_back)
        results.append(attend(sorted_rows[offset_back], remote))
    sorted_out = jnp.stack(results).reshape(question_count, QLEN, col_count)
    blended = sorted_out[inverse_order].reshape(row_count, col_count)
    token_pos = jnp.arange(row_count, dtype=jnp.int32) % QLEN
    live_rows = token_pos < jnp.repeat(question_len, QLEN, total_repeat_length=row_count)
    attended = jnp.where(live_rows[:, None], blended, 0.0).astype(jnp.bfloat16)
    zero_sum = jnp.zeros((row_count, out_weight.shape[1]), jnp.float32)
    gathered_cols = lax.all_gather(attended, "tensor", axis=1, tiled=True)
    weight_rows = lax.slice_in_dim(out_weight, 0, gathered_cols.shape[1], axis=0)
    answers = zero_sum + jnp.dot(gathered_cols, weight_rows, preferred_element_type=jnp.float32)
    return answers.astype(jnp.bfloat16)


def make_plan(info_ref, slot_ref, len_ref, plan_ref, work_ref):
    count = slot_ref.shape[0]
    per = count // NEED
    half = per * QLEN // 2
    odd = info_ref[1]
    for g in range(NEED):
        work_ref[g] = g * per
        work_ref[NEED + g] = 0

    def step(q, carry):
        slot = slot_ref[q]
        length = len_ref[q]
        last = jnp.where(slot == 1, 3 - odd, 2 + odd)
        seg = jnp.where(slot == 0, 0, jnp.where(slot == 2, 1, last))
        at = work_ref[seg]
        first = work_ref[NEED + seg]
        plan_ref[at] = q
        plan_ref[count + at] = first
        plan_ref[2 * count + at] = length
        work_ref[seg] = at + 1
        work_ref[NEED + seg] = first + length
        return carry

    lax.fori_loop(0, count, step, 0)
    begin = jnp.int32(0)
    for g in range(NEED):
        live = work_ref[NEED + g]
        plan_ref[3 * count + g] = live
        plan_ref[3 * count + NEED + g] = begin
        begin = begin + jnp.maximum(live - half, 0)
    plan_ref[3 * count + 2 * NEED] = begin


def segment_rows(q_ref, plan_ref, seg, low, rows):
    count = q_ref.shape[0] // QLEN
    per = count // NEED
    width = per * QLEN
    lane = lax.broadcasted_iota(jnp.int32, (1, width), 1)
    owner = lane // QLEN
    inner = lane % QLEN
    first = jnp.zeros((1, width), jnp.int32)
    length = jnp.zeros((1, width), jnp.int32)
    blocks = []
    for k in range(per):
        q = plan_ref[seg * per + k]
        blocks.append(q_ref[pl.ds(pl.multiple_of(q * QLEN, QLEN), QLEN), :])
        first = jnp.where(owner == k, plan_ref[count + seg * per + k], first)
        length = jnp.where(owner == k, plan_ref[2 * count + seg * per + k], length)
    target = jnp.where(inner < length, first + inner, -1)
    row = lax.broadcasted_iota(jnp.int32, (rows, width), 0) + low
    pick = jnp.where(row == target, 1.0, 0.0).astype(BF16)
    return jnp.dot(pick, jnp.concatenate(blocks, axis=0), preferred_element_type=F32).astype(BF16)


def load_image(kv_ref, keys_ref, ones_ref):
    dim = kv_ref.shape[1] // 2
    keys_ref[...] = kv_ref[:, :dim].T
    ones_ref[:, :dim] = kv_ref[:, dim:]
    ones_ref[:, dim:] = jnp.ones((kv_ref.shape[0], dim), BF16)


def attend_rows(x, keys_ref, ones_ref, out_ref, base):
    dim = keys_ref.shape[0]
    rows, cols = x.shape
    heads = cols // dim
    group = max(1, min(heads, 256 // rows))
    for low in range(0, heads, group):
        members = range(low, min(low + group, heads))
        q = [x[:, h * dim:(h + 1) * dim] for h in members]
        q = q[0] if len(q) == 1 else jnp.concatenate(q, axis=0)
        s = jnp.dot(q, keys_ref[...], preferred_element_type=F32)
        top = jnp.max(s, axis=1, keepdims=True)
        e = jnp.exp2((s - top) * (LOG2E * dim ** (-0.5))).astype(BF16)
        o = jnp.dot(e, ones_ref[...], preferred_element_type=F32)
        o = (o[:, :dim] / o[:, dim:]).astype(BF16)
        for i, h in enumerate(members):
            out_ref[pl.ds(base, rows), h * dim:(h + 1) * dim] = o[i * rows:(i + 1) * rows, :]


def first_kernel(info_ref, slot_ref, len_ref, q_ref, kv_ref, plan_ref, out_ref, work_ref, keys_ref, ones_ref):
    make_plan(info_ref, slot_ref, len_ref, plan_ref, work_ref)
    load_image(kv_ref, keys_ref, ones_ref)
    attend_rows(segment_rows(q_ref, plan_ref, 0, 0, out_ref.shape[0]), keys_ref, ones_ref, out_ref, 0)


def head_kernel(seg, plan_ref, q_ref, kv_ref, out_ref, keys_ref, ones_ref):
    load_image(kv_ref, keys_ref, ones_ref)
    attend_rows(segment_rows(q_ref, plan_ref, seg, 0, out_ref.shape[0]), keys_ref, ones_ref, out_ref, 0)


def tails_kernel(plan_ref, q_ref, kv0_ref, kv1_ref, kv2_ref, kv3_ref, out_ref, tails_ref, keys_ref, ones_ref):
    count = q_ref.shape[0] // QLEN
    width = tails_ref.shape[0]
    half = width // NEED
    seg = pl.program_id(0)
    live = plan_ref[3 * count + seg] - half

    @pl.when(seg == 0)
    def _():
        tails_ref[...] = jnp.zeros(tails_ref.shape, tails_ref.dtype)

    for g, kv_ref in enumerate((kv0_ref, kv1_ref, kv2_ref, kv3_ref)):
        @pl.when((seg == g) & (live > 0))
        def _():
            load_image(kv_ref, keys_ref, ones_ref)

    for low, high in ((0, half // 4), (half // 4, half // 2), (half // 2, half)):
        @pl.when((live > low) & (live <= high))
        def _():
            x = segment_rows(q_ref, plan_ref, seg, half, high)
            attend_rows(x, keys_ref, ones_ref, tails_ref, pl.multiple_of(seg * half, half))

    @pl.when(seg == NEED - 1)
    def _():
        lane = lax.broadcasted_iota(jnp.int32, (1, width), 1)
        target = jnp.full((1, width), -1, jnp.int32)
        for g in range(NEED):
            inner = lane - g * half
            here = (inner >= 0) & (inner < plan_ref[3 * count + g] - half)
            target = jnp.where(here, plan_ref[3 * count + NEED + g] + inner, target)
        row = lax.broadcasted_iota(jnp.int32, (out_ref.shape[0], width), 0)
        pick = jnp.where(row == target, 1.0, 0.0).astype(BF16)
        out_ref[...] = jnp.dot(pick, tails_ref[...], preferred_element_type=F32).astype(BF16)


def columns(info_ref, line):
    me = info_ref[0]
    upper = me >= line // 2
    pair = jnp.where(upper, 5 - me, 1 - me)
    return me, pair, jnp.where(upper, 1, 2), jnp.where(upper, 0, 3)


def from_afar(info_ref, line, middle_ref, ends_ref, k):
    me = info_ref[0]
    rows = middle_ref.shape[0] // 2
    part = pl.ds(k * rows, rows)
    return jnp.where((me == 0) | (me == line - 1), ends_ref[part, :], middle_ref[part, :])


def over_columns(out_ref, body):
    wide = min(256, out_ref.shape[1])

    def step(n, carry):
        cols = pl.ds(pl.multiple_of(n * wide, wide), wide)
        out_ref[:, cols] = body(cols).astype(out_ref.dtype)
        return carry

    lax.fori_loop(0, out_ref.shape[1] // wide, step, 0)


def project_kernel(info_ref, *refs):
    *chunks, w_ref, out_ref, x_ref = refs
    depth = chunks[0].shape[1]
    line = w_ref.shape[0] // depth
    places = columns(info_ref, line)

    @pl.when(pl.program_id(0) == 0)
    def _():
        low = 0
        for own, other, middle, ends in zip(chunks[0::4], chunks[1::4], chunks[2::4], chunks[3::4]):
            rows = pl.ds(low, own.shape[0])
            x_ref[0, rows, :] = own[...]
            x_ref[1, rows, :] = other[...]
            x_ref[2, rows, :] = from_afar(info_ref, line, middle, ends, 0)
            x_ref[3, rows, :] = from_afar(info_ref, line, middle, ends, 1)
            low += own.shape[0]

    def body(cols):
        total = None
        for k, at in enumerate(places):
            w = w_ref[pl.ds(pl.multiple_of(at * depth, depth), depth), cols]
            y = jnp.dot(x_ref[k], w, preferred_element_type=F32)
            total = y if total is None else total + y
        return total

    over_columns(out_ref, body)


def begin_kernel(info_ref, own_ref, other_ref, w_ref, out_ref):
    depth = own_ref.shape[1]
    upper = info_ref[0] % 2

    def body(cols):
        total = None
        for x_ref, at in ((own_ref, upper), (other_ref, 1 - upper)):
            w = w_ref[pl.ds(pl.multiple_of(at * depth, depth), depth), cols]
            y = jnp.dot(x_ref[...], w, preferred_element_type=F32)
            total = y if total is None else total + y
        return total

    over_columns(out_ref, body)


def pick_rows(plan_ref, pick_ref, tails):
    rows, width = pick_ref.shape
    count = rows // QLEN
    per = count // NEED
    half = per * QLEN // 2
    sub = lax.broadcasted_iota(jnp.int32, (QLEN, 1), 0)
    lane = lax.broadcasted_iota(jnp.int32, (QLEN, width), 1)

    def step(p, carry):
        seg = p // per
        at = plan_ref[count + p] + sub
        here = at >= half if tails else at < half
        at = at - half + plan_ref[3 * count + NEED + seg] if tails else at + seg * half
        at = jnp.where(here & (sub < plan_ref[2 * count + p]), at, -1)
        block = pl.ds(pl.multiple_of(plan_ref[p] * QLEN, QLEN), QLEN)
        pick_ref[block, :] = jnp.where(lane == at, 1.0, 0.0).astype(BF16)
        return carry

    lax.fori_loop(0, count, step, 0)


def over_rows(pick_ref, y, out_ref, placed_ref=None):
    tall = out_ref.shape[0] // 4

    def step(i, carry):
        rows = pl.ds(pl.multiple_of(i * tall, tall), tall)
        z = jnp.dot(pick_ref[rows, :], y, preferred_element_type=F32)
        if placed_ref is not None:
            z = z + placed_ref[rows, :].astype(F32)
        out_ref[rows, :] = z.astype(out_ref.dtype)
        return carry

    lax.fori_loop(0, 4, step, 0)


def place_kernel(plan_ref, *refs):
    *compact, out_ref, pick_ref = refs

    @pl.when(pl.program_id(0) == 0)
    def _():
        pick_rows(plan_ref, pick_ref, False)

    over_rows(pick_ref, jnp.concatenate([c[...] for c in compact], axis=0), out_ref)


def finish_kernel(info_ref, plan_ref, middle_ref, ends_ref, begun_ref, placed_ref, w_ref, out_ref, pick_ref, x_ref, y_ref):
    depth = middle_ref.shape[1]
    line = 2 * (w_ref.shape[0] // depth)
    places = columns(info_ref, line)[2:]

    @pl.when(pl.program_id(0) == 0)
    def _():
        pick_rows(plan_ref, pick_ref, True)
        for k in range(2):
            x_ref[k] = from_afar(info_ref, line, middle_ref, ends_ref, k)

    def body(cols):
        total = begun_ref[:, cols]
        for k, at in enumerate(places):
            w = w_ref[pl.ds(pl.multiple_of(at % 2 * depth, depth), depth), cols]
            total = total + jnp.dot(x_ref[k], w, preferred_element_type=F32)
        return total

    over_columns(y_ref, body)
    over_rows(pick_ref, y_ref[...], out_ref, placed_ref)


SMEM = pl.BlockSpec(memory_space=pltpu.SMEM)
VMEM = pl.BlockSpec(memory_space=pltpu.VMEM)


def on_device_line(queries, kv_cache, question_slot, question_len, out_weight):
    row_count, col_count = queries.shape
    count = row_count // QLEN
    seg_rows = row_count // NEED
    half = seg_rows // 2
    image = kv_cache[0]
    tokens, dim = image.shape[0], image.shape[1] // 2
    heads = col_count // dim
    out_cols = out_weight.shape[1]
    line = lax.axis_size("tensor")
    ring = lax.axis_size("serve")
    info = jnp.stack([lax.axis_index("tensor"), lax.axis_index("serve") % 2]).astype(jnp.int32)

    kv_two = lax.ppermute(image, "serve", [(i, (i + 2) % ring) for i in range(ring)])
    kv_mix = lax.ppermute(image, "serve", [(i, i + 1) if i % 2 == 0 else (i, (i + 3) % ring) for i in range(ring)])
    params = pltpu.CompilerParams(vmem_limit_bytes=40 * MIB)
    plan_size = 3 * count + 2 * NEED + 8

    def cost(micros):
        return pl.CostEstimate(flops=int(micros * 0.3e9), bytes_accessed=image.size, transcendentals=0)

    scratch = [pltpu.VMEM((dim, tokens), BF16), pltpu.VMEM((tokens, 2 * dim), BF16)]
    plan, head0 = pl.pallas_call(
        first_kernel,
        out_shape=(
            jax.ShapeDtypeStruct((plan_size,), jnp.int32),
            jax.ShapeDtypeStruct((half, col_count), BF16),
        ),
        in_specs=[SMEM, SMEM, SMEM, VMEM, VMEM],
        out_specs=(SMEM, VMEM),
        scratch_shapes=[pltpu.SMEM((2 * NEED,), jnp.int32)] + scratch,
        compiler_params=params,
        cost_estimate=cost(5),
        name="first_head",
    )(info, question_slot, question_len, queries, image)

    def resident(*arrays):
        return [pl.BlockSpec(a.shape, lambda n: (0, 0)) for a in arrays]

    def head(seg, key_value):
        return pl.pallas_call(
            functools.partial(head_kernel, seg),
            out_shape=jax.ShapeDtypeStruct((half, col_count), BF16),
            in_specs=[SMEM, VMEM, VMEM],
            out_specs=VMEM,
            scratch_shapes=scratch,
            compiler_params=params,
            cost_estimate=cost(3),
            name="head",
        )(plan, queries, key_value)

    def tails(rows, *key_values):
        return pl.pallas_call(
            tails_kernel,
            out_shape=jax.ShapeDtypeStruct((rows, col_count), BF16),
            grid=(NEED,),
            in_specs=[SMEM] + resident(queries, *key_values),
            out_specs=pl.BlockSpec((rows, col_count), lambda n: (0, 0)),
            scratch_shapes=[pltpu.VMEM((NEED * half, col_count), BF16)] + scratch,
            compiler_params=params,
            cost_estimate=cost(8),
            name="tails",
        )(plan, queries, *key_values)

    def paired(chunk):
        return chunk, lax.ppermute(chunk, "tensor", [(i, i ^ 1) for i in range(line)])

    def crossed(chunk):
        both = jnp.concatenate(chunk, axis=0)
        return *chunk, lax.ppermute(both, "tensor", [(1, 2), (2, 1)])

    def ended(chunk):
        return *chunk, lax.ppermute(chunk[2], "tensor", [(1, 0), (2, 3)])

    tile = 512
    steps = (out_cols // tile,)
    w_spec = pl.BlockSpec((out_weight.shape[0], tile), lambda n: (0, n))

    def tiled(rows):
        return pl.BlockSpec((rows, tile), lambda n: (0, n))

    def project(*chunks):
        arrays = [a for c in chunks for a in c]
        rows = sum(c[0].shape[0] for c in chunks)
        return pl.pallas_call(
            project_kernel,
            out_shape=jax.ShapeDtypeStruct((rows, out_cols), BF16),
            grid=steps,
            in_specs=[SMEM] + resident(*arrays) + [w_spec],
            out_specs=tiled(rows),
            scratch_shapes=[pltpu.VMEM((line, rows, col_count), BF16)],
            compiler_params=params,
            cost_estimate=cost(10),
            name="project",
        )(info, *arrays, out_weight)

    def half_weight(far):
        def index(n, info_ref):
            upper = info_ref[0] // (line // 2)
            return 1 - upper if far else upper, n

        return pl.BlockSpec((out_weight.shape[0] // 2, tile), index)

    def with_info(in_specs, out_specs, scratch_shapes=()):
        return pltpu.PrefetchScalarGridSpec(
            num_scalar_prefetch=1, grid=steps, in_specs=in_specs, out_specs=out_specs, scratch_shapes=scratch_shapes)

    def fixed(*arrays):
        return [pl.BlockSpec(a.shape, lambda n, info_ref: (0, 0)) for a in arrays]

    def strip(rows):
        return pl.BlockSpec((rows, tile), lambda n, info_ref: (0, n))

    def begin(own, other):
        rows = own.shape[0]
        return pl.pallas_call(
            begin_kernel,
            out_shape=jax.ShapeDtypeStruct((rows, out_cols), F32),
            grid_spec=with_info(fixed(own, other) + [half_weight(False)], strip(rows)),
            compiler_params=params,
            cost_estimate=cost(4),
            name="begin",
        )(info, own, other, out_weight)

    def place(*compact):
        return pl.pallas_call(
            place_kernel,
            out_shape=jax.ShapeDtypeStruct((row_count, out_cols), BF16),
            grid=steps,
            in_specs=[SMEM] + [tiled(c.shape[0]) for c in compact],
            out_specs=tiled(row_count),
            scratch_shapes=[pltpu.VMEM((row_count, sum(c.shape[0] for c in compact)), BF16)],
            compiler_params=params,
            cost_estimate=cost(5),
            name="place",
        )(plan, *compact)

    def finish(middle, ends, begun, placed):
        rows = begun.shape[0]
        return pl.pallas_call(
            finish_kernel,
            out_shape=jax.ShapeDtypeStruct((row_count, out_cols), BF16),
            grid_spec=with_info(
                [SMEM] + fixed(middle, ends) + [strip(rows), strip(row_count), half_weight(True)],
                strip(row_count),
                [
                    pltpu.VMEM((row_count, rows), BF16),
                    pltpu.VMEM((2, rows, col_count), BF16),
                    pltpu.VMEM((rows, tile), BF16),
                ],
            ),
            compiler_params=params,
            cost_estimate=cost(5),
            name="finish",
        )(info, plan, middle, ends, begun, placed, out_weight)

    def after(value, other):
        return lax.optimization_barrier((value, other))[0]

    chunk0 = paired(head0)
    kv_two, chunk0 = lax.optimization_barrier((kv_two, chunk0))
    kv_swap = lax.ppermute(kv_two, "serve", [(i, i ^ 1) for i in range(ring)])
    chunk0 = crossed(chunk0)
    chunk1 = paired(head(1, kv_two))
    kv_mix = after(kv_mix, chunk1[1])
    chunk0 = ended(chunk0)
    chunk1 = crossed(chunk1)
    kv_swap = after(kv_swap, chunk0[3])
    chunk2 = crossed(paired(head(2, kv_mix)))
    chunk3 = crossed(paired(head(3, kv_swap)))
    chunk1 = ended(chunk1)
    chunk2 = ended(chunk2)
    rest = tails(NEED * half, image, kv_two, after(kv_mix, chunk3[1]), kv_swap)
    done01 = project(chunk0, chunk1)
    live_rest = plan[3 * count + 2 * NEED]
    sizes = [half * k // 4 for k in (3, 5, 6, 7, 9, 16)]

    def branch(size, rest, done01, chunk2, chunk3):
        own, other = paired(rest[:size])
        chunk3 = ended(chunk3)
        own, other, middle, ends = ended(crossed((own, other)))
        begun = begin(own, other)
        placed = place(done01, project(chunk2, chunk3))
        return finish(middle, ends, begun, placed)

    index = sum([(live_rest > s).astype(jnp.int32) for s in sizes[:-1]])
    branches = [functools.partial(branch, s) for s in sizes]
    return lax.switch(index, branches, rest, done01, chunk2, chunk3)


def solution(mesh):
    plain = mesh.shape["tensor"] == KVH == 4 and mesh.shape["serve"] % 2 == 0 and NEED == 4
    return jax.shard_map(
        on_device_line if plain else on_device_general,
        mesh=mesh,
        in_specs=(
            P("serve", "tensor"),
            P("serve", "tensor", None),
            P("serve"),
            P("serve"),
            P(None, "tensor"),
        ),
        out_specs=P("serve", "tensor"),
        check_vma=False,
    )
```

```python
import functools

import jax
import jax.numpy as jnp
from jax import lax
from jax.experimental import pallas as pl
from jax.experimental.pallas import tpu as pltpu
from jax.sharding import PartitionSpec as P

KVH = 4
P_SIZE = 1600
QLEN = 32
NEED = 4
LOG2E = 1.4426950408889634
MIB = 1 << 20
F32 = jnp.float32
BF16 = jnp.bfloat16


def swapped(shard, axis, bit):
    return lax.ppermute(shard, axis, [(i, i ^ 1 << bit) for i in range(lax.axis_size(axis))])


def shifted(value, axis, steps):
    count = lax.axis_size(axis)
    pairs = [(source, (source + steps) % count) for source in range(count)]
    return lax.ppermute(value, axis, pairs)


def attend(query_rows, key_value):
    row_count = query_rows.shape[0]
    head_count = key_value.shape[0]
    head_dim = key_value.shape[2] // 2
    grouped = query_rows.reshape(row_count, head_count, -1, head_dim)
    key_part = key_value[:, :, :head_dim]
    value_part = key_value[:, :, head_dim:]
    scores = jnp.einsum(
        "rkgd,kpd->kgrp", grouped, key_part, preferred_element_type=jnp.float32
    ) * head_dim ** (-0.5)
    row_max = jnp.max(scores, axis=3, keepdims=True)
    exp_scores = jnp.exp(scores - row_max)
    sum_exp = jnp.sum(exp_scores, axis=3, keepdims=True)
    weights = (exp_scores / sum_exp).astype(jnp.bfloat16)
    blended = jnp.einsum("kgrp,kpd->rkgd", weights, value_part, preferred_element_type=jnp.float32)
    return blended.reshape(row_count, -1)


def on_device_general(queries, kv_cache, question_slot, question_len, out_weight):
    row_count, col_count = queries.shape
    head_dim = kv_cache.shape[2] // 2
    question_count = row_count // QLEN
    per_slot = question_count // NEED
    head_piece = kv_cache[0]
    sharing = lax.axis_size("tensor") // KVH
    if sharing > 1:
        for bit_number in range(sharing.bit_length() - 1):
            partner_piece = swapped(head_piece, "tensor", bit_number)
            upper_member = lax.axis_index("tensor") // 2**bit_number % 2 == 1
            head_piece = jnp.where(
                upper_member,
                jnp.concatenate([partner_piece, head_piece], axis=0),
                jnp.concatenate([head_piece, partner_piece], axis=0),
            )
    key_value = head_piece.reshape(-1, P_SIZE, 2 * head_dim)
    ordering = jnp.argsort(question_slot, stable=True)
    inverse_order = jnp.argsort(ordering, stable=True)
    sorted_rows = queries.reshape(question_count, QLEN, col_count)[ordering]
    sorted_rows = sorted_rows.reshape(NEED, per_slot * QLEN, col_count)
    results = []
    for offset_back in range(NEED):
        if offset_back == 0:
            remote = key_value
        else:
            remote = shifted(key_value, "serve", offset_back)
        results.append(attend(sorted_rows[offset_back], remote))
    sorted_out = jnp.stack(results).reshape(question_count, QLEN, col_count)
    blended = sorted_out[inverse_order].reshape(row_count, col_count)
    token_pos = jnp.arange(row_count, dtype=jnp.int32) % QLEN
    live_rows = token_pos < jnp.repeat(question_len, QLEN, total_repeat_length=row_count)
    attended = jnp.where(live_rows[:, None], blended, 0.0).astype(jnp.bfloat16)
    zero_sum = jnp.zeros((row_count, out_weight.shape[1]), jnp.float32)
    gathered_cols = lax.all_gather(attended, "tensor", axis=1, tiled=True)
    weight_rows = lax.slice_in_dim(out_weight, 0, gathered_cols.shape[1], axis=0)
    answers = zero_sum + jnp.dot(gathered_cols, weight_rows, preferred_element_type=jnp.float32)
    return answers.astype(jnp.bfloat16)


def make_plan(info_ref, slot_ref, len_ref, plan_ref, work_ref):
    count = slot_ref.shape[0]
    per = count // NEED
    half = per * QLEN // 2
    odd = info_ref[1]
    for g in range(NEED):
        work_ref[g] = g * per
        work_ref[NEED + g] = 0

    def step(q, carry):
        slot = slot_ref[q]
        length = len_ref[q]
        last = jnp.where(slot == 1, 3 - odd, 2 + odd)
        seg = jnp.where(slot == 0, 0, jnp.where(slot == 2, 1, last))
        at = work_ref[seg]
        first = work_ref[NEED + seg]
        plan_ref[at] = q
        plan_ref[count + at] = first
        plan_ref[2 * count + at] = length
        work_ref[seg] = at + 1
        work_ref[NEED + seg] = first + length
        return carry

    lax.fori_loop(0, count, step, 0)
    begin = jnp.int32(0)
    for g in range(NEED):
        live = work_ref[NEED + g]
        plan_ref[3 * count + g] = live
        plan_ref[3 * count + NEED + g] = begin
        begin = begin + jnp.maximum(live - half, 0)
    plan_ref[3 * count + 2 * NEED] = begin


def segment_rows(q_ref, plan_ref, seg, low, rows):
    count = q_ref.shape[0] // QLEN
    per = count // NEED
    width = per * QLEN
    lane = lax.broadcasted_iota(jnp.int32, (1, width), 1)
    owner = lane // QLEN
    inner = lane % QLEN
    first = jnp.zeros((1, width), jnp.int32)
    length = jnp.zeros((1, width), jnp.int32)
    blocks = []
    for k in range(per):
        q = plan_ref[seg * per + k]
        blocks.append(q_ref[pl.ds(pl.multiple_of(q * QLEN, QLEN), QLEN), :])
        first = jnp.where(owner == k, plan_ref[count + seg * per + k], first)
        length = jnp.where(owner == k, plan_ref[2 * count + seg * per + k], length)
    target = jnp.where(inner < length, first + inner, -1)
    row = lax.broadcasted_iota(jnp.int32, (rows, width), 0) + low
    pick = jnp.where(row == target, 1.0, 0.0).astype(BF16)
    return jnp.dot(pick, jnp.concatenate(blocks, axis=0), preferred_element_type=F32).astype(BF16)


def load_image(kv_ref, keys_ref, ones_ref):
    dim = kv_ref.shape[1] // 2
    keys_ref[...] = kv_ref[:, :dim].T
    ones_ref[:, :dim] = kv_ref[:, dim:]
    ones_ref[:, dim:] = jnp.ones((kv_ref.shape[0], dim), BF16)


def attend_rows(x, keys_ref, ones_ref, out_ref, base):
    dim = keys_ref.shape[0]
    rows, cols = x.shape
    heads = cols // dim
    group = max(1, min(heads, 256 // rows))
    for low in range(0, heads, group):
        members = range(low, min(low + group, heads))
        q = [x[:, h * dim:(h + 1) * dim] for h in members]
        q = q[0] if len(q) == 1 else jnp.concatenate(q, axis=0)
        s = jnp.dot(q, keys_ref[...], preferred_element_type=F32)
        top = jnp.max(s, axis=1, keepdims=True)
        e = jnp.exp2((s - top) * (LOG2E * dim ** (-0.5))).astype(BF16)
        o = jnp.dot(e, ones_ref[...], preferred_element_type=F32)
        o = (o[:, :dim] / o[:, dim:]).astype(BF16)
        for i, h in enumerate(members):
            out_ref[pl.ds(base, rows), h * dim:(h + 1) * dim] = o[i * rows:(i + 1) * rows, :]


def first_kernel(info_ref, slot_ref, len_ref, q_ref, kv_ref, plan_ref, out_ref, work_ref, keys_ref, ones_ref):
    make_plan(info_ref, slot_ref, len_ref, plan_ref, work_ref)
    load_image(kv_ref, keys_ref, ones_ref)
    attend_rows(segment_rows(q_ref, plan_ref, 0, 0, out_ref.shape[0]), keys_ref, ones_ref, out_ref, 0)


def head_kernel(seg, plan_ref, q_ref, kv_ref, out_ref, keys_ref, ones_ref):
    load_image(kv_ref, keys_ref, ones_ref)
    attend_rows(segment_rows(q_ref, plan_ref, seg, 0, out_ref.shape[0]), keys_ref, ones_ref, out_ref, 0)


def tails_kernel(plan_ref, q_ref, kv0_ref, kv1_ref, kv2_ref, kv3_ref, out_ref, tails_ref, keys_ref, ones_ref):
    count = q_ref.shape[0] // QLEN
    width = tails_ref.shape[0]
    half = width // NEED
    seg = pl.program_id(0)
    live = plan_ref[3 * count + seg] - half

    @pl.when(seg == 0)
    def _():
        tails_ref[...] = jnp.zeros(tails_ref.shape, tails_ref.dtype)

    for g, kv_ref in enumerate((kv0_ref, kv1_ref, kv2_ref, kv3_ref)):
        @pl.when((seg == g) & (live > 0))
        def _():
            load_image(kv_ref, keys_ref, ones_ref)

    for low, high in ((0, half // 4), (half // 4, half // 2), (half // 2, half)):
        @pl.when((live > low) & (live <= high))
        def _():
            x = segment_rows(q_ref, plan_ref, seg, half, high)
            attend_rows(x, keys_ref, ones_ref, tails_ref, pl.multiple_of(seg * half, half))

    @pl.when(seg == NEED - 1)
    def _():
        lane = lax.broadcasted_iota(jnp.int32, (1, width), 1)
        target = jnp.full((1, width), -1, jnp.int32)
        for g in range(NEED):
            inner = lane - g * half
            here = (inner >= 0) & (inner < plan_ref[3 * count + g] - half)
            target = jnp.where(here, plan_ref[3 * count + NEED + g] + inner, target)
        row = lax.broadcasted_iota(jnp.int32, (out_ref.shape[0], width), 0)
        pick = jnp.where(row == target, 1.0, 0.0).astype(BF16)
        out_ref[...] = jnp.dot(pick, tails_ref[...], preferred_element_type=F32).astype(BF16)


def columns(info_ref, line):
    me = info_ref[0]
    upper = me >= line // 2
    pair = jnp.where(upper, 5 - me, 1 - me)
    return me, pair, jnp.where(upper, 1, 2), jnp.where(upper, 0, 3)


def from_afar(info_ref, line, middle_ref, ends_ref, k):
    me = info_ref[0]
    rows = middle_ref.shape[0] // 2
    part = pl.ds(k * rows, rows)
    return jnp.where((me == 0) | (me == line - 1), ends_ref[part, :], middle_ref[part, :])


def project_kernel(info_ref, *refs):
    *chunks, w_ref, out_ref = refs
    depth = chunks[0].shape[1]
    line = w_ref.shape[0] // depth
    total = None
    for k, at in enumerate(columns(info_ref, line)):
        if k < 2:
            pieces = [c[...] for c in chunks[k::4]]
        else:
            pieces = [from_afar(info_ref, line, m, e, k - 2) for m, e in zip(chunks[2::4], chunks[3::4])]
        x = pieces[0] if len(pieces) == 1 else jnp.concatenate(pieces, axis=0)
        w = w_ref[pl.ds(pl.multiple_of(at * depth, depth), depth), :]
        y = jnp.dot(x, w, preferred_element_type=F32)
        total = y if total is None else total + y
    out_ref[...] = total.astype(out_ref.dtype)


def pick_rows(plan_ref, pick_ref, segs, tails):
    rows, width = pick_ref.shape
    count = rows // QLEN
    per = count // NEED
    half = per * QLEN // 2
    sub = lax.broadcasted_iota(jnp.int32, (QLEN, 1), 0)
    lane = lax.broadcasted_iota(jnp.int32, (QLEN, width), 1)
    for seg in range(NEED):
        def step(p, carry):
            at = plan_ref[count + p] + sub
            head = at + (seg - segs[0]) * half if seg in segs else jnp.full_like(at, -1)
            tail = at + (len(segs) - 1) * half + plan_ref[3 * count + NEED + seg] if tails else jnp.full_like(at, -1)
            at = jnp.where(at < half, head, tail)
            at = jnp.where(sub < plan_ref[2 * count + p], at, -1)
            block = pl.ds(pl.multiple_of(plan_ref[p] * QLEN, QLEN), QLEN)
            pick_ref[block, :] = jnp.where(lane == at, 1.0, 0.0).astype(BF16)
            return carry

        lax.fori_loop(seg * per, (seg + 1) * per, step, 0, unroll=4)


def place_kernel(segs, plan_ref, compact_ref, out_ref, pick_ref):
    @pl.when(pl.program_id(0) == 0)
    def _():
        pick_rows(plan_ref, pick_ref, segs, False)

    out_ref[...] = jnp.dot(pick_ref[...], compact_ref[...], preferred_element_type=F32).astype(out_ref.dtype)


def begin_kernel(segs, info_ref, plan_ref, own3_ref, other3_ref, own_ref, other_ref, w_ref, out_ref, pick_ref):
    @pl.when(pl.program_id(0) == 0)
    def _():
        pick_rows(plan_ref, pick_ref, segs, True)

    depth = own_ref.shape[1]
    upper = info_ref[0] % 2
    total = None
    for x_refs, at in (((own3_ref, own_ref), upper), ((other3_ref, other_ref), 1 - upper)):
        x = jnp.concatenate([r[...] for r in x_refs], axis=0)
        w = w_ref[pl.ds(pl.multiple_of(at * depth, depth), depth), :]
        y = jnp.dot(x, w, preferred_element_type=F32)
        total = y if total is None else total + y
    out_ref[...] = total


def finish_kernel(info_ref, middle3_ref, ends3_ref, middle_ref, ends_ref, pick_ref, begun_ref, done_ref, placed_ref,
                  w_ref, out_ref, x_ref):
    depth = middle_ref.shape[1]
    line = 2 * (w_ref.shape[0] // depth)
    places = columns(info_ref, line)[2:]

    @pl.when(pl.program_id(0) == 0)
    def _():
        low = middle3_ref.shape[0] // 2
        for k in range(2):
            x_ref[k, :low, :] = from_afar(info_ref, line, middle3_ref, ends3_ref, k)
            x_ref[k, low:, :] = from_afar(info_ref, line, middle_ref, ends_ref, k)

    y = begun_ref[...]
    for k, at in enumerate(places):
        w = w_ref[pl.ds(pl.multiple_of(at % 2 * depth, depth), depth), :]
        y = y + jnp.dot(x_ref[k], w, preferred_element_type=F32)
    y = jnp.concatenate([done_ref[...], y.astype(BF16)], axis=0)
    z = jnp.dot(pick_ref[...], y, preferred_element_type=F32)
    out_ref[...] = (placed_ref[...].astype(F32) + z).astype(out_ref.dtype)


SMEM = pl.BlockSpec(memory_space=pltpu.SMEM)
VMEM = pl.BlockSpec(memory_space=pltpu.VMEM)


def on_device_line(queries, kv_cache, question_slot, question_len, out_weight):
    row_count, col_count = queries.shape
    count = row_count // QLEN
    seg_rows = row_count // NEED
    half = seg_rows // 2
    image = kv_cache[0]
    tokens, dim = image.shape[0], image.shape[1] // 2
    heads = col_count // dim
    out_cols = out_weight.shape[1]
    line = lax.axis_size("tensor")
    ring = lax.axis_size("serve")
    info = jnp.stack([lax.axis_index("tensor"), lax.axis_index("serve") % 2]).astype(jnp.int32)

    kv_two = lax.ppermute(image, "serve", [(i, (i + 2) % ring) for i in range(ring)])
    kv_mix = lax.ppermute(image, "serve", [(i, i + 1) if i % 2 == 0 else (i, (i + 3) % ring) for i in range(ring)])
    params = pltpu.CompilerParams(vmem_limit_bytes=40 * MIB)
    plan_size = 3 * count + 2 * NEED + 8

    def cost(micros):
        return pl.CostEstimate(flops=int(micros * 0.3e9), bytes_accessed=image.size, transcendentals=0)

    scratch = [pltpu.VMEM((dim, tokens), BF16), pltpu.VMEM((tokens, 2 * dim), BF16)]
    plan, head0 = pl.pallas_call(
        first_kernel,
        out_shape=(
            jax.ShapeDtypeStruct((plan_size,), jnp.int32),
            jax.ShapeDtypeStruct((half, col_count), BF16),
        ),
        in_specs=[SMEM, SMEM, SMEM, VMEM, VMEM],
        out_specs=(SMEM, VMEM),
        scratch_shapes=[pltpu.SMEM((2 * NEED,), jnp.int32)] + scratch,
        compiler_params=params,
        cost_estimate=cost(5),
        name="first_head",
    )(info, question_slot, question_len, queries, image)

    def resident(*arrays):
        return [pl.BlockSpec(a.shape, lambda n: (0, 0)) for a in arrays]

    def head(seg, key_value):
        return pl.pallas_call(
            functools.partial(head_kernel, seg),
            out_shape=jax.ShapeDtypeStruct((half, col_count), BF16),
            in_specs=[SMEM, VMEM, VMEM],
            out_specs=VMEM,
            scratch_shapes=scratch,
            compiler_params=params,
            cost_estimate=cost(3),
            name="head",
        )(plan, queries, key_value)

    def tails(rows, *key_values):
        return pl.pallas_call(
            tails_kernel,
            out_shape=jax.ShapeDtypeStruct((rows, col_count), BF16),
            grid=(NEED,),
            in_specs=[SMEM] + resident(queries, *key_values),
            out_specs=pl.BlockSpec((rows, col_count), lambda n: (0, 0)),
            scratch_shapes=[pltpu.VMEM((NEED * half, col_count), BF16)] + scratch,
            compiler_params=params,
            cost_estimate=cost(8),
            name="tails",
        )(plan, queries, *key_values)

    def paired(chunk):
        return chunk, lax.ppermute(chunk, "tensor", [(i, i ^ 1) for i in range(line)])

    def crossed(chunk):
        both = jnp.concatenate(chunk, axis=0)
        return *chunk, lax.ppermute(both, "tensor", [(1, 2), (2, 1)])

    def ended(chunk):
        return *chunk, lax.ppermute(chunk[2], "tensor", [(1, 0), (2, 3)])

    tile = 512
    steps = (out_cols // tile,)
    w_spec = pl.BlockSpec((out_weight.shape[0], tile), lambda n: (0, n))

    def tiled(rows):
        return pl.BlockSpec((rows, tile), lambda n: (0, n))

    def project(*chunks):
        arrays = [a for c in chunks for a in c]
        rows = sum(c[0].shape[0] for c in chunks)
        return pl.pallas_call(
            project_kernel,
            out_shape=jax.ShapeDtypeStruct((rows, out_cols), BF16),
            grid=steps,
            in_specs=[SMEM] + resident(*arrays) + [w_spec],
            out_specs=tiled(rows),
            compiler_params=params,
            cost_estimate=cost(10),
            name="project",
        )(info, *arrays, out_weight)

    def half_weight(far):
        def index(n, info_ref):
            upper = info_ref[0] // (line // 2)
            return 1 - upper if far else upper, n

        return pl.BlockSpec((out_weight.shape[0] // 2, tile), index)

    def with_info(in_specs, out_specs, scratch_shapes=()):
        return pltpu.PrefetchScalarGridSpec(
            num_scalar_prefetch=1, grid=steps, in_specs=in_specs, out_specs=out_specs, scratch_shapes=scratch_shapes)

    def fixed(*arrays):
        return [pl.BlockSpec(a.shape, lambda n, info_ref: (0, 0)) for a in arrays]

    def strip(rows):
        return pl.BlockSpec((rows, tile), lambda n, info_ref: (0, n))

    def place(segs, compact):
        return pl.pallas_call(
            functools.partial(place_kernel, segs),
            out_shape=jax.ShapeDtypeStruct((row_count, out_cols), BF16),
            grid=steps,
            in_specs=[SMEM, tiled(compact.shape[0])],
            out_specs=tiled(row_count),
            scratch_shapes=[pltpu.VMEM((row_count, compact.shape[0]), BF16)],
            compiler_params=params,
            cost_estimate=cost(5),
            name="place",
        )(plan, compact)

    def begin(segs, own3, other3, own, other):
        rows = own3.shape[0] + own.shape[0]
        width = len(segs) * half + own.shape[0]
        return pl.pallas_call(
            functools.partial(begin_kernel, segs),
            out_shape=(
                jax.ShapeDtypeStruct((rows, out_cols), F32),
                jax.ShapeDtypeStruct((row_count, width), BF16),
            ),
            grid_spec=with_info(
                [SMEM] + fixed(own3, other3, own, other) + [half_weight(False)],
                (strip(rows), pl.BlockSpec((row_count, width), lambda n, info_ref: (0, 0))),
            ),
            compiler_params=params,
            cost_estimate=cost(5),
            name="begin",
        )(info, plan, own3, other3, own, other, out_weight)

    def finish(middle3, ends3, middle, ends, pick, begun, done, placed):
        rows = begun.shape[0]
        return pl.pallas_call(
            finish_kernel,
            out_shape=jax.ShapeDtypeStruct((row_count, out_cols), BF16),
            grid_spec=with_info(
                fixed(middle3, ends3, middle, ends, pick)
                + [strip(rows), strip(done.shape[0]), strip(row_count), half_weight(True)],
                strip(row_count),
                [pltpu.VMEM((2, rows, col_count), BF16)],
            ),
            compiler_params=params,
            cost_estimate=cost(7),
            name="finish",
        )(info, middle3, ends3, middle, ends, pick, begun, done, placed, out_weight)

    def after(value, other):
        return lax.optimization_barrier((value, other))[0]

    chunk0 = paired(head0)
    kv_two, chunk0 = lax.optimization_barrier((kv_two, chunk0))
    kv_swap = lax.ppermute(kv_two, "serve", [(i, i ^ 1) for i in range(ring)])
    chunk0 = crossed(chunk0)
    chunk1 = paired(head(1, kv_two))
    kv_mix = after(kv_mix, chunk1[1])
    chunk0 = ended(chunk0)
    chunk1 = crossed(chunk1)
    chunk2 = paired(head(2, kv_mix))
    kv_swap = after(kv_swap, chunk2[1])
    chunk2 = crossed((chunk2[0], after(chunk2[1], chunk0[3])))
    chunk3 = crossed(paired(head(3, kv_swap)))
    chunk1 = ended(chunk1)
    chunk2 = ended(chunk2)
    rest = tails(NEED * half, image, kv_two, after(kv_mix, chunk3[1]), kv_swap)
    placed = place((0, 1), project(chunk0, chunk1))
    live_rest = plan[3 * count + 2 * NEED]
    sizes = [int(half * k) // 4 for k in (4, 5.5, 7, 9, 16)]

    def branch(size, rest, placed, chunk2, chunk3):
        own, other = paired(rest[:size])
        own3, other3, middle3, ends3 = ended(chunk3)
        own, other, middle = crossed((own, other))
        own, other, middle, ends = ended((own, other, after(middle, ends3)))
        begun, pick = begin((2, 3), own3, other3, own, other)
        done = project(chunk2)
        return finish(middle3, ends3, middle, ends, pick, begun, done, placed)

    index = sum([(live_rest > s).astype(jnp.int32) for s in sizes[:-1]])
    branches = [functools.partial(branch, s) for s in sizes]
    return lax.switch(index, branches, rest, placed, chunk2, chunk3)


def solution(mesh):
    plain = mesh.shape["tensor"] == KVH == 4 and mesh.shape["serve"] % 2 == 0 and NEED == 4
    return jax.shard_map(
        on_device_line if plain else on_device_general,
        mesh=mesh,
        in_specs=(
            P("serve", "tensor"),
            P("serve", "tensor", None),
            P("serve"),
            P("serve"),
            P(None, "tensor"),
        ),
        out_specs=P("serve", "tensor"),
        check_vma=False,
    )
```

```python
import functools

import jax
import jax.numpy as jnp
from jax import lax
from jax.experimental import pallas as pl
from jax.experimental.pallas import tpu as pltpu
from jax.sharding import PartitionSpec as P

KVH = 4
P_SIZE = 1600
QLEN = 32
NEED = 4
LOG2E = 1.4426950408889634
MIB = 1 << 20
F32 = jnp.float32
BF16 = jnp.bfloat16


def swapped(shard, axis, bit):
    return lax.ppermute(shard, axis, [(i, i ^ 1 << bit) for i in range(lax.axis_size(axis))])


def shifted(value, axis, steps):
    count = lax.axis_size(axis)
    pairs = [(source, (source + steps) % count) for source in range(count)]
    return lax.ppermute(value, axis, pairs)


def attend(query_rows, key_value):
    row_count = query_rows.shape[0]
    head_count = key_value.shape[0]
    head_dim = key_value.shape[2] // 2
    grouped = query_rows.reshape(row_count, head_count, -1, head_dim)
    key_part = key_value[:, :, :head_dim]
    value_part = key_value[:, :, head_dim:]
    scores = jnp.einsum(
        "rkgd,kpd->kgrp", grouped, key_part, preferred_element_type=jnp.float32
    ) * head_dim ** (-0.5)
    row_max = jnp.max(scores, axis=3, keepdims=True)
    exp_scores = jnp.exp(scores - row_max)
    sum_exp = jnp.sum(exp_scores, axis=3, keepdims=True)
    weights = (exp_scores / sum_exp).astype(jnp.bfloat16)
    blended = jnp.einsum("kgrp,kpd->rkgd", weights, value_part, preferred_element_type=jnp.float32)
    return blended.reshape(row_count, -1)


def on_device_general(queries, kv_cache, question_slot, question_len, out_weight):
    row_count, col_count = queries.shape
    head_dim = kv_cache.shape[2] // 2
    question_count = row_count // QLEN
    per_slot = question_count // NEED
    head_piece = kv_cache[0]
    sharing = lax.axis_size("tensor") // KVH
    if sharing > 1:
        for bit_number in range(sharing.bit_length() - 1):
            partner_piece = swapped(head_piece, "tensor", bit_number)
            upper_member = lax.axis_index("tensor") // 2**bit_number % 2 == 1
            head_piece = jnp.where(
                upper_member,
                jnp.concatenate([partner_piece, head_piece], axis=0),
                jnp.concatenate([head_piece, partner_piece], axis=0),
            )
    key_value = head_piece.reshape(-1, P_SIZE, 2 * head_dim)
    ordering = jnp.argsort(question_slot, stable=True)
    inverse_order = jnp.argsort(ordering, stable=True)
    sorted_rows = queries.reshape(question_count, QLEN, col_count)[ordering]
    sorted_rows = sorted_rows.reshape(NEED, per_slot * QLEN, col_count)
    results = []
    for offset_back in range(NEED):
        if offset_back == 0:
            remote = key_value
        else:
            remote = shifted(key_value, "serve", offset_back)
        results.append(attend(sorted_rows[offset_back], remote))
    sorted_out = jnp.stack(results).reshape(question_count, QLEN, col_count)
    blended = sorted_out[inverse_order].reshape(row_count, col_count)
    token_pos = jnp.arange(row_count, dtype=jnp.int32) % QLEN
    live_rows = token_pos < jnp.repeat(question_len, QLEN, total_repeat_length=row_count)
    attended = jnp.where(live_rows[:, None], blended, 0.0).astype(jnp.bfloat16)
    zero_sum = jnp.zeros((row_count, out_weight.shape[1]), jnp.float32)
    gathered_cols = lax.all_gather(attended, "tensor", axis=1, tiled=True)
    weight_rows = lax.slice_in_dim(out_weight, 0, gathered_cols.shape[1], axis=0)
    answers = zero_sum + jnp.dot(gathered_cols, weight_rows, preferred_element_type=jnp.float32)
    return answers.astype(jnp.bfloat16)


def make_plan(info_ref, slot_ref, len_ref, plan_ref, work_ref):
    count = slot_ref.shape[0]
    per = count // NEED
    half = per * QLEN // 2
    odd = info_ref[1]
    for g in range(NEED):
        work_ref[g] = g * per
        work_ref[NEED + g] = 0

    def step(q, carry):
        slot = slot_ref[q]
        length = len_ref[q]
        last = jnp.where(slot == 1, 3 - odd, 2 + odd)
        seg = jnp.where(slot == 0, 0, jnp.where(slot == 2, 1, last))
        at = work_ref[seg]
        first = work_ref[NEED + seg]
        plan_ref[at] = q
        plan_ref[count + at] = first
        plan_ref[2 * count + at] = length
        work_ref[seg] = at + 1
        work_ref[NEED + seg] = first + length
        return carry

    lax.fori_loop(0, count, step, 0)
    begin = jnp.int32(0)
    for g in range(NEED):
        live = work_ref[NEED + g]
        plan_ref[3 * count + g] = live
        plan_ref[3 * count + NEED + g] = begin
        begin = begin + jnp.maximum(live - half, 0)
    plan_ref[3 * count + 2 * NEED] = begin


def segment_rows(q_ref, plan_ref, seg, low, rows):
    count = q_ref.shape[0] // QLEN
    per = count // NEED
    width = per * QLEN
    lane = lax.broadcasted_iota(jnp.int32, (1, width), 1)
    owner = lane // QLEN
    inner = lane % QLEN
    first = jnp.zeros((1, width), jnp.int32)
    length = jnp.zeros((1, width), jnp.int32)
    blocks = []
    for k in range(per):
        q = plan_ref[seg * per + k]
        blocks.append(q_ref[pl.ds(pl.multiple_of(q * QLEN, QLEN), QLEN), :])
        first = jnp.where(owner == k, plan_ref[count + seg * per + k], first)
        length = jnp.where(owner == k, plan_ref[2 * count + seg * per + k], length)
    target = jnp.where(inner < length, first + inner, -1)
    row = lax.broadcasted_iota(jnp.int32, (rows, width), 0) + low
    pick = jnp.where(row == target, 1.0, 0.0).astype(BF16)
    return jnp.dot(pick, jnp.concatenate(blocks, axis=0), preferred_element_type=F32).astype(BF16)


def load_image(kv_ref, keys_ref, ones_ref):
    dim = kv_ref.shape[1] // 2
    keys_ref[...] = kv_ref[:, :dim].T
    ones_ref[:, :dim] = kv_ref[:, dim:]
    ones_ref[:, dim:] = jnp.ones((kv_ref.shape[0], dim), BF16)


def attend_rows(x, keys_ref, ones_ref, out_ref, base):
    dim = keys_ref.shape[0]
    rows, cols = x.shape
    heads = cols // dim
    group = max(1, min(heads, 256 // rows))
    for low in range(0, heads, group):
        members = range(low, min(low + group, heads))
        q = [x[:, h * dim:(h + 1) * dim] for h in members]
        q = q[0] if len(q) == 1 else jnp.concatenate(q, axis=0)
        s = jnp.dot(q, keys_ref[...], preferred_element_type=F32)
        top = jnp.max(s, axis=1, keepdims=True)
        e = jnp.exp2((s - top) * (LOG2E * dim ** (-0.5))).astype(BF16)
        o = jnp.dot(e, ones_ref[...], preferred_element_type=F32)
        o = (o[:, :dim] / o[:, dim:]).astype(BF16)
        for i, h in enumerate(members):
            out_ref[pl.ds(base, rows), h * dim:(h + 1) * dim] = o[i * rows:(i + 1) * rows, :]


def first_kernel(info_ref, slot_ref, len_ref, q_ref, kv_ref, plan_ref, out_ref, work_ref, keys_ref, ones_ref):
    make_plan(info_ref, slot_ref, len_ref, plan_ref, work_ref)
    load_image(kv_ref, keys_ref, ones_ref)
    attend_rows(segment_rows(q_ref, plan_ref, 0, 0, out_ref.shape[0]), keys_ref, ones_ref, out_ref, 0)


def head_kernel(seg, plan_ref, q_ref, kv_ref, out_ref, keys_ref, ones_ref):
    load_image(kv_ref, keys_ref, ones_ref)
    attend_rows(segment_rows(q_ref, plan_ref, seg, 0, out_ref.shape[0]), keys_ref, ones_ref, out_ref, 0)


def tails_kernel(plan_ref, q_ref, kv0_ref, kv1_ref, kv2_ref, kv3_ref, out_ref, tails_ref, keys_ref, ones_ref):
    count = q_ref.shape[0] // QLEN
    width = tails_ref.shape[0]
    half = width // NEED
    seg = pl.program_id(0)
    live = plan_ref[3 * count + seg] - half

    @pl.when(seg == 0)
    def _():
        tails_ref[...] = jnp.zeros(tails_ref.shape, tails_ref.dtype)

    for g, kv_ref in enumerate((kv0_ref, kv1_ref, kv2_ref, kv3_ref)):
        @pl.when((seg == g) & (live > 0))
        def _():
            load_image(kv_ref, keys_ref, ones_ref)

    for low, high in ((0, half // 4), (half // 4, half // 2), (half // 2, half)):
        @pl.when((live > low) & (live <= high))
        def _():
            x = segment_rows(q_ref, plan_ref, seg, half, high)
            attend_rows(x, keys_ref, ones_ref, tails_ref, pl.multiple_of(seg * half, half))

    @pl.when(seg == NEED - 1)
    def _():
        lane = lax.broadcasted_iota(jnp.int32, (1, width), 1)
        target = jnp.full((1, width), -1, jnp.int32)
        for g in range(NEED):
            inner = lane - g * half
            here = (inner >= 0) & (inner < plan_ref[3 * count + g] - half)
            target = jnp.where(here, plan_ref[3 * count + NEED + g] + inner, target)
        row = lax.broadcasted_iota(jnp.int32, (out_ref.shape[0], width), 0)
        pick = jnp.where(row == target, 1.0, 0.0).astype(BF16)
        out_ref[...] = jnp.dot(pick, tails_ref[...], preferred_element_type=F32).astype(BF16)


def columns(info_ref, line):
    me = info_ref[0]
    upper = me >= line // 2
    pair = jnp.where(upper, 5 - me, 1 - me)
    return me, pair, jnp.where(upper, 1, 2), jnp.where(upper, 0, 3)


def from_afar(info_ref, line, middle_ref, ends_ref, k):
    me = info_ref[0]
    rows = middle_ref.shape[0] // 2
    part = pl.ds(k * rows, rows)
    return jnp.where((me == 0) | (me == line - 1), ends_ref[part, :], middle_ref[part, :])


def project_kernel(info_ref, *refs):
    *chunks, w_ref, out_ref = refs
    depth = chunks[0].shape[1]
    line = w_ref.shape[0] // depth
    total = None
    for k, at in enumerate(columns(info_ref, line)):
        if k < 2:
            pieces = [c[...] for c in chunks[k::4]]
        else:
            pieces = [from_afar(info_ref, line, m, e, k - 2) for m, e in zip(chunks[2::4], chunks[3::4])]
        x = pieces[0] if len(pieces) == 1 else jnp.concatenate(pieces, axis=0)
        w = w_ref[pl.ds(pl.multiple_of(at * depth, depth), depth), :]
        y = jnp.dot(x, w, preferred_element_type=F32)
        total = y if total is None else total + y
    out_ref[...] = total.astype(out_ref.dtype)


def pick_rows(plan_ref, pick_ref, segs, tails):
    rows, width = pick_ref.shape
    count = rows // QLEN
    per = count // NEED
    half = per * QLEN // 2
    sub = lax.broadcasted_iota(jnp.int32, (QLEN, 1), 0)
    lane = lax.broadcasted_iota(jnp.int32, (QLEN, width), 1)
    for seg in range(NEED):
        def step(p, carry):
            at = plan_ref[count + p] + sub
            head = at + (seg - segs[0]) * half if seg in segs else jnp.full_like(at, -1)
            tail = at + (len(segs) - 1) * half + plan_ref[3 * count + NEED + seg] if tails else jnp.full_like(at, -1)
            at = jnp.where(at < half, head, tail)
            at = jnp.where(sub < plan_ref[2 * count + p], at, -1)
            block = pl.ds(pl.multiple_of(plan_ref[p] * QLEN, QLEN), QLEN)
            pick_ref[block, :] = jnp.where(lane == at, 1.0, 0.0).astype(BF16)
            return carry

        lax.fori_loop(seg * per, (seg + 1) * per, step, 0, unroll=4)


def place_kernel(segs, plan_ref, compact_ref, out_ref, pick_ref):
    @pl.when(pl.program_id(0) == 0)
    def _():
        pick_rows(plan_ref, pick_ref, segs, False)

    out_ref[...] = jnp.dot(pick_ref[...], compact_ref[...], preferred_element_type=F32).astype(out_ref.dtype)


def begin_kernel(segs, info_ref, plan_ref, own3_ref, other3_ref, own_ref, other_ref, w_ref, out_ref, pick_ref):
    @pl.when(pl.program_id(0) == 0)
    def _():
        pick_rows(plan_ref, pick_ref, segs, True)

    depth = own_ref.shape[1]
    upper = info_ref[0] % 2
    total = None
    for x_refs, at in (((own3_ref, own_ref), upper), ((other3_ref, other_ref), 1 - upper)):
        x = jnp.concatenate([r[...] for r in x_refs], axis=0)
        w = w_ref[pl.ds(pl.multiple_of(at * depth, depth), depth), :]
        y = jnp.dot(x, w, preferred_element_type=F32)
        total = y if total is None else total + y
    out_ref[...] = total


def finish_kernel(info_ref, middle3_ref, ends3_ref, middle_ref, ends_ref, pick_ref, begun_ref, placed_ref, w_ref,
                  out_ref, x_ref):
    depth = middle_ref.shape[1]
    line = 2 * (w_ref.shape[0] // depth)
    places = columns(info_ref, line)[2:]

    @pl.when(pl.program_id(0) == 0)
    def _():
        low = middle3_ref.shape[0] // 2
        for k in range(2):
            x_ref[k, :low, :] = from_afar(info_ref, line, middle3_ref, ends3_ref, k)
            x_ref[k, low:, :] = from_afar(info_ref, line, middle_ref, ends_ref, k)

    y = begun_ref[...]
    for k, at in enumerate(places):
        w = w_ref[pl.ds(pl.multiple_of(at % 2 * depth, depth), depth), :]
        y = y + jnp.dot(x_ref[k], w, preferred_element_type=F32)
    z = jnp.dot(pick_ref[...], y.astype(BF16), preferred_element_type=F32)
    out_ref[...] = (placed_ref[...].astype(F32) + z).astype(out_ref.dtype)


SMEM = pl.BlockSpec(memory_space=pltpu.SMEM)
VMEM = pl.BlockSpec(memory_space=pltpu.VMEM)


def on_device_line(queries, kv_cache, question_slot, question_len, out_weight):
    row_count, col_count = queries.shape
    count = row_count // QLEN
    seg_rows = row_count // NEED
    half = seg_rows // 2
    image = kv_cache[0]
    tokens, dim = image.shape[0], image.shape[1] // 2
    heads = col_count // dim
    out_cols = out_weight.shape[1]
    line = lax.axis_size("tensor")
    ring = lax.axis_size("serve")
    info = jnp.stack([lax.axis_index("tensor"), lax.axis_index("serve") % 2]).astype(jnp.int32)

    kv_two = lax.ppermute(image, "serve", [(i, (i + 2) % ring) for i in range(ring)])
    kv_mix = lax.ppermute(image, "serve", [(i, i + 1) if i % 2 == 0 else (i, (i + 3) % ring) for i in range(ring)])
    params = pltpu.CompilerParams(vmem_limit_bytes=40 * MIB)
    plan_size = 3 * count + 2 * NEED + 8

    def cost(micros):
        return pl.CostEstimate(flops=int(micros * 0.3e9), bytes_accessed=image.size, transcendentals=0)

    scratch = [pltpu.VMEM((dim, tokens), BF16), pltpu.VMEM((tokens, 2 * dim), BF16)]
    plan, head0 = pl.pallas_call(
        first_kernel,
        out_shape=(
            jax.ShapeDtypeStruct((plan_size,), jnp.int32),
            jax.ShapeDtypeStruct((half, col_count), BF16),
        ),
        in_specs=[SMEM, SMEM, SMEM, VMEM, VMEM],
        out_specs=(SMEM, VMEM),
        scratch_shapes=[pltpu.SMEM((2 * NEED,), jnp.int32)] + scratch,
        compiler_params=params,
        cost_estimate=cost(5),
        name="first_head",
    )(info, question_slot, question_len, queries, image)

    def resident(*arrays):
        return [pl.BlockSpec(a.shape, lambda n: (0, 0)) for a in arrays]

    def head(seg, key_value):
        return pl.pallas_call(
            functools.partial(head_kernel, seg),
            out_shape=jax.ShapeDtypeStruct((half, col_count), BF16),
            in_specs=[SMEM, VMEM, VMEM],
            out_specs=VMEM,
            scratch_shapes=scratch,
            compiler_params=params,
            cost_estimate=cost(3),
            name="head",
        )(plan, queries, key_value)

    def tails(rows, *key_values):
        return pl.pallas_call(
            tails_kernel,
            out_shape=jax.ShapeDtypeStruct((rows, col_count), BF16),
            grid=(NEED,),
            in_specs=[SMEM] + resident(queries, *key_values),
            out_specs=pl.BlockSpec((rows, col_count), lambda n: (0, 0)),
            scratch_shapes=[pltpu.VMEM((NEED * half, col_count), BF16)] + scratch,
            compiler_params=params,
            cost_estimate=cost(8),
            name="tails",
        )(plan, queries, *key_values)

    def paired(chunk):
        return chunk, lax.ppermute(chunk, "tensor", [(i, i ^ 1) for i in range(line)])

    def crossed(chunk):
        both = jnp.concatenate(chunk, axis=0)
        return *chunk, lax.ppermute(both, "tensor", [(1, 2), (2, 1)])

    def ended(chunk):
        return *chunk, lax.ppermute(chunk[2], "tensor", [(1, 0), (2, 3)])

    tile = min(256, out_cols)
    wide = min(512, out_cols)
    steps = (out_cols // tile,)
    w_spec = pl.BlockSpec((out_weight.shape[0], tile), lambda n: (0, n))

    def tiled(rows):
        return pl.BlockSpec((rows, tile), lambda n: (0, n))

    def project(*chunks):
        arrays = [a for c in chunks for a in c]
        rows = sum(c[0].shape[0] for c in chunks)
        return pl.pallas_call(
            project_kernel,
            out_shape=jax.ShapeDtypeStruct((rows, out_cols), BF16),
            grid=steps,
            in_specs=[SMEM] + resident(*arrays) + [w_spec],
            out_specs=tiled(rows),
            compiler_params=params,
            cost_estimate=cost(10),
            name="project",
        )(info, *arrays, out_weight)

    def half_weight(far, tile):
        def index(n, info_ref):
            upper = info_ref[0] // (line // 2)
            return 1 - upper if far else upper, n

        return pl.BlockSpec((out_weight.shape[0] // 2, tile), index)

    def with_info(tile, in_specs, out_specs, scratch_shapes=()):
        return pltpu.PrefetchScalarGridSpec(
            num_scalar_prefetch=1, grid=(out_cols // tile,), in_specs=in_specs, out_specs=out_specs, scratch_shapes=scratch_shapes)

    def fixed(*arrays):
        return [pl.BlockSpec(a.shape, lambda n, info_ref: (0, 0)) for a in arrays]

    def strip(rows, tile):
        return pl.BlockSpec((rows, tile), lambda n, info_ref: (0, n))

    def place(segs, compact):
        return pl.pallas_call(
            functools.partial(place_kernel, segs),
            out_shape=jax.ShapeDtypeStruct((row_count, out_cols), BF16),
            grid=steps,
            in_specs=[SMEM, tiled(compact.shape[0])],
            out_specs=tiled(row_count),
            scratch_shapes=[pltpu.VMEM((row_count, compact.shape[0]), BF16)],
            compiler_params=params,
            cost_estimate=cost(5),
            name="place",
        )(plan, compact)

    def begin(segs, own3, other3, own, other):
        rows = own3.shape[0] + own.shape[0]
        width = len(segs) * half + own.shape[0]
        return pl.pallas_call(
            functools.partial(begin_kernel, segs),
            out_shape=(
                jax.ShapeDtypeStruct((rows, out_cols), F32),
                jax.ShapeDtypeStruct((row_count, width), BF16),
            ),
            grid_spec=with_info(
                tile,
                [SMEM] + fixed(own3, other3, own, other) + [half_weight(False, tile)],
                (strip(rows, tile), pl.BlockSpec((row_count, width), lambda n, info_ref: (0, 0))),
            ),
            compiler_params=params,
            cost_estimate=cost(5),
            name="begin",
        )(info, plan, own3, other3, own, other, out_weight)

    def finish(middle3, ends3, middle, ends, pick, begun, placed):
        rows = begun.shape[0]
        return pl.pallas_call(
            finish_kernel,
            out_shape=jax.ShapeDtypeStruct((row_count, out_cols), BF16),
            grid_spec=with_info(
                wide,
                fixed(middle3, ends3, middle, ends, pick)
                + [strip(rows, wide), strip(row_count, wide), half_weight(True, wide)],
                strip(row_count, wide),
                [pltpu.VMEM((2, rows, col_count), BF16)],
            ),
            compiler_params=params,
            cost_estimate=cost(7),
            name="finish",
        )(info, middle3, ends3, middle, ends, pick, begun, placed, out_weight)

    def after(value, other):
        return lax.optimization_barrier((value, other))[0]

    chunk0 = paired(head0)
    kv_two, chunk0 = lax.optimization_barrier((kv_two, chunk0))
    kv_swap = lax.ppermute(kv_two, "serve", [(i, i ^ 1) for i in range(ring)])
    chunk0 = crossed(chunk0)
    chunk1 = paired(head(1, kv_two))
    kv_mix = after(kv_mix, chunk1[1])
    chunk0 = ended(chunk0)
    chunk1 = crossed(chunk1)
    chunk2 = paired(head(2, kv_mix))
    head3 = head(3, kv_swap)
    chunk1 = ended((*chunk1[:2], after(chunk1[2], head3)))
    chunk2 = crossed((chunk2[0], after(chunk2[1], (chunk0[3], head3))))
    chunk3 = crossed(paired(head3))
    rest = tails(NEED * half, image, kv_two, after(kv_mix, chunk3[1]), kv_swap)
    early = half * 3 // 2
    rest_pair = paired(rest[:early])
    chunk2 = ended(chunk2)
    live_rest = plan[3 * count + 2 * NEED]
    sizes = [int(half * k) // 4 for k in (4, 5, 6, 7.5, 10, 16)]

    def branch(size, rest, rest_pair, chunk0, chunk1, chunk2, chunk3):
        own, other = rest_pair
        if size > early:
            own, other = [
                jnp.concatenate(pieces, axis=0) for pieces in zip(rest_pair, paired(rest[early:size]))]
        own, other, middle = crossed((own[:size], other[:size]))
        own3, other3, middle3, ends3 = ended(chunk3)
        done = project(chunk0, chunk1, chunk2)
        middle = after(middle, (ends3, done))
        own, other, middle, ends = ended((own, other, middle))
        begun, pick = begin((3,), own3, other3, own, other)
        return finish(middle3, ends3, middle, ends, pick, begun, place((0, 1, 2), done))

    index = sum([(live_rest > s).astype(jnp.int32) for s in sizes[:-1]])
    branches = [functools.partial(branch, s) for s in sizes]
    return lax.switch(index, branches, rest, rest_pair, chunk0, chunk1, chunk2, chunk3)


def solution(mesh):
    plain = mesh.shape["tensor"] == KVH == 4 and mesh.shape["serve"] % 2 == 0 and NEED == 4
    return jax.shard_map(
        on_device_line if plain else on_device_general,
        mesh=mesh,
        in_specs=(
            P("serve", "tensor"),
            P("serve", "tensor", None),
            P("serve"),
            P("serve"),
            P(None, "tensor"),
        ),
        out_specs=P("serve", "tensor"),
        check_vma=False,
    )
```

```python
import functools

import jax
import jax.numpy as jnp
from jax import lax
from jax.experimental import pallas as pl
from jax.experimental.pallas import tpu as pltpu
from jax.sharding import PartitionSpec as P

KVH = 4
P_SIZE = 1600
QLEN = 32
NEED = 4
LOG2E = 1.4426950408889634
MIB = 1 << 20
F32 = jnp.float32
BF16 = jnp.bfloat16


def swapped(shard, axis, bit):
    return lax.ppermute(shard, axis, [(i, i ^ 1 << bit) for i in range(lax.axis_size(axis))])


def shifted(value, axis, steps):
    count = lax.axis_size(axis)
    pairs = [(source, (source + steps) % count) for source in range(count)]
    return lax.ppermute(value, axis, pairs)


def attend(query_rows, key_value):
    row_count = query_rows.shape[0]
    head_count = key_value.shape[0]
    head_dim = key_value.shape[2] // 2
    grouped = query_rows.reshape(row_count, head_count, -1, head_dim)
    key_part = key_value[:, :, :head_dim]
    value_part = key_value[:, :, head_dim:]
    scores = jnp.einsum(
        "rkgd,kpd->kgrp", grouped, key_part, preferred_element_type=jnp.float32
    ) * head_dim ** (-0.5)
    row_max = jnp.max(scores, axis=3, keepdims=True)
    exp_scores = jnp.exp(scores - row_max)
    sum_exp = jnp.sum(exp_scores, axis=3, keepdims=True)
    weights = (exp_scores / sum_exp).astype(jnp.bfloat16)
    blended = jnp.einsum("kgrp,kpd->rkgd", weights, value_part, preferred_element_type=jnp.float32)
    return blended.reshape(row_count, -1)


def on_device_general(queries, kv_cache, question_slot, question_len, out_weight):
    row_count, col_count = queries.shape
    head_dim = kv_cache.shape[2] // 2
    question_count = row_count // QLEN
    per_slot = question_count // NEED
    head_piece = kv_cache[0]
    sharing = lax.axis_size("tensor") // KVH
    if sharing > 1:
        for bit_number in range(sharing.bit_length() - 1):
            partner_piece = swapped(head_piece, "tensor", bit_number)
            upper_member = lax.axis_index("tensor") // 2**bit_number % 2 == 1
            head_piece = jnp.where(
                upper_member,
                jnp.concatenate([partner_piece, head_piece], axis=0),
                jnp.concatenate([head_piece, partner_piece], axis=0),
            )
    key_value = head_piece.reshape(-1, P_SIZE, 2 * head_dim)
    ordering = jnp.argsort(question_slot, stable=True)
    inverse_order = jnp.argsort(ordering, stable=True)
    sorted_rows = queries.reshape(question_count, QLEN, col_count)[ordering]
    sorted_rows = sorted_rows.reshape(NEED, per_slot * QLEN, col_count)
    results = []
    for offset_back in range(NEED):
        if offset_back == 0:
            remote = key_value
        else:
            remote = shifted(key_value, "serve", offset_back)
        results.append(attend(sorted_rows[offset_back], remote))
    sorted_out = jnp.stack(results).reshape(question_count, QLEN, col_count)
    blended = sorted_out[inverse_order].reshape(row_count, col_count)
    token_pos = jnp.arange(row_count, dtype=jnp.int32) % QLEN
    live_rows = token_pos < jnp.repeat(question_len, QLEN, total_repeat_length=row_count)
    attended = jnp.where(live_rows[:, None], blended, 0.0).astype(jnp.bfloat16)
    zero_sum = jnp.zeros((row_count, out_weight.shape[1]), jnp.float32)
    gathered_cols = lax.all_gather(attended, "tensor", axis=1, tiled=True)
    weight_rows = lax.slice_in_dim(out_weight, 0, gathered_cols.shape[1], axis=0)
    answers = zero_sum + jnp.dot(gathered_cols, weight_rows, preferred_element_type=jnp.float32)
    return answers.astype(jnp.bfloat16)


def make_plan(info_ref, slot_ref, len_ref, plan_ref, work_ref):
    count = slot_ref.shape[0]
    per = count // NEED
    half = per * QLEN // 2
    odd = info_ref[1]
    for g in range(NEED):
        work_ref[g] = g * per
        work_ref[NEED + g] = 0

    def step(q, carry):
        slot = slot_ref[q]
        length = len_ref[q]
        last = jnp.where(slot == 1, 3 - odd, 2 + odd)
        seg = jnp.where(slot == 0, 0, jnp.where(slot == 2, 1, last))
        at = work_ref[seg]
        first = work_ref[NEED + seg]
        plan_ref[at] = q
        plan_ref[count + at] = first
        plan_ref[2 * count + at] = length
        work_ref[seg] = at + 1
        work_ref[NEED + seg] = first + length
        return carry

    lax.fori_loop(0, count, step, 0)
    begin = jnp.int32(0)
    for g in range(NEED):
        live = work_ref[NEED + g]
        plan_ref[3 * count + g] = live
        plan_ref[3 * count + NEED + g] = begin
        begin = begin + jnp.maximum(live - half, 0)
    plan_ref[3 * count + 2 * NEED] = begin


def segment_rows(q_ref, plan_ref, seg, low, rows):
    count = q_ref.shape[0] // QLEN
    per = count // NEED
    width = per * QLEN
    lane = lax.broadcasted_iota(jnp.int32, (1, width), 1)
    owner = lane // QLEN
    inner = lane % QLEN
    first = jnp.zeros((1, width), jnp.int32)
    length = jnp.zeros((1, width), jnp.int32)
    blocks = []
    for k in range(per):
        q = plan_ref[seg * per + k]
        blocks.append(q_ref[pl.ds(pl.multiple_of(q * QLEN, QLEN), QLEN), :])
        first = jnp.where(owner == k, plan_ref[count + seg * per + k], first)
        length = jnp.where(owner == k, plan_ref[2 * count + seg * per + k], length)
    target = jnp.where(inner < length, first + inner, -1)
    row = lax.broadcasted_iota(jnp.int32, (rows, width), 0) + low
    pick = jnp.where(row == target, 1.0, 0.0).astype(BF16)
    return jnp.dot(pick, jnp.concatenate(blocks, axis=0), preferred_element_type=F32).astype(BF16)


def load_image(kv_ref, keys_ref, ones_ref):
    dim = kv_ref.shape[1] // 2
    keys_ref[...] = kv_ref[:, :dim].T
    ones_ref[:, :dim] = kv_ref[:, dim:]
    ones_ref[:, dim:] = jnp.ones((kv_ref.shape[0], dim), BF16)


def attend_rows(x, keys_ref, ones_ref, out_ref, base):
    dim = keys_ref.shape[0]
    rows, cols = x.shape
    heads = cols // dim
    group = max(1, min(heads, 256 // rows))
    for low in range(0, heads, group):
        members = range(low, min(low + group, heads))
        q = [x[:, h * dim:(h + 1) * dim] for h in members]
        q = q[0] if len(q) == 1 else jnp.concatenate(q, axis=0)
        s = jnp.dot(q, keys_ref[...], preferred_element_type=F32)
        top = jnp.max(s, axis=1, keepdims=True)
        e = jnp.exp2((s - top) * (LOG2E * dim ** (-0.5))).astype(BF16)
        o = jnp.dot(e, ones_ref[...], preferred_element_type=F32)
        o = (o[:, :dim] / o[:, dim:]).astype(BF16)
        for i, h in enumerate(members):
            out_ref[pl.ds(base, rows), h * dim:(h + 1) * dim] = o[i * rows:(i + 1) * rows, :]


def first_kernel(info_ref, slot_ref, len_ref, q_ref, kv_ref, plan_ref, up_ref, low_ref, work_ref, keys_ref, ones_ref,
                 both_ref):
    make_plan(info_ref, slot_ref, len_ref, plan_ref, work_ref)
    load_image(kv_ref, keys_ref, ones_ref)
    rows = up_ref.shape[0]
    attend_rows(segment_rows(q_ref, plan_ref, 0, 0, 2 * rows), keys_ref, ones_ref, both_ref, 0)
    up_ref[...] = both_ref[:rows, :]
    low_ref[...] = both_ref[rows:, :]


def head_kernel(seg, plan_ref, q_ref, kv_ref, out_ref, keys_ref, ones_ref):
    load_image(kv_ref, keys_ref, ones_ref)
    attend_rows(segment_rows(q_ref, plan_ref, seg, 0, out_ref.shape[0]), keys_ref, ones_ref, out_ref, 0)


def tails_kernel(plan_ref, q_ref, kv0_ref, kv1_ref, kv2_ref, kv3_ref, out_ref, tails_ref, keys_ref, ones_ref):
    count = q_ref.shape[0] // QLEN
    width = tails_ref.shape[0]
    half = width // NEED
    seg = pl.program_id(0)
    live = plan_ref[3 * count + seg] - half

    @pl.when(seg == 0)
    def _():
        tails_ref[...] = jnp.zeros(tails_ref.shape, tails_ref.dtype)

    for g, kv_ref in enumerate((kv0_ref, kv1_ref, kv2_ref, kv3_ref)):
        @pl.when((seg == g) & (live > 0))
        def _():
            load_image(kv_ref, keys_ref, ones_ref)

    for low, high in ((0, half // 4), (half // 4, half // 2), (half // 2, half)):
        @pl.when((live > low) & (live <= high))
        def _():
            x = segment_rows(q_ref, plan_ref, seg, half, high)
            attend_rows(x, keys_ref, ones_ref, tails_ref, pl.multiple_of(seg * half, half))

    @pl.when(seg == NEED - 1)
    def _():
        lane = lax.broadcasted_iota(jnp.int32, (1, width), 1)
        target = jnp.full((1, width), -1, jnp.int32)
        for g in range(NEED):
            inner = lane - g * half
            here = (inner >= 0) & (inner < plan_ref[3 * count + g] - half)
            target = jnp.where(here, plan_ref[3 * count + NEED + g] + inner, target)
        row = lax.broadcasted_iota(jnp.int32, (out_ref.shape[0], width), 0)
        pick = jnp.where(row == target, 1.0, 0.0).astype(BF16)
        out_ref[...] = jnp.dot(pick, tails_ref[...], preferred_element_type=F32).astype(BF16)


def columns(info_ref, line):
    me = info_ref[0]
    upper = me >= line // 2
    pair = jnp.where(upper, 5 - me, 1 - me)
    return me, pair, jnp.where(upper, 1, 2), jnp.where(upper, 0, 3)


def from_afar(info_ref, line, middle_ref, ends_ref, k):
    me = info_ref[0]
    rows = middle_ref.shape[0] // 2
    part = pl.ds(k * rows, rows)
    return jnp.where((me == 0) | (me == line - 1), ends_ref[part, :], middle_ref[part, :])


def project_kernel(info_ref, *refs):
    *chunks, w_ref, out_ref = refs
    depth = chunks[0].shape[1]
    line = w_ref.shape[0] // depth
    total = None
    for k, at in enumerate(columns(info_ref, line)):
        if k < 2:
            pieces = [c[...] for c in chunks[k::4]]
        else:
            pieces = [from_afar(info_ref, line, m, e, k - 2) for m, e in zip(chunks[2::4], chunks[3::4])]
        x = pieces[0] if len(pieces) == 1 else jnp.concatenate(pieces, axis=0)
        w = w_ref[pl.ds(pl.multiple_of(at * depth, depth), depth), :]
        y = jnp.dot(x, w, preferred_element_type=F32)
        total = y if total is None else total + y
    out_ref[...] = total.astype(out_ref.dtype)


def pick_rows(plan_ref, pick_ref, segs, tails):
    rows, width = pick_ref.shape
    count = rows // QLEN
    per = count // NEED
    half = per * QLEN // 2
    sub = lax.broadcasted_iota(jnp.int32, (QLEN, 1), 0)
    lane = lax.broadcasted_iota(jnp.int32, (QLEN, width), 1)
    for seg in range(NEED):
        def step(p, carry):
            at = plan_ref[count + p] + sub
            head = at + (seg - segs[0]) * half if seg in segs else jnp.full_like(at, -1)
            tail = at + len(segs) * half - half + plan_ref[3 * count + NEED + seg] if tails else jnp.full_like(at, -1)
            at = jnp.where(at < half, head, tail)
            at = jnp.where(sub < plan_ref[2 * count + p], at, -1)
            block = pl.ds(pl.multiple_of(plan_ref[p] * QLEN, QLEN), QLEN)
            pick_ref[block, :] = jnp.where(lane == at, 1.0, 0.0).astype(BF16)
            return carry

        lax.fori_loop(seg * per, (seg + 1) * per, step, 0, unroll=4)


def place_kernel(segs, plan_ref, *refs):
    *compact, out_ref, pick_ref = refs

    @pl.when(pl.program_id(0) == 0)
    def _():
        pick_rows(plan_ref, pick_ref, segs, False)

    y = jnp.concatenate([c[...] for c in compact], axis=0)
    out_ref[...] = jnp.dot(pick_ref[...], y, preferred_element_type=F32).astype(out_ref.dtype)


def begin_kernel(info_ref, plan_ref, own_ref, other_ref, w_ref, out_ref, pick_ref):
    @pl.when(pl.program_id(0) == 0)
    def _():
        pick_rows(plan_ref, pick_ref, (), True)

    depth = own_ref.shape[1]
    upper = info_ref[0] % 2
    total = None
    for x_ref, at in ((own_ref, upper), (other_ref, 1 - upper)):
        w = w_ref[pl.ds(pl.multiple_of(at * depth, depth), depth), :]
        y = jnp.dot(x_ref[...], w, preferred_element_type=F32)
        total = y if total is None else total + y
    out_ref[...] = total


def finish_kernel(info_ref, middle_ref, ends_ref, pick_ref, begun_ref, placed_ref, w_ref, out_ref, x_ref):
    depth = middle_ref.shape[1]
    line = 2 * (w_ref.shape[0] // depth)
    places = columns(info_ref, line)[2:]

    @pl.when(pl.program_id(0) == 0)
    def _():
        for k in range(2):
            x_ref[k] = from_afar(info_ref, line, middle_ref, ends_ref, k)

    y = begun_ref[...]
    for k, at in enumerate(places):
        w = w_ref[pl.ds(pl.multiple_of(at % 2 * depth, depth), depth), :]
        y = y + jnp.dot(x_ref[k], w, preferred_element_type=F32)
    z = jnp.dot(pick_ref[...], y.astype(BF16), preferred_element_type=F32)
    out_ref[...] = (placed_ref[...].astype(F32) + z).astype(out_ref.dtype)


SMEM = pl.BlockSpec(memory_space=pltpu.SMEM)
VMEM = pl.BlockSpec(memory_space=pltpu.VMEM)


def on_device_line(queries, kv_cache, question_slot, question_len, out_weight):
    row_count, col_count = queries.shape
    count = row_count // QLEN
    seg_rows = row_count // NEED
    half = seg_rows // 2
    image = kv_cache[0]
    tokens, dim = image.shape[0], image.shape[1] // 2
    heads = col_count // dim
    out_cols = out_weight.shape[1]
    line = lax.axis_size("tensor")
    ring = lax.axis_size("serve")
    info = jnp.stack([lax.axis_index("tensor"), lax.axis_index("serve") % 2]).astype(jnp.int32)

    kv_two = lax.ppermute(image, "serve", [(i, (i + 2) % ring) for i in range(ring)])
    kv_mix = lax.ppermute(image, "serve", [(i, i + 1) if i % 2 == 0 else (i, (i + 3) % ring) for i in range(ring)])
    params = pltpu.CompilerParams(vmem_limit_bytes=40 * MIB)
    plan_size = 3 * count + 2 * NEED + 8

    def cost(micros):
        return pl.CostEstimate(flops=int(micros * 0.3e9), bytes_accessed=image.size, transcendentals=0)

    scratch = [pltpu.VMEM((dim, tokens), BF16), pltpu.VMEM((tokens, 2 * dim), BF16)]
    plan, head_up, head_low = pl.pallas_call(
        first_kernel,
        out_shape=(
            jax.ShapeDtypeStruct((plan_size,), jnp.int32),
            jax.ShapeDtypeStruct((half // 2, col_count), BF16),
            jax.ShapeDtypeStruct((half // 2, col_count), BF16),
        ),
        in_specs=[SMEM, SMEM, SMEM, VMEM, VMEM],
        out_specs=(SMEM, VMEM, VMEM),
        scratch_shapes=[pltpu.SMEM((2 * NEED,), jnp.int32)] + scratch + [pltpu.VMEM((half, col_count), BF16)],
        compiler_params=params,
        cost_estimate=cost(5),
        name="first_head",
    )(info, question_slot, question_len, queries, image)

    def resident(*arrays):
        return [pl.BlockSpec(a.shape, lambda n: (0, 0)) for a in arrays]

    def head(seg, key_value):
        return pl.pallas_call(
            functools.partial(head_kernel, seg),
            out_shape=jax.ShapeDtypeStruct((half, col_count), BF16),
            in_specs=[SMEM, VMEM, VMEM],
            out_specs=VMEM,
            scratch_shapes=scratch,
            compiler_params=params,
            cost_estimate=cost(3),
            name="head",
        )(plan, queries, key_value)

    def tails(rows, *key_values):
        return pl.pallas_call(
            tails_kernel,
            out_shape=jax.ShapeDtypeStruct((rows, col_count), BF16),
            grid=(NEED,),
            in_specs=[SMEM] + resident(queries, *key_values),
            out_specs=pl.BlockSpec((rows, col_count), lambda n: (0, 0)),
            scratch_shapes=[pltpu.VMEM((NEED * half, col_count), BF16)] + scratch,
            compiler_params=params,
            cost_estimate=cost(8),
            name="tails",
        )(plan, queries, *key_values)

    def paired(chunk):
        return chunk, lax.ppermute(chunk, "tensor", [(i, i ^ 1) for i in range(line)])

    def crossed(chunk):
        both = jnp.concatenate(chunk, axis=0)
        return *chunk, lax.ppermute(both, "tensor", [(1, 2), (2, 1)])

    def ended(chunk):
        return *chunk, lax.ppermute(chunk[2], "tensor", [(1, 0), (2, 3)])

    tile = min(256, out_cols)
    wide = min(512, out_cols)
    steps = (out_cols // tile,)
    w_spec = pl.BlockSpec((out_weight.shape[0], tile), lambda n: (0, n))

    def tiled(rows):
        return pl.BlockSpec((rows, tile), lambda n: (0, n))

    def project(*chunks):
        arrays = [a for c in chunks for a in c]
        rows = sum(c[0].shape[0] for c in chunks)
        return pl.pallas_call(
            project_kernel,
            out_shape=jax.ShapeDtypeStruct((rows, out_cols), BF16),
            grid=steps,
            in_specs=[SMEM] + resident(*arrays) + [w_spec],
            out_specs=tiled(rows),
            compiler_params=params,
            cost_estimate=cost(10),
            name="project",
        )(info, *arrays, out_weight)

    def half_weight(far, tile):
        def index(n, info_ref):
            upper = info_ref[0] // (line // 2)
            return 1 - upper if far else upper, n

        return pl.BlockSpec((out_weight.shape[0] // 2, tile), index)

    def with_info(tile, in_specs, out_specs, scratch_shapes=()):
        return pltpu.PrefetchScalarGridSpec(
            num_scalar_prefetch=1, grid=(out_cols // tile,), in_specs=in_specs, out_specs=out_specs, scratch_shapes=scratch_shapes)

    def fixed(*arrays):
        return [pl.BlockSpec(a.shape, lambda n, info_ref: (0, 0)) for a in arrays]

    def strip(rows, tile):
        return pl.BlockSpec((rows, tile), lambda n, info_ref: (0, n))

    def place(segs, *compact):
        return pl.pallas_call(
            functools.partial(place_kernel, segs),
            out_shape=jax.ShapeDtypeStruct((row_count, out_cols), BF16),
            grid=steps,
            in_specs=[SMEM] + [tiled(c.shape[0]) for c in compact],
            out_specs=tiled(row_count),
            scratch_shapes=[pltpu.VMEM((row_count, sum(c.shape[0] for c in compact)), BF16)],
            compiler_params=params,
            cost_estimate=cost(5),
            name="place",
        )(plan, *compact)

    def begin(own, other):
        rows = own.shape[0]
        return pl.pallas_call(
            begin_kernel,
            out_shape=(
                jax.ShapeDtypeStruct((rows, out_cols), F32),
                jax.ShapeDtypeStruct((row_count, rows), BF16),
            ),
            grid_spec=with_info(
                tile,
                [SMEM] + fixed(own, other) + [half_weight(False, tile)],
                (strip(rows, tile), pl.BlockSpec((row_count, rows), lambda n, info_ref: (0, 0))),
            ),
            compiler_params=params,
            cost_estimate=cost(5),
            name="begin",
        )(info, plan, own, other, out_weight)

    def finish(middle, ends, pick, begun, placed):
        rows = begun.shape[0]
        return pl.pallas_call(
            finish_kernel,
            out_shape=jax.ShapeDtypeStruct((row_count, out_cols), BF16),
            grid_spec=with_info(
                wide,
                fixed(middle, ends, pick)
                + [strip(rows, wide), strip(row_count, wide), half_weight(True, wide)],
                strip(row_count, wide),
                [pltpu.VMEM((2, rows, col_count), BF16)],
            ),
            compiler_params=params,
            cost_estimate=cost(7),
            name="finish",
        )(info, middle, ends, pick, begun, placed, out_weight)

    def after(value, other):
        return lax.optimization_barrier((value, other))[0]

    up, low = crossed(paired(head_up)), paired(head_low)
    kv_two, low, _ = lax.optimization_barrier((kv_two, low, up[2]))
    kv_swap = lax.ppermute(kv_two, "serve", [(i, i ^ 1) for i in range(ring)])
    low = crossed(low)
    up = ended(up)
    chunk1 = paired(head(1, kv_two))
    kv_mix = after(kv_mix, (chunk1[1], low[2]))
    low = ended(low)
    chunk1 = crossed((chunk1[0], after(chunk1[1], up[3])))
    chunk2 = paired(head(2, kv_mix))
    head3 = head(3, kv_swap)
    chunk1 = ended((*chunk1[:2], after(chunk1[2], head3)))
    chunk2 = crossed((chunk2[0], after(chunk2[1], (low[3], head3))))
    chunk3 = crossed(paired(head3))
    rest = tails(NEED * half, image, kv_two, after(kv_mix, chunk3[1]), kv_swap)
    early = half * 3 // 2
    rest_pair = paired(rest[:early])
    chunk2 = ended((*chunk2[:2], after(chunk2[2], rest)))
    live_rest = plan[3 * count + 2 * NEED]
    sizes = [int(half * k) // 4 for k in (16, 10, 7.5, 6, 5, 4)]

    def branch(size, rest, rest_pair, up, low, chunk1, chunk2, chunk3):
        own, other = rest_pair
        if size > early:
            own, other = [
                jnp.concatenate(pieces, axis=0) for pieces in zip(rest_pair, paired(rest[early:size]))]
        own, other, middle = crossed((own[:size], other[:size]))
        chunk3 = ended(chunk3)
        done = project(up, low, chunk1, chunk2)
        middle = after(middle, (chunk3[3], done))
        own, other, middle, ends = ended((own, other, middle))
        begun, pick = begin(own, other)
        return finish(middle, ends, pick, begun, place((0, 1, 2, 3), done, project(chunk3)))

    index = sum([(live_rest <= s).astype(jnp.int32) for s in sizes[1:]])
    branches = [functools.partial(branch, s) for s in sizes]
    return lax.switch(index, branches, rest, rest_pair, up, low, chunk1, chunk2, chunk3)


def solution(mesh):
    plain = mesh.shape["tensor"] == KVH == 4 and mesh.shape["serve"] % 2 == 0 and NEED == 4
    return jax.shard_map(
        on_device_line if plain else on_device_general,
        mesh=mesh,
        in_specs=(
            P("serve", "tensor"),
            P("serve", "tensor", None),
            P("serve"),
            P("serve"),
            P(None, "tensor"),
        ),
        out_specs=P("serve", "tensor"),
        check_vma=False,
    )
```

```python
import functools

import jax
import jax.numpy as jnp
from jax import lax
from jax.experimental import pallas as pl
from jax.experimental.pallas import tpu as pltpu
from jax.sharding import PartitionSpec as P

KVH = 4
P_SIZE = 1600
QLEN = 32
NEED = 4
LOG2E = 1.4426950408889634
MIB = 1 << 20
F32 = jnp.float32
BF16 = jnp.bfloat16


def swapped(shard, axis, bit):
    return lax.ppermute(shard, axis, [(i, i ^ 1 << bit) for i in range(lax.axis_size(axis))])


def shifted(value, axis, steps):
    count = lax.axis_size(axis)
    pairs = [(source, (source + steps) % count) for source in range(count)]
    return lax.ppermute(value, axis, pairs)


def attend(query_rows, key_value):
    row_count = query_rows.shape[0]
    head_count = key_value.shape[0]
    head_dim = key_value.shape[2] // 2
    grouped = query_rows.reshape(row_count, head_count, -1, head_dim)
    key_part = key_value[:, :, :head_dim]
    value_part = key_value[:, :, head_dim:]
    scores = jnp.einsum(
        "rkgd,kpd->kgrp", grouped, key_part, preferred_element_type=jnp.float32
    ) * head_dim ** (-0.5)
    row_max = jnp.max(scores, axis=3, keepdims=True)
    exp_scores = jnp.exp(scores - row_max)
    sum_exp = jnp.sum(exp_scores, axis=3, keepdims=True)
    weights = (exp_scores / sum_exp).astype(jnp.bfloat16)
    blended = jnp.einsum("kgrp,kpd->rkgd", weights, value_part, preferred_element_type=jnp.float32)
    return blended.reshape(row_count, -1)


def on_device_general(queries, kv_cache, question_slot, question_len, out_weight):
    row_count, col_count = queries.shape
    head_dim = kv_cache.shape[2] // 2
    question_count = row_count // QLEN
    per_slot = question_count // NEED
    head_piece = kv_cache[0]
    sharing = lax.axis_size("tensor") // KVH
    if sharing > 1:
        for bit_number in range(sharing.bit_length() - 1):
            partner_piece = swapped(head_piece, "tensor", bit_number)
            upper_member = lax.axis_index("tensor") // 2**bit_number % 2 == 1
            head_piece = jnp.where(
                upper_member,
                jnp.concatenate([partner_piece, head_piece], axis=0),
                jnp.concatenate([head_piece, partner_piece], axis=0),
            )
    key_value = head_piece.reshape(-1, P_SIZE, 2 * head_dim)
    ordering = jnp.argsort(question_slot, stable=True)
    inverse_order = jnp.argsort(ordering, stable=True)
    sorted_rows = queries.reshape(question_count, QLEN, col_count)[ordering]
    sorted_rows = sorted_rows.reshape(NEED, per_slot * QLEN, col_count)
    results = []
    for offset_back in range(NEED):
        if offset_back == 0:
            remote = key_value
        else:
            remote = shifted(key_value, "serve", offset_back)
        results.append(attend(sorted_rows[offset_back], remote))
    sorted_out = jnp.stack(results).reshape(question_count, QLEN, col_count)
    blended = sorted_out[inverse_order].reshape(row_count, col_count)
    token_pos = jnp.arange(row_count, dtype=jnp.int32) % QLEN
    live_rows = token_pos < jnp.repeat(question_len, QLEN, total_repeat_length=row_count)
    attended = jnp.where(live_rows[:, None], blended, 0.0).astype(jnp.bfloat16)
    zero_sum = jnp.zeros((row_count, out_weight.shape[1]), jnp.float32)
    gathered_cols = lax.all_gather(attended, "tensor", axis=1, tiled=True)
    weight_rows = lax.slice_in_dim(out_weight, 0, gathered_cols.shape[1], axis=0)
    answers = zero_sum + jnp.dot(gathered_cols, weight_rows, preferred_element_type=jnp.float32)
    return answers.astype(jnp.bfloat16)


def make_plan(info_ref, slot_ref, len_ref, plan_ref, work_ref):
    count = slot_ref.shape[0]
    per = count // NEED
    half = per * QLEN // 2
    odd = info_ref[1]
    for g in range(NEED):
        work_ref[g] = g * per
        work_ref[NEED + g] = 0

    def step(q, carry):
        slot = slot_ref[q]
        length = len_ref[q]
        last = jnp.where(slot == 1, 3 - odd, 2 + odd)
        seg = jnp.where(slot == 0, 0, jnp.where(slot == 2, 1, last))
        at = work_ref[seg]
        first = work_ref[NEED + seg]
        plan_ref[at] = q
        plan_ref[count + at] = first
        plan_ref[2 * count + at] = length
        work_ref[seg] = at + 1
        work_ref[NEED + seg] = first + length
        return carry

    lax.fori_loop(0, count, step, 0)
    begin = jnp.int32(0)
    for g in range(NEED):
        live = work_ref[NEED + g]
        plan_ref[3 * count + g] = live
        plan_ref[3 * count + NEED + g] = begin
        begin = begin + jnp.maximum(live - half, 0)
    plan_ref[3 * count + 2 * NEED] = begin


def segment_rows(q_ref, plan_ref, seg, low, rows):
    count = q_ref.shape[0] // QLEN
    per = count // NEED
    width = per * QLEN
    lane = lax.broadcasted_iota(jnp.int32, (1, width), 1)
    owner = lane // QLEN
    inner = lane % QLEN
    first = jnp.zeros((1, width), jnp.int32)
    length = jnp.zeros((1, width), jnp.int32)
    blocks = []
    for k in range(per):
        q = plan_ref[seg * per + k]
        blocks.append(q_ref[pl.ds(pl.multiple_of(q * QLEN, QLEN), QLEN), :])
        first = jnp.where(owner == k, plan_ref[count + seg * per + k], first)
        length = jnp.where(owner == k, plan_ref[2 * count + seg * per + k], length)
    target = jnp.where(inner < length, first + inner, -1)
    row = lax.broadcasted_iota(jnp.int32, (rows, width), 0) + low
    pick = jnp.where(row == target, 1.0, 0.0).astype(BF16)
    return jnp.dot(pick, jnp.concatenate(blocks, axis=0), preferred_element_type=F32).astype(BF16)


def load_image(kv_ref, keys_ref, ones_ref):
    dim = kv_ref.shape[1] // 2
    keys_ref[...] = kv_ref[:, :dim].T
    ones_ref[:, :dim] = kv_ref[:, dim:]
    ones_ref[:, dim:] = jnp.ones((kv_ref.shape[0], dim), BF16)


def attend_rows(x, keys_ref, ones_ref, out_ref, base):
    dim = keys_ref.shape[0]
    rows, cols = x.shape
    heads = cols // dim
    group = max(1, min(heads, 256 // rows))
    for low in range(0, heads, group):
        members = range(low, min(low + group, heads))
        q = [x[:, h * dim:(h + 1) * dim] for h in members]
        q = q[0] if len(q) == 1 else jnp.concatenate(q, axis=0)
        s = jnp.dot(q, keys_ref[...], preferred_element_type=F32)
        top = jnp.max(s, axis=1, keepdims=True)
        e = jnp.exp2((s - top) * (LOG2E * dim ** (-0.5))).astype(BF16)
        o = jnp.dot(e, ones_ref[...], preferred_element_type=F32)
        o = (o[:, :dim] / o[:, dim:]).astype(BF16)
        for i, h in enumerate(members):
            out_ref[pl.ds(base, rows), h * dim:(h + 1) * dim] = o[i * rows:(i + 1) * rows, :]


def first_kernel(info_ref, slot_ref, len_ref, q_ref, kv_ref, plan_ref, up_ref, low_ref, work_ref, keys_ref, ones_ref,
                 both_ref):
    make_plan(info_ref, slot_ref, len_ref, plan_ref, work_ref)
    load_image(kv_ref, keys_ref, ones_ref)
    rows = up_ref.shape[0]
    attend_rows(segment_rows(q_ref, plan_ref, 0, 0, 2 * rows), keys_ref, ones_ref, both_ref, 0)
    up_ref[...] = both_ref[:rows, :]
    low_ref[...] = both_ref[rows:, :]


def head_kernel(seg, plan_ref, q_ref, kv_ref, out_ref, keys_ref, ones_ref):
    load_image(kv_ref, keys_ref, ones_ref)
    attend_rows(segment_rows(q_ref, plan_ref, seg, 0, out_ref.shape[0]), keys_ref, ones_ref, out_ref, 0)


def tails_kernel(plan_ref, q_ref, kv0_ref, kv1_ref, kv2_ref, kv3_ref, out_ref, tails_ref, keys_ref, ones_ref):
    count = q_ref.shape[0] // QLEN
    width = tails_ref.shape[0]
    half = width // NEED
    seg = pl.program_id(0)
    live = plan_ref[3 * count + seg] - half

    @pl.when(seg == 0)
    def _():
        tails_ref[...] = jnp.zeros(tails_ref.shape, tails_ref.dtype)

    for g, kv_ref in enumerate((kv0_ref, kv1_ref, kv2_ref, kv3_ref)):
        @pl.when((seg == g) & (live > 0))
        def _():
            load_image(kv_ref, keys_ref, ones_ref)

    for low, high in ((0, half // 4), (half // 4, half // 2), (half // 2, half)):
        @pl.when((live > low) & (live <= high))
        def _():
            x = segment_rows(q_ref, plan_ref, seg, half, high)
            attend_rows(x, keys_ref, ones_ref, tails_ref, pl.multiple_of(seg * half, half))

    @pl.when(seg == NEED - 1)
    def _():
        lane = lax.broadcasted_iota(jnp.int32, (1, width), 1)
        target = jnp.full((1, width), -1, jnp.int32)
        for g in range(NEED):
            inner = lane - g * half
            here = (inner >= 0) & (inner < plan_ref[3 * count + g] - half)
            target = jnp.where(here, plan_ref[3 * count + NEED + g] + inner, target)
        row = lax.broadcasted_iota(jnp.int32, (out_ref.shape[0], width), 0)
        pick = jnp.where(row == target, 1.0, 0.0).astype(BF16)
        out_ref[...] = jnp.dot(pick, tails_ref[...], preferred_element_type=F32).astype(BF16)


def columns(info_ref, line):
    me = info_ref[0]
    upper = me >= line // 2
    pair = jnp.where(upper, 5 - me, 1 - me)
    return me, pair, jnp.where(upper, 1, 2), jnp.where(upper, 0, 3)


def from_afar(info_ref, line, middle_ref, ends_ref, k):
    me = info_ref[0]
    rows = middle_ref.shape[0] // 2
    part = pl.ds(k * rows, rows)
    return jnp.where((me == 0) | (me == line - 1), ends_ref[part, :], middle_ref[part, :])


def project_kernel(info_ref, *refs):
    *chunks, w_ref, out_ref = refs
    depth = chunks[0].shape[1]
    line = w_ref.shape[0] // depth
    total = None
    for k, at in enumerate(columns(info_ref, line)):
        if k < 2:
            pieces = [c[...] for c in chunks[k::4]]
        else:
            pieces = [from_afar(info_ref, line, m, e, k - 2) for m, e in zip(chunks[2::4], chunks[3::4])]
        x = pieces[0] if len(pieces) == 1 else jnp.concatenate(pieces, axis=0)
        w = w_ref[pl.ds(pl.multiple_of(at * depth, depth), depth), :]
        y = jnp.dot(x, w, preferred_element_type=F32)
        total = y if total is None else total + y
    out_ref[...] = total.astype(out_ref.dtype)


def pick_rows(plan_ref, pick_ref, segs, tails):
    rows, width = pick_ref.shape
    count = rows // QLEN
    per = count // NEED
    half = per * QLEN // 2
    sub = lax.broadcasted_iota(jnp.int32, (QLEN, 1), 0)
    lane = lax.broadcasted_iota(jnp.int32, (QLEN, width), 1)
    for seg in range(NEED):
        def step(p, carry):
            at = plan_ref[count + p] + sub
            head = at + (seg - segs[0]) * half if seg in segs else jnp.full_like(at, -1)
            tail = at + len(segs) * half - half + plan_ref[3 * count + NEED + seg] if tails else jnp.full_like(at, -1)
            at = jnp.where(at < half, head, tail)
            at = jnp.where(sub < plan_ref[2 * count + p], at, -1)
            block = pl.ds(pl.multiple_of(plan_ref[p] * QLEN, QLEN), QLEN)
            pick_ref[block, :] = jnp.where(lane == at, 1.0, 0.0).astype(BF16)
            return carry

        lax.fori_loop(seg * per, (seg + 1) * per, step, 0, unroll=4)


def place_kernel(segs, plan_ref, *refs):
    *compact, out_ref, pick_ref = refs

    @pl.when(pl.program_id(0) == 0)
    def _():
        pick_rows(plan_ref, pick_ref, segs, False)

    y = jnp.concatenate([c[...] for c in compact], axis=0)
    out_ref[...] = jnp.dot(pick_ref[...], y, preferred_element_type=F32).astype(out_ref.dtype)


def begin_kernel(segs, info_ref, plan_ref, own3_ref, other3_ref, own_ref, other_ref, w_ref, out_ref, pick_ref):
    @pl.when(pl.program_id(0) == 0)
    def _():
        pick_rows(plan_ref, pick_ref, segs, True)

    depth = own_ref.shape[1]
    upper = info_ref[0] % 2
    total = None
    for x_refs, at in (((own3_ref, own_ref), upper), ((other3_ref, other_ref), 1 - upper)):
        x = jnp.concatenate([r[...] for r in x_refs], axis=0)
        w = w_ref[pl.ds(pl.multiple_of(at * depth, depth), depth), :]
        y = jnp.dot(x, w, preferred_element_type=F32)
        total = y if total is None else total + y
    out_ref[...] = total


def finish_kernel(info_ref, middle3_ref, ends3_ref, middle_ref, ends_ref, pick_ref, begun_ref, placed_ref, w_ref,
                  out_ref, x_ref):
    depth = middle_ref.shape[1]
    line = 2 * (w_ref.shape[0] // depth)
    places = columns(info_ref, line)[2:]

    @pl.when(pl.program_id(0) == 0)
    def _():
        low = middle3_ref.shape[0] // 2
        for k in range(2):
            x_ref[k, :low, :] = from_afar(info_ref, line, middle3_ref, ends3_ref, k)
            x_ref[k, low:, :] = from_afar(info_ref, line, middle_ref, ends_ref, k)

    y = begun_ref[...]
    for k, at in enumerate(places):
        w = w_ref[pl.ds(pl.multiple_of(at % 2 * depth, depth), depth), :]
        y = y + jnp.dot(x_ref[k], w, preferred_element_type=F32)
    z = jnp.dot(pick_ref[...], y.astype(BF16), preferred_element_type=F32)
    out_ref[...] = (placed_ref[...].astype(F32) + z).astype(out_ref.dtype)


SMEM = pl.BlockSpec(memory_space=pltpu.SMEM)
VMEM = pl.BlockSpec(memory_space=pltpu.VMEM)


def on_device_line(queries, kv_cache, question_slot, question_len, out_weight):
    row_count, col_count = queries.shape
    count = row_count // QLEN
    seg_rows = row_count // NEED
    half = seg_rows // 2
    image = kv_cache[0]
    tokens, dim = image.shape[0], image.shape[1] // 2
    heads = col_count // dim
    out_cols = out_weight.shape[1]
    line = lax.axis_size("tensor")
    ring = lax.axis_size("serve")
    info = jnp.stack([lax.axis_index("tensor"), lax.axis_index("serve") % 2]).astype(jnp.int32)

    kv_two = lax.ppermute(image, "serve", [(i, (i + 2) % ring) for i in range(ring)])
    kv_mix = lax.ppermute(image, "serve", [(i, i + 1) if i % 2 == 0 else (i, (i + 3) % ring) for i in range(ring)])
    params = pltpu.CompilerParams(vmem_limit_bytes=40 * MIB)
    plan_size = 3 * count + 2 * NEED + 8

    def cost(micros):
        return pl.CostEstimate(flops=int(micros * 0.3e9), bytes_accessed=image.size, transcendentals=0)

    scratch = [pltpu.VMEM((dim, tokens), BF16), pltpu.VMEM((tokens, 2 * dim), BF16)]
    plan, head_up, head_low = pl.pallas_call(
        first_kernel,
        out_shape=(
            jax.ShapeDtypeStruct((plan_size,), jnp.int32),
            jax.ShapeDtypeStruct((half // 2, col_count), BF16),
            jax.ShapeDtypeStruct((half // 2, col_count), BF16),
        ),
        in_specs=[SMEM, SMEM, SMEM, VMEM, VMEM],
        out_specs=(SMEM, VMEM, VMEM),
        scratch_shapes=[pltpu.SMEM((2 * NEED,), jnp.int32)] + scratch + [pltpu.VMEM((half, col_count), BF16)],
        compiler_params=params,
        cost_estimate=cost(5),
        name="first_head",
    )(info, question_slot, question_len, queries, image)

    def resident(*arrays):
        return [pl.BlockSpec(a.shape, lambda n: (0, 0)) for a in arrays]

    def head(seg, key_value):
        return pl.pallas_call(
            functools.partial(head_kernel, seg),
            out_shape=jax.ShapeDtypeStruct((half, col_count), BF16),
            in_specs=[SMEM, VMEM, VMEM],
            out_specs=VMEM,
            scratch_shapes=scratch,
            compiler_params=params,
            cost_estimate=cost(3),
            name="head",
        )(plan, queries, key_value)

    def tails(rows, *key_values):
        return pl.pallas_call(
            tails_kernel,
            out_shape=jax.ShapeDtypeStruct((rows, col_count), BF16),
            grid=(NEED,),
            in_specs=[SMEM] + resident(queries, *key_values),
            out_specs=pl.BlockSpec((rows, col_count), lambda n: (0, 0)),
            scratch_shapes=[pltpu.VMEM((NEED * half, col_count), BF16)] + scratch,
            compiler_params=params,
            cost_estimate=cost(8),
            name="tails",
        )(plan, queries, *key_values)

    def paired(chunk):
        return chunk, lax.ppermute(chunk, "tensor", [(i, i ^ 1) for i in range(line)])

    def crossed(chunk):
        both = jnp.concatenate(chunk, axis=0)
        return *chunk, lax.ppermute(both, "tensor", [(1, 2), (2, 1)])

    def ended(chunk):
        return *chunk, lax.ppermute(chunk[2], "tensor", [(1, 0), (2, 3)])

    tile = min(512, out_cols)
    steps = (out_cols // tile,)
    w_spec = pl.BlockSpec((out_weight.shape[0], tile), lambda n: (0, n))

    def tiled(rows):
        return pl.BlockSpec((rows, tile), lambda n: (0, n))

    def project(*chunks):
        arrays = [a for c in chunks for a in c]
        rows = sum(c[0].shape[0] for c in chunks)
        return pl.pallas_call(
            project_kernel,
            out_shape=jax.ShapeDtypeStruct((rows, out_cols), BF16),
            grid=steps,
            in_specs=[SMEM] + resident(*arrays) + [w_spec],
            out_specs=tiled(rows),
            compiler_params=params,
            cost_estimate=cost(10),
            name="project",
        )(info, *arrays, out_weight)

    def half_weight(far, tile):
        def index(n, info_ref):
            upper = info_ref[0] // (line // 2)
            return 1 - upper if far else upper, n

        return pl.BlockSpec((out_weight.shape[0] // 2, tile), index)

    def with_info(tile, in_specs, out_specs, scratch_shapes=()):
        return pltpu.PrefetchScalarGridSpec(
            num_scalar_prefetch=1, grid=(out_cols // tile,), in_specs=in_specs, out_specs=out_specs, scratch_shapes=scratch_shapes)

    def fixed(*arrays):
        return [pl.BlockSpec(a.shape, lambda n, info_ref: (0, 0)) for a in arrays]

    def strip(rows, tile):
        return pl.BlockSpec((rows, tile), lambda n, info_ref: (0, n))

    def place(segs, *compact):
        return pl.pallas_call(
            functools.partial(place_kernel, segs),
            out_shape=jax.ShapeDtypeStruct((row_count, out_cols), BF16),
            grid=steps,
            in_specs=[SMEM] + [tiled(c.shape[0]) for c in compact],
            out_specs=tiled(row_count),
            scratch_shapes=[pltpu.VMEM((row_count, sum(c.shape[0] for c in compact)), BF16)],
            compiler_params=params,
            cost_estimate=cost(5),
            name="place",
        )(plan, *compact)

    def begin(segs, own3, other3, own, other):
        rows = own3.shape[0] + own.shape[0]
        width = len(segs) * half + own.shape[0]
        return pl.pallas_call(
            functools.partial(begin_kernel, segs),
            out_shape=(
                jax.ShapeDtypeStruct((rows, out_cols), F32),
                jax.ShapeDtypeStruct((row_count, width), BF16),
            ),
            grid_spec=with_info(
                tile,
                [SMEM] + fixed(own3, other3, own, other) + [half_weight(False, tile)],
                (strip(rows, tile), pl.BlockSpec((row_count, width), lambda n, info_ref: (0, 0))),
            ),
            compiler_params=params,
            cost_estimate=cost(5),
            name="begin",
        )(info, plan, own3, other3, own, other, out_weight)

    def finish(middle3, ends3, middle, ends, pick, begun, placed):
        rows = begun.shape[0]
        return pl.pallas_call(
            finish_kernel,
            out_shape=jax.ShapeDtypeStruct((row_count, out_cols), BF16),
            grid_spec=with_info(
                tile,
                fixed(middle3, ends3, middle, ends, pick)
                + [strip(rows, tile), strip(row_count, tile), half_weight(True, tile)],
                strip(row_count, tile),
                [pltpu.VMEM((2, rows, col_count), BF16)],
            ),
            compiler_params=params,
            cost_estimate=cost(7),
            name="finish",
        )(info, middle3, ends3, middle, ends, pick, begun, placed, out_weight)

    def after(value, other):
        return lax.optimization_barrier((value, other))[0]

    up, low = crossed(paired(head_up)), paired(head_low)
    kv_two, low, _ = lax.optimization_barrier((kv_two, low, up[2]))
    kv_swap = lax.ppermute(kv_two, "serve", [(i, i ^ 1) for i in range(ring)])
    low = crossed(low)
    up = ended(up)
    chunk1 = paired(head(1, kv_two))
    kv_mix = after(kv_mix, (chunk1[1], low[2]))
    low = ended(low)
    chunk1 = crossed((chunk1[0], after(chunk1[1], up[3])))
    chunk2 = paired(head(2, kv_mix))
    head3 = head(3, kv_swap)
    chunk1 = ended((*chunk1[:2], after(chunk1[2], head3)))
    chunk2 = crossed((chunk2[0], after(chunk2[1], (low[3], head3))))
    chunk3 = crossed(paired(head3))
    rest = tails(NEED * half, image, kv_two, after(kv_mix, chunk3[1]), kv_swap)
    early = half * 3 // 2
    rest_pair = paired(rest[:early])
    chunk2 = ended((*chunk2[:2], after(chunk2[2], rest)))
    live_rest = plan[3 * count + 2 * NEED]
    sizes = [int(half * k) // 4 for k in (4, 5.5, 7, 9, 16)]

    def branch(size, rest, rest_pair, up, low, chunk1, chunk2, chunk3):
        own, other = rest_pair
        if size > early:
            own, other = [
                jnp.concatenate(pieces, axis=0) for pieces in zip(rest_pair, paired(rest[early:size]))]
        own, other, middle = crossed((own[:size], other[:size]))
        own3, other3, middle3, ends3 = ended(chunk3)
        done = project(up, low, chunk1, chunk2)
        middle = after(middle, (ends3, done))
        own, other, middle, ends = ended((own, other, middle))
        begun, pick = begin((3,), own3, other3, own, other)
        return finish(middle3, ends3, middle, ends, pick, begun, place((0, 1, 2), done))

    index = sum([(live_rest > s).astype(jnp.int32) for s in sizes[:-1]])
    branches = [functools.partial(branch, s) for s in sizes]
    return lax.switch(index, branches, rest, rest_pair, up, low, chunk1, chunk2, chunk3)


def solution(mesh):
    plain = mesh.shape["tensor"] == KVH == 4 and mesh.shape["serve"] % 2 == 0 and NEED == 4
    return jax.shard_map(
        on_device_line if plain else on_device_general,
        mesh=mesh,
        in_specs=(
            P("serve", "tensor"),
            P("serve", "tensor", None),
            P("serve"),
            P("serve"),
            P(None, "tensor"),
        ),
        out_specs=P("serve", "tensor"),
        check_vma=False,
    )
```

```python
import functools

import jax
import jax.numpy as jnp
from jax import lax
from jax.experimental import pallas as pl
from jax.experimental.pallas import tpu as pltpu
from jax.sharding import PartitionSpec as P

KVH = 4
P_SIZE = 1600
QLEN = 32
NEED = 4
LOG2E = 1.4426950408889634
MIB = 1 << 20
F32 = jnp.float32
BF16 = jnp.bfloat16


def swapped(shard, axis, bit):
    return lax.ppermute(shard, axis, [(i, i ^ 1 << bit) for i in range(lax.axis_size(axis))])


def shifted(value, axis, steps):
    count = lax.axis_size(axis)
    pairs = [(source, (source + steps) % count) for source in range(count)]
    return lax.ppermute(value, axis, pairs)


def attend(query_rows, key_value):
    row_count = query_rows.shape[0]
    head_count = key_value.shape[0]
    head_dim = key_value.shape[2] // 2
    grouped = query_rows.reshape(row_count, head_count, -1, head_dim)
    key_part = key_value[:, :, :head_dim]
    value_part = key_value[:, :, head_dim:]
    scores = jnp.einsum(
        "rkgd,kpd->kgrp", grouped, key_part, preferred_element_type=jnp.float32
    ) * head_dim ** (-0.5)
    row_max = jnp.max(scores, axis=3, keepdims=True)
    exp_scores = jnp.exp(scores - row_max)
    sum_exp = jnp.sum(exp_scores, axis=3, keepdims=True)
    weights = (exp_scores / sum_exp).astype(jnp.bfloat16)
    blended = jnp.einsum("kgrp,kpd->rkgd", weights, value_part, preferred_element_type=jnp.float32)
    return blended.reshape(row_count, -1)


def on_device_general(queries, kv_cache, question_slot, question_len, out_weight):
    row_count, col_count = queries.shape
    head_dim = kv_cache.shape[2] // 2
    question_count = row_count // QLEN
    per_slot = question_count // NEED
    head_piece = kv_cache[0]
    sharing = lax.axis_size("tensor") // KVH
    if sharing > 1:
        for bit_number in range(sharing.bit_length() - 1):
            partner_piece = swapped(head_piece, "tensor", bit_number)
            upper_member = lax.axis_index("tensor") // 2**bit_number % 2 == 1
            head_piece = jnp.where(
                upper_member,
                jnp.concatenate([partner_piece, head_piece], axis=0),
                jnp.concatenate([head_piece, partner_piece], axis=0),
            )
    key_value = head_piece.reshape(-1, P_SIZE, 2 * head_dim)
    ordering = jnp.argsort(question_slot, stable=True)
    inverse_order = jnp.argsort(ordering, stable=True)
    sorted_rows = queries.reshape(question_count, QLEN, col_count)[ordering]
    sorted_rows = sorted_rows.reshape(NEED, per_slot * QLEN, col_count)
    results = []
    for offset_back in range(NEED):
        if offset_back == 0:
            remote = key_value
        else:
            remote = shifted(key_value, "serve", offset_back)
        results.append(attend(sorted_rows[offset_back], remote))
    sorted_out = jnp.stack(results).reshape(question_count, QLEN, col_count)
    blended = sorted_out[inverse_order].reshape(row_count, col_count)
    token_pos = jnp.arange(row_count, dtype=jnp.int32) % QLEN
    live_rows = token_pos < jnp.repeat(question_len, QLEN, total_repeat_length=row_count)
    attended = jnp.where(live_rows[:, None], blended, 0.0).astype(jnp.bfloat16)
    zero_sum = jnp.zeros((row_count, out_weight.shape[1]), jnp.float32)
    gathered_cols = lax.all_gather(attended, "tensor", axis=1, tiled=True)
    weight_rows = lax.slice_in_dim(out_weight, 0, gathered_cols.shape[1], axis=0)
    answers = zero_sum + jnp.dot(gathered_cols, weight_rows, preferred_element_type=jnp.float32)
    return answers.astype(jnp.bfloat16)


def make_plan(info_ref, slot_ref, len_ref, plan_ref, work_ref):
    count = slot_ref.shape[0]
    per = count // NEED
    half = per * QLEN // 2
    odd = info_ref[1]
    for g in range(NEED):
        work_ref[g] = g * per
        work_ref[NEED + g] = 0

    def step(q, carry):
        slot = slot_ref[q]
        length = len_ref[q]
        last = jnp.where(slot == 1, 3 - odd, 2 + odd)
        seg = jnp.where(slot == 0, 0, jnp.where(slot == 2, 1, last))
        at = work_ref[seg]
        first = work_ref[NEED + seg]
        plan_ref[at] = q
        plan_ref[count + at] = first
        plan_ref[2 * count + at] = length
        work_ref[seg] = at + 1
        work_ref[NEED + seg] = first + length
        return carry

    lax.fori_loop(0, count, step, 0)
    begin = jnp.int32(0)
    for g in range(NEED):
        live = work_ref[NEED + g]
        plan_ref[3 * count + g] = live
        plan_ref[3 * count + NEED + g] = begin
        begin = begin + jnp.maximum(live - half, 0)
    plan_ref[3 * count + 2 * NEED] = begin


def segment_rows(q_ref, plan_ref, seg, low, rows):
    count = q_ref.shape[0] // QLEN
    per = count // NEED
    width = per * QLEN
    lane = lax.broadcasted_iota(jnp.int32, (1, width), 1)
    owner = lane // QLEN
    inner = lane % QLEN
    first = jnp.zeros((1, width), jnp.int32)
    length = jnp.zeros((1, width), jnp.int32)
    blocks = []
    for k in range(per):
        q = plan_ref[seg * per + k]
        blocks.append(q_ref[pl.ds(pl.multiple_of(q * QLEN, QLEN), QLEN), :])
        first = jnp.where(owner == k, plan_ref[count + seg * per + k], first)
        length = jnp.where(owner == k, plan_ref[2 * count + seg * per + k], length)
    target = jnp.where(inner < length, first + inner, -1)
    row = lax.broadcasted_iota(jnp.int32, (rows, width), 0) + low
    pick = jnp.where(row == target, 1.0, 0.0).astype(BF16)
    return jnp.dot(pick, jnp.concatenate(blocks, axis=0), preferred_element_type=F32).astype(BF16)


def load_image(kv_ref, keys_ref, ones_ref):
    dim = kv_ref.shape[1] // 2
    keys_ref[...] = kv_ref[:, :dim].T
    ones_ref[:, :dim] = kv_ref[:, dim:]
    ones_ref[:, dim:] = jnp.ones((kv_ref.shape[0], dim), BF16)


def attend_rows(rows_ref, rows, keys_ref, ones_ref, out_ref, base):
    dim = keys_ref.shape[0]
    heads = rows_ref.shape[1] // dim
    group = max(1, min(heads, 256 // rows))

    def step(n, carry):
        places = [pl.ds(pl.multiple_of((n * group + i) * dim, dim), dim) for i in range(group)]
        q = [rows_ref[:rows, cols] for cols in places]
        q = q[0] if len(q) == 1 else jnp.concatenate(q, axis=0)
        s = jnp.dot(q, keys_ref[...], preferred_element_type=F32)
        top = jnp.max(s, axis=1, keepdims=True)
        e = jnp.exp2((s - top) * (LOG2E * dim ** (-0.5))).astype(BF16)
        o = jnp.dot(e, ones_ref[...], preferred_element_type=F32)
        o = (o[:, :dim] / o[:, dim:]).astype(BF16)
        for i, cols in enumerate(places):
            out_ref[pl.ds(base, rows), cols] = o[i * rows:(i + 1) * rows, :]
        return carry

    steps = heads // group
    lax.fori_loop(0, steps, step, 0, unroll=min(steps, 2))


def first_kernel(info_ref, slot_ref, len_ref, q_ref, kv_ref, plan_ref, up_ref, low_ref, work_ref, keys_ref, ones_ref,
                 rows_ref, both_ref):
    make_plan(info_ref, slot_ref, len_ref, plan_ref, work_ref)
    load_image(kv_ref, keys_ref, ones_ref)
    rows = up_ref.shape[0]
    rows_ref[...] = segment_rows(q_ref, plan_ref, 0, 0, 2 * rows)
    attend_rows(rows_ref, 2 * rows, keys_ref, ones_ref, both_ref, 0)
    up_ref[...] = both_ref[:rows, :]
    low_ref[...] = both_ref[rows:, :]


def head_kernel(seg, plan_ref, q_ref, kv_ref, out_ref, keys_ref, ones_ref, rows_ref):
    load_image(kv_ref, keys_ref, ones_ref)
    rows_ref[...] = segment_rows(q_ref, plan_ref, seg, 0, out_ref.shape[0])
    attend_rows(rows_ref, out_ref.shape[0], keys_ref, ones_ref, out_ref, 0)


def tails_kernel(plan_ref, q_ref, kv0_ref, kv1_ref, kv2_ref, kv3_ref, out_ref, tails_ref, keys_ref, ones_ref,
                 rows_ref):
    count = q_ref.shape[0] // QLEN
    width = tails_ref.shape[0]
    half = width // NEED
    seg = pl.program_id(0)
    live = plan_ref[3 * count + seg] - half

    @pl.when(seg == 0)
    def _():
        tails_ref[...] = jnp.zeros(tails_ref.shape, tails_ref.dtype)

    for g, kv_ref in enumerate((kv0_ref, kv1_ref, kv2_ref, kv3_ref)):
        @pl.when((seg == g) & (live > 0))
        def _():
            load_image(kv_ref, keys_ref, ones_ref)

    @pl.when(live > 0)
    def _():
        rows_ref[...] = segment_rows(q_ref, plan_ref, seg, half, half)

    for low, high in ((0, half // 4), (half // 4, half // 2), (half // 2, half)):
        @pl.when((live > low) & (live <= high))
        def _():
            attend_rows(rows_ref, high, keys_ref, ones_ref, tails_ref, pl.multiple_of(seg * half, half))

    @pl.when(seg == NEED - 1)
    def _():
        lane = lax.broadcasted_iota(jnp.int32, (1, width), 1)
        target = jnp.full((1, width), -1, jnp.int32)
        for g in range(NEED):
            inner = lane - g * half
            here = (inner >= 0) & (inner < plan_ref[3 * count + g] - half)
            target = jnp.where(here, plan_ref[3 * count + NEED + g] + inner, target)

        def pack(n, carry):
            low = pl.multiple_of(n * half, half)
            row = lax.broadcasted_iota(jnp.int32, (half, width), 0) + low
            pick = jnp.where(row == target, 1.0, 0.0).astype(BF16)
            out_ref[pl.ds(low, half), :] = jnp.dot(pick, tails_ref[...], preferred_element_type=F32).astype(BF16)
            return carry

        lax.fori_loop(0, out_ref.shape[0] // half, pack, 0)


def columns(info_ref, line):
    me = info_ref[0]
    upper = me >= line // 2
    pair = jnp.where(upper, 5 - me, 1 - me)
    return me, pair, jnp.where(upper, 1, 2), jnp.where(upper, 0, 3)


def from_afar(info_ref, line, middle_ref, ends_ref, k):
    me = info_ref[0]
    rows = middle_ref.shape[0] // 2
    part = pl.ds(k * rows, rows)
    return jnp.where((me == 0) | (me == line - 1), ends_ref[part, :], middle_ref[part, :])


def project_kernel(info_ref, *refs):
    *chunks, w_ref, out_ref = refs
    depth = chunks[0].shape[1]
    line = w_ref.shape[0] // depth
    total = None
    for k, at in enumerate(columns(info_ref, line)):
        if k < 2:
            pieces = [c[...] for c in chunks[k::4]]
        else:
            pieces = [from_afar(info_ref, line, m, e, k - 2) for m, e in zip(chunks[2::4], chunks[3::4])]
        x = pieces[0] if len(pieces) == 1 else jnp.concatenate(pieces, axis=0)
        w = w_ref[pl.ds(pl.multiple_of(at * depth, depth), depth), :]
        y = jnp.dot(x, w, preferred_element_type=F32)
        total = y if total is None else total + y
    out_ref[...] = total.astype(out_ref.dtype)


def pick_rows(plan_ref, pick_ref, segs, tails):
    rows, width = pick_ref.shape
    count = rows // QLEN
    per = count // NEED
    half = per * QLEN // 2
    sub = lax.broadcasted_iota(jnp.int32, (QLEN, 1), 0)
    lane = lax.broadcasted_iota(jnp.int32, (QLEN, width), 1)
    first = segs[0] if segs else 0

    def step(p, carry):
        seg = p // per
        at = plan_ref[count + p] + sub
        head = jnp.where((seg >= first) & (seg < first + len(segs)), at + (seg - first) * half, -1)
        tail = at + (len(segs) - 1) * half + plan_ref[3 * count + NEED + seg] if tails else jnp.full_like(at, -1)
        at = jnp.where(at < half, head, tail)
        at = jnp.where(sub < plan_ref[2 * count + p], at, -1)
        block = pl.ds(pl.multiple_of(plan_ref[p] * QLEN, QLEN), QLEN)
        pick_ref[block, :] = jnp.where(lane == at, 1.0, 0.0).astype(BF16)
        return carry

    lax.fori_loop(0, count, step, 0, unroll=2)


def over_rows(out_ref, body):
    tall = out_ref.shape[0] // 2

    def step(n, carry):
        rows = pl.ds(pl.multiple_of(n * tall, tall), tall)
        out_ref[rows, :] = body(rows).astype(out_ref.dtype)
        return carry

    lax.fori_loop(0, 2, step, 0)


def place_kernel(segs, plan_ref, *refs):
    *compact, out_ref, pick_ref = refs

    @pl.when(pl.program_id(0) == 0)
    def _():
        pick_rows(plan_ref, pick_ref, segs, False)

    y = jnp.concatenate([c[...] for c in compact], axis=0)
    over_rows(out_ref, lambda rows: jnp.dot(pick_ref[rows, :], y, preferred_element_type=F32))


def begin_kernel(segs, info_ref, plan_ref, own3_ref, other3_ref, own_ref, other_ref, w_ref, out_ref, pick_ref):
    @pl.when(pl.program_id(0) == 0)
    def _():
        pick_rows(plan_ref, pick_ref, segs, True)

    depth = own_ref.shape[1]
    upper = info_ref[0] % 2
    total = None
    for x_refs, at in (((own3_ref, own_ref), upper), ((other3_ref, other_ref), 1 - upper)):
        x = jnp.concatenate([r[...] for r in x_refs], axis=0)
        w = w_ref[pl.ds(pl.multiple_of(at * depth, depth), depth), :]
        y = jnp.dot(x, w, preferred_element_type=F32)
        total = y if total is None else total + y
    out_ref[...] = total


def finish_kernel(info_ref, middle3_ref, ends3_ref, middle_ref, ends_ref, pick_ref, begun_ref, placed_ref, w_ref,
                  out_ref, x_ref):
    depth = middle_ref.shape[1]
    line = 2 * (w_ref.shape[0] // depth)
    places = columns(info_ref, line)[2:]

    @pl.when(pl.program_id(0) == 0)
    def _():
        low = middle3_ref.shape[0] // 2
        for k in range(2):
            x_ref[k, :low, :] = from_afar(info_ref, line, middle3_ref, ends3_ref, k)
            x_ref[k, low:, :] = from_afar(info_ref, line, middle_ref, ends_ref, k)

    y = begun_ref[...]
    for k, at in enumerate(places):
        w = w_ref[pl.ds(pl.multiple_of(at % 2 * depth, depth), depth), :]
        y = y + jnp.dot(x_ref[k], w, preferred_element_type=F32)
    y = y.astype(BF16)

    def body(rows):
        return placed_ref[rows, :].astype(F32) + jnp.dot(pick_ref[rows, :], y, preferred_element_type=F32)

    over_rows(out_ref, body)


SMEM = pl.BlockSpec(memory_space=pltpu.SMEM)
VMEM = pl.BlockSpec(memory_space=pltpu.VMEM)


def on_device_line(queries, kv_cache, question_slot, question_len, out_weight):
    row_count, col_count = queries.shape
    count = row_count // QLEN
    seg_rows = row_count // NEED
    half = seg_rows // 2
    image = kv_cache[0]
    tokens, dim = image.shape[0], image.shape[1] // 2
    heads = col_count // dim
    out_cols = out_weight.shape[1]
    line = lax.axis_size("tensor")
    ring = lax.axis_size("serve")
    info = jnp.stack([lax.axis_index("tensor"), lax.axis_index("serve") % 2]).astype(jnp.int32)

    kv_two = lax.ppermute(image, "serve", [(i, (i + 2) % ring) for i in range(ring)])
    kv_mix = lax.ppermute(image, "serve", [(i, i + 1) if i % 2 == 0 else (i, (i + 3) % ring) for i in range(ring)])
    params = pltpu.CompilerParams(vmem_limit_bytes=40 * MIB)
    plan_size = 3 * count + 2 * NEED + 8

    def cost(micros):
        return pl.CostEstimate(flops=int(micros * 0.3e9), bytes_accessed=image.size, transcendentals=0)

    scratch = [
        pltpu.VMEM((dim, tokens), BF16),
        pltpu.VMEM((tokens, 2 * dim), BF16),
        pltpu.VMEM((half, col_count), BF16),
    ]
    plan, head_up, head_low = pl.pallas_call(
        first_kernel,
        out_shape=(
            jax.ShapeDtypeStruct((plan_size,), jnp.int32),
            jax.ShapeDtypeStruct((half // 2, col_count), BF16),
            jax.ShapeDtypeStruct((half // 2, col_count), BF16),
        ),
        in_specs=[SMEM, SMEM, SMEM, VMEM, VMEM],
        out_specs=(SMEM, VMEM, VMEM),
        scratch_shapes=[pltpu.SMEM((2 * NEED,), jnp.int32)] + scratch + [pltpu.VMEM((half, col_count), BF16)],
        compiler_params=params,
        cost_estimate=cost(5),
        name="first_head",
    )(info, question_slot, question_len, queries, image)

    def resident(*arrays):
        return [pl.BlockSpec(a.shape, lambda n: (0, 0)) for a in arrays]

    def head(seg, key_value):
        return pl.pallas_call(
            functools.partial(head_kernel, seg),
            out_shape=jax.ShapeDtypeStruct((half, col_count), BF16),
            in_specs=[SMEM, VMEM, VMEM],
            out_specs=VMEM,
            scratch_shapes=scratch,
            compiler_params=params,
            cost_estimate=cost(3),
            name="head",
        )(plan, queries, key_value)

    def tails(rows, *key_values):
        return pl.pallas_call(
            tails_kernel,
            out_shape=jax.ShapeDtypeStruct((rows, col_count), BF16),
            grid=(NEED,),
            in_specs=[SMEM] + resident(queries, *key_values),
            out_specs=pl.BlockSpec((rows, col_count), lambda n: (0, 0)),
            scratch_shapes=[pltpu.VMEM((NEED * half, col_count), BF16)] + scratch,
            compiler_params=params,
            cost_estimate=cost(8),
            name="tails",
        )(plan, queries, *key_values)

    def paired(chunk):
        return chunk, lax.ppermute(chunk, "tensor", [(i, i ^ 1) for i in range(line)])

    def crossed(chunk):
        both = jnp.concatenate(chunk, axis=0)
        return *chunk, lax.ppermute(both, "tensor", [(1, 2), (2, 1)])

    def ended(chunk):
        return *chunk, lax.ppermute(chunk[2], "tensor", [(1, 0), (2, 3)])

    tile = min(512, out_cols)
    steps = (out_cols // tile,)
    w_spec = pl.BlockSpec((out_weight.shape[0], tile), lambda n: (0, n))

    def tiled(rows):
        return pl.BlockSpec((rows, tile), lambda n: (0, n))

    def project(*chunks):
        arrays = [a for c in chunks for a in c]
        rows = sum(c[0].shape[0] for c in chunks)
        return pl.pallas_call(
            project_kernel,
            out_shape=jax.ShapeDtypeStruct((rows, out_cols), BF16),
            grid=steps,
            in_specs=[SMEM] + resident(*arrays) + [w_spec],
            out_specs=tiled(rows),
            compiler_params=params,
            cost_estimate=cost(10),
            name="project",
        )(info, *arrays, out_weight)

    def half_weight(far, tile):
        def index(n, info_ref):
            upper = info_ref[0] // (line // 2)
            return 1 - upper if far else upper, n

        return pl.BlockSpec((out_weight.shape[0] // 2, tile), index)

    def with_info(tile, in_specs, out_specs, scratch_shapes=()):
        return pltpu.PrefetchScalarGridSpec(
            num_scalar_prefetch=1, grid=(out_cols // tile,), in_specs=in_specs, out_specs=out_specs, scratch_shapes=scratch_shapes)

    def fixed(*arrays):
        return [pl.BlockSpec(a.shape, lambda n, info_ref: (0, 0)) for a in arrays]

    def strip(rows, tile):
        return pl.BlockSpec((rows, tile), lambda n, info_ref: (0, n))

    def place(segs, *compact):
        return pl.pallas_call(
            functools.partial(place_kernel, segs),
            out_shape=jax.ShapeDtypeStruct((row_count, out_cols), BF16),
            grid=steps,
            in_specs=[SMEM] + [tiled(c.shape[0]) for c in compact],
            out_specs=tiled(row_count),
            scratch_shapes=[pltpu.VMEM((row_count, sum(c.shape[0] for c in compact)), BF16)],
            compiler_params=params,
            cost_estimate=cost(5),
            name="place",
        )(plan, *compact)

    def begin(segs, own3, other3, own, other):
        rows = own3.shape[0] + own.shape[0]
        width = len(segs) * half + own.shape[0]
        return pl.pallas_call(
            functools.partial(begin_kernel, segs),
            out_shape=(
                jax.ShapeDtypeStruct((rows, out_cols), F32),
                jax.ShapeDtypeStruct((row_count, width), BF16),
            ),
            grid_spec=with_info(
                tile,
                [SMEM] + fixed(own3, other3, own, other) + [half_weight(False, tile)],
                (strip(rows, tile), pl.BlockSpec((row_count, width), lambda n, info_ref: (0, 0))),
            ),
            compiler_params=params,
            cost_estimate=cost(5),
            name="begin",
        )(info, plan, own3, other3, own, other, out_weight)

    def finish(middle3, ends3, middle, ends, pick, begun, placed):
        rows = begun.shape[0]
        return pl.pallas_call(
            finish_kernel,
            out_shape=jax.ShapeDtypeStruct((row_count, out_cols), BF16),
            grid_spec=with_info(
                tile,
                fixed(middle3, ends3, middle, ends, pick)
                + [strip(rows, tile), strip(row_count, tile), half_weight(True, tile)],
                strip(row_count, tile),
                [pltpu.VMEM((2, rows, col_count), BF16)],
            ),
            compiler_params=params,
            cost_estimate=cost(7),
            name="finish",
        )(info, middle3, ends3, middle, ends, pick, begun, placed, out_weight)

    def after(value, other):
        return lax.optimization_barrier((value, other))[0]

    up, low = crossed(paired(head_up)), paired(head_low)
    kv_two, low, _ = lax.optimization_barrier((kv_two, low, up[2]))
    kv_swap = lax.ppermute(kv_two, "serve", [(i, i ^ 1) for i in range(ring)])
    low = crossed(low)
    up = ended(up)
    chunk1 = paired(head(1, kv_two))
    kv_mix = after(kv_mix, (chunk1[1], low[2]))
    low = ended(low)
    chunk1 = crossed((chunk1[0], after(chunk1[1], up[3])))
    chunk2 = paired(head(2, kv_mix))
    head3 = head(3, kv_swap)
    chunk1 = ended((*chunk1[:2], after(chunk1[2], head3)))
    chunk2 = crossed((chunk2[0], after(chunk2[1], (low[3], head3))))
    chunk3 = crossed(paired(head3))
    rest = tails(NEED * half, image, kv_two, after(kv_mix, chunk3[1]), kv_swap)
    early = half * 3 // 2
    rest_pair = paired(rest[:early])
    chunk2 = ended((*chunk2[:2], after(chunk2[2], rest)))
    live_rest = plan[3 * count + 2 * NEED]
    sizes = [int(half * k) // 4 for k in (4, 5.5, 7, 9, 16)]

    def branch(size, rest, rest_pair, up, low, chunk1, chunk2, chunk3):
        own, other = rest_pair
        if size > early:
            own, other = [
                jnp.concatenate(pieces, axis=0) for pieces in zip(rest_pair, paired(rest[early:size]))]
        own, other, middle = crossed((own[:size], other[:size]))
        own3, other3, middle3, ends3 = ended(chunk3)
        done = project(up, low, chunk1, chunk2)
        middle = after(middle, (ends3, done))
        own, other, middle, ends = ended((own, other, middle))
        begun, pick = begin((3,), own3, other3, own, other)
        return finish(middle3, ends3, middle, ends, pick, begun, place((0, 1, 2), done))

    index = sum([(live_rest > s).astype(jnp.int32) for s in sizes[:-1]])
    branches = [functools.partial(branch, s) for s in sizes]
    return lax.switch(index, branches, rest, rest_pair, up, low, chunk1, chunk2, chunk3)


def solution(mesh):
    plain = mesh.shape["tensor"] == KVH == 4 and mesh.shape["serve"] % 2 == 0 and NEED == 4
    return jax.shard_map(
        on_device_line if plain else on_device_general,
        mesh=mesh,
        in_specs=(
            P("serve", "tensor"),
            P("serve", "tensor", None),
            P("serve"),
            P("serve"),
            P(None, "tensor"),
        ),
        out_specs=P("serve", "tensor"),
        check_vma=False,
    )
```

```python
import functools

import jax
import jax.numpy as jnp
from jax import lax
from jax.experimental import pallas as pl
from jax.experimental.pallas import tpu as pltpu
from jax.sharding import PartitionSpec as P

KVH = 4
P_SIZE = 1600
QLEN = 32
NEED = 4
LOG2E = 1.4426950408889634
MIB = 1 << 20
F32 = jnp.float32
BF16 = jnp.bfloat16


def swapped(shard, axis, bit):
    return lax.ppermute(shard, axis, [(i, i ^ 1 << bit) for i in range(lax.axis_size(axis))])


def shifted(value, axis, steps):
    count = lax.axis_size(axis)
    pairs = [(source, (source + steps) % count) for source in range(count)]
    return lax.ppermute(value, axis, pairs)


def attend(query_rows, key_value):
    row_count = query_rows.shape[0]
    head_count = key_value.shape[0]
    head_dim = key_value.shape[2] // 2
    grouped = query_rows.reshape(row_count, head_count, -1, head_dim)
    key_part = key_value[:, :, :head_dim]
    value_part = key_value[:, :, head_dim:]
    scores = jnp.einsum(
        "rkgd,kpd->kgrp", grouped, key_part, preferred_element_type=jnp.float32
    ) * head_dim ** (-0.5)
    row_max = jnp.max(scores, axis=3, keepdims=True)
    exp_scores = jnp.exp(scores - row_max)
    sum_exp = jnp.sum(exp_scores, axis=3, keepdims=True)
    weights = (exp_scores / sum_exp).astype(jnp.bfloat16)
    blended = jnp.einsum("kgrp,kpd->rkgd", weights, value_part, preferred_element_type=jnp.float32)
    return blended.reshape(row_count, -1)


def on_device_general(queries, kv_cache, question_slot, question_len, out_weight):
    row_count, col_count = queries.shape
    head_dim = kv_cache.shape[2] // 2
    question_count = row_count // QLEN
    per_slot = question_count // NEED
    head_piece = kv_cache[0]
    sharing = lax.axis_size("tensor") // KVH
    if sharing > 1:
        for bit_number in range(sharing.bit_length() - 1):
            partner_piece = swapped(head_piece, "tensor", bit_number)
            upper_member = lax.axis_index("tensor") // 2**bit_number % 2 == 1
            head_piece = jnp.where(
                upper_member,
                jnp.concatenate([partner_piece, head_piece], axis=0),
                jnp.concatenate([head_piece, partner_piece], axis=0),
            )
    key_value = head_piece.reshape(-1, P_SIZE, 2 * head_dim)
    ordering = jnp.argsort(question_slot, stable=True)
    inverse_order = jnp.argsort(ordering, stable=True)
    sorted_rows = queries.reshape(question_count, QLEN, col_count)[ordering]
    sorted_rows = sorted_rows.reshape(NEED, per_slot * QLEN, col_count)
    results = []
    for offset_back in range(NEED):
        if offset_back == 0:
            remote = key_value
        else:
            remote = shifted(key_value, "serve", offset_back)
        results.append(attend(sorted_rows[offset_back], remote))
    sorted_out = jnp.stack(results).reshape(question_count, QLEN, col_count)
    blended = sorted_out[inverse_order].reshape(row_count, col_count)
    token_pos = jnp.arange(row_count, dtype=jnp.int32) % QLEN
    live_rows = token_pos < jnp.repeat(question_len, QLEN, total_repeat_length=row_count)
    attended = jnp.where(live_rows[:, None], blended, 0.0).astype(jnp.bfloat16)
    zero_sum = jnp.zeros((row_count, out_weight.shape[1]), jnp.float32)
    gathered_cols = lax.all_gather(attended, "tensor", axis=1, tiled=True)
    weight_rows = lax.slice_in_dim(out_weight, 0, gathered_cols.shape[1], axis=0)
    answers = zero_sum + jnp.dot(gathered_cols, weight_rows, preferred_element_type=jnp.float32)
    return answers.astype(jnp.bfloat16)


def make_plan(slot_ref, len_ref, plan_ref, work_ref):
    count = slot_ref.shape[0]
    per = count // NEED
    half = per * QLEN // 2
    for g in range(NEED):
        work_ref[g] = g * per
        work_ref[NEED + g] = 0

    def step(q, carry):
        seg = slot_ref[q]
        length = len_ref[q]
        at = work_ref[seg]
        first = work_ref[NEED + seg]
        plan_ref[at] = q
        plan_ref[count + at] = first
        plan_ref[2 * count + at] = length
        work_ref[seg] = at + 1
        work_ref[NEED + seg] = first + length
        return carry

    lax.fori_loop(0, count, step, 0)
    begin = jnp.int32(0)
    for g in range(NEED):
        live = work_ref[NEED + g]
        plan_ref[3 * count + g] = live
        plan_ref[3 * count + NEED + g] = begin
        begin = begin + jnp.maximum(live - half, 0)
    plan_ref[3 * count + 2 * NEED] = begin


def segment_rows(q_ref, plan_ref, seg, low, rows):
    count = q_ref.shape[0] // QLEN
    per = count // NEED
    width = per * QLEN
    lane = lax.broadcasted_iota(jnp.int32, (1, width), 1)
    owner = lane // QLEN
    inner = lane % QLEN
    first = jnp.zeros((1, width), jnp.int32)
    length = jnp.zeros((1, width), jnp.int32)
    blocks = []
    for k in range(per):
        q = plan_ref[seg * per + k]
        blocks.append(q_ref[pl.ds(pl.multiple_of(q * QLEN, QLEN), QLEN), :])
        first = jnp.where(owner == k, plan_ref[count + seg * per + k], first)
        length = jnp.where(owner == k, plan_ref[2 * count + seg * per + k], length)
    target = jnp.where(inner < length, first + inner, -1)
    row = lax.broadcasted_iota(jnp.int32, (rows, width), 0) + low
    pick = jnp.where(row == target, 1.0, 0.0).astype(BF16)
    return jnp.dot(pick, jnp.concatenate(blocks, axis=0), preferred_element_type=F32).astype(BF16)


def load_image(kv_ref, keys_ref, ones_ref):
    dim = kv_ref.shape[1] // 2
    keys_ref[...] = kv_ref[:, :dim].T
    ones_ref[:, :dim] = kv_ref[:, dim:]
    ones_ref[:, dim:] = jnp.ones((kv_ref.shape[0], dim), BF16)


def attend_rows(rows_ref, rows, keys_ref, ones_ref, out_ref, base):
    dim = keys_ref.shape[0]
    heads = rows_ref.shape[1] // dim
    group = max(1, min(heads, 256 // rows))

    def step(n, carry):
        places = [pl.ds(pl.multiple_of((n * group + i) * dim, dim), dim) for i in range(group)]
        q = [rows_ref[:rows, cols] for cols in places]
        q = q[0] if len(q) == 1 else jnp.concatenate(q, axis=0)
        s = jnp.dot(q, keys_ref[...], preferred_element_type=F32)
        top = jnp.max(s, axis=1, keepdims=True)
        e = jnp.exp2((s - top) * (LOG2E * dim ** (-0.5))).astype(BF16)
        o = jnp.dot(e, ones_ref[...], preferred_element_type=F32)
        o = (o[:, :dim] / o[:, dim:]).astype(BF16)
        for i, cols in enumerate(places):
            out_ref[pl.ds(base, rows), cols] = o[i * rows:(i + 1) * rows, :]
        return carry

    steps = heads // group
    lax.fori_loop(0, steps, step, 0, unroll=min(steps, 2))


def first_kernel(slot_ref, len_ref, q_ref, kv_ref, plan_ref, up_ref, low_ref, work_ref, keys_ref, ones_ref,
                 rows_ref, both_ref):
    make_plan(slot_ref, len_ref, plan_ref, work_ref)
    load_image(kv_ref, keys_ref, ones_ref)
    rows = up_ref.shape[0]
    rows_ref[...] = segment_rows(q_ref, plan_ref, 0, 0, 2 * rows)
    attend_rows(rows_ref, 2 * rows, keys_ref, ones_ref, both_ref, 0)
    up_ref[...] = both_ref[:rows, :]
    low_ref[...] = both_ref[rows:, :]


def head_kernel(seg, plan_ref, q_ref, kv_ref, out_ref, keys_ref, ones_ref, rows_ref):
    load_image(kv_ref, keys_ref, ones_ref)
    rows_ref[...] = segment_rows(q_ref, plan_ref, seg, 0, out_ref.shape[0])
    attend_rows(rows_ref, out_ref.shape[0], keys_ref, ones_ref, out_ref, 0)


def tails_kernel(plan_ref, q_ref, kv0_ref, kv1_ref, kv2_ref, kv3_ref, out_ref, tails_ref, keys_ref, ones_ref,
                 rows_ref):
    count = q_ref.shape[0] // QLEN
    width = tails_ref.shape[0]
    half = width // NEED
    seg = pl.program_id(0)
    live = plan_ref[3 * count + seg] - half

    @pl.when(seg == 0)
    def _():
        tails_ref[...] = jnp.zeros(tails_ref.shape, tails_ref.dtype)

    for g, kv_ref in enumerate((kv0_ref, kv1_ref, kv2_ref, kv3_ref)):
        @pl.when((seg == g) & (live > 0))
        def _():
            load_image(kv_ref, keys_ref, ones_ref)

    @pl.when(live > 0)
    def _():
        rows_ref[...] = segment_rows(q_ref, plan_ref, seg, half, half)

    for low, high in ((0, half // 4), (half // 4, half // 2), (half // 2, half)):
        @pl.when((live > low) & (live <= high))
        def _():
            attend_rows(rows_ref, high, keys_ref, ones_ref, tails_ref, pl.multiple_of(seg * half, half))

    @pl.when(seg == NEED - 1)
    def _():
        lane = lax.broadcasted_iota(jnp.int32, (1, width), 1)
        target = jnp.full((1, width), -1, jnp.int32)
        for g in range(NEED):
            inner = lane - g * half
            here = (inner >= 0) & (inner < plan_ref[3 * count + g] - half)
            target = jnp.where(here, plan_ref[3 * count + NEED + g] + inner, target)

        def pack(n, carry):
            low = pl.multiple_of(n * half, half)
            row = lax.broadcasted_iota(jnp.int32, (half, width), 0) + low
            pick = jnp.where(row == target, 1.0, 0.0).astype(BF16)
            out_ref[pl.ds(low, half), :] = jnp.dot(pick, tails_ref[...], preferred_element_type=F32).astype(BF16)
            return carry

        lax.fori_loop(0, out_ref.shape[0] // half, pack, 0)


def columns(info_ref, line):
    me = info_ref[0]
    upper = me >= line // 2
    pair = jnp.where(upper, 5 - me, 1 - me)
    return me, pair, jnp.where(upper, 1, 2), jnp.where(upper, 0, 3)


def from_afar(info_ref, line, middle_ref, ends_ref, k):
    me = info_ref[0]
    rows = middle_ref.shape[0] // 2
    part = pl.ds(k * rows, rows)
    return jnp.where((me == 0) | (me == line - 1), ends_ref[part, :], middle_ref[part, :])


def project_kernel(info_ref, *refs):
    *chunks, w_ref, out_ref = refs
    depth = chunks[0].shape[1]
    line = w_ref.shape[0] // depth
    total = None
    for k, at in enumerate(columns(info_ref, line)):
        if k < 2:
            pieces = [c[...] for c in chunks[k::4]]
        else:
            pieces = [from_afar(info_ref, line, m, e, k - 2) for m, e in zip(chunks[2::4], chunks[3::4])]
        x = pieces[0] if len(pieces) == 1 else jnp.concatenate(pieces, axis=0)
        w = w_ref[pl.ds(pl.multiple_of(at * depth, depth), depth), :]
        y = jnp.dot(x, w, preferred_element_type=F32)
        total = y if total is None else total + y
    out_ref[...] = total.astype(out_ref.dtype)


def pick_rows(plan_ref, pick_ref, segs, tails):
    rows, width = pick_ref.shape
    count = rows // QLEN
    per = count // NEED
    half = per * QLEN // 2
    sub = lax.broadcasted_iota(jnp.int32, (QLEN, 1), 0)
    lane = lax.broadcasted_iota(jnp.int32, (QLEN, width), 1)
    first = segs[0] if segs else 0

    def step(p, carry):
        seg = p // per
        at = plan_ref[count + p] + sub
        head = jnp.where((seg >= first) & (seg < first + len(segs)), at + (seg - first) * half, -1)
        tail = at + (len(segs) - 1) * half + plan_ref[3 * count + NEED + seg] if tails else jnp.full_like(at, -1)
        at = jnp.where(at < half, head, tail)
        at = jnp.where(sub < plan_ref[2 * count + p], at, -1)
        block = pl.ds(pl.multiple_of(plan_ref[p] * QLEN, QLEN), QLEN)
        pick_ref[block, :] = jnp.where(lane == at, 1.0, 0.0).astype(BF16)
        return carry

    lax.fori_loop(0, count, step, 0, unroll=2)


def over_rows(out_ref, body):
    tall = out_ref.shape[0] // 2

    def step(n, carry):
        rows = pl.ds(pl.multiple_of(n * tall, tall), tall)
        out_ref[rows, :] = body(rows).astype(out_ref.dtype)
        return carry

    lax.fori_loop(0, 2, step, 0)


def place_kernel(segs, plan_ref, *refs):
    *compact, out_ref, pick_ref = refs

    @pl.when(pl.program_id(0) == 0)
    def _():
        pick_rows(plan_ref, pick_ref, segs, False)

    y = jnp.concatenate([c[...] for c in compact], axis=0)
    over_rows(out_ref, lambda rows: jnp.dot(pick_ref[rows, :], y, preferred_element_type=F32))


def begin_kernel(segs, info_ref, plan_ref, own3_ref, other3_ref, own_ref, other_ref, w_ref, out_ref, pick_ref):
    @pl.when(pl.program_id(0) == 0)
    def _():
        pick_rows(plan_ref, pick_ref, segs, True)

    depth = own_ref.shape[1]
    upper = info_ref[0] % 2
    total = None
    for x_refs, at in (((own3_ref, own_ref), upper), ((other3_ref, other_ref), 1 - upper)):
        x = jnp.concatenate([r[...] for r in x_refs], axis=0)
        w = w_ref[pl.ds(pl.multiple_of(at * depth, depth), depth), :]
        y = jnp.dot(x, w, preferred_element_type=F32)
        total = y if total is None else total + y
    out_ref[...] = total


def finish_kernel(info_ref, middle3_ref, ends3_ref, middle_ref, ends_ref, pick_ref, begun_ref, placed_ref, w_ref,
                  out_ref, x_ref):
    depth = middle_ref.shape[1]
    line = 2 * (w_ref.shape[0] // depth)
    places = columns(info_ref, line)[2:]

    @pl.when(pl.program_id(0) == 0)
    def _():
        low = middle3_ref.shape[0] // 2
        for k in range(2):
            x_ref[k, :low, :] = from_afar(info_ref, line, middle3_ref, ends3_ref, k)
            x_ref[k, low:, :] = from_afar(info_ref, line, middle_ref, ends_ref, k)

    y = begun_ref[...]
    for k, at in enumerate(places):
        w = w_ref[pl.ds(pl.multiple_of(at % 2 * depth, depth), depth), :]
        y = y + jnp.dot(x_ref[k], w, preferred_element_type=F32)
    y = y.astype(BF16)

    def body(rows):
        return placed_ref[rows, :].astype(F32) + jnp.dot(pick_ref[rows, :], y, preferred_element_type=F32)

    over_rows(out_ref, body)


SMEM = pl.BlockSpec(memory_space=pltpu.SMEM)
VMEM = pl.BlockSpec(memory_space=pltpu.VMEM)


def on_device_line(queries, kv_cache, question_slot, question_len, out_weight):
    row_count, col_count = queries.shape
    count = row_count // QLEN
    seg_rows = row_count // NEED
    half = seg_rows // 2
    image = kv_cache[0]
    tokens, dim = image.shape[0], image.shape[1] // 2
    heads = col_count // dim
    out_cols = out_weight.shape[1]
    line = lax.axis_size("tensor")
    ring = lax.axis_size("serve")
    info = lax.axis_index("tensor").astype(jnp.int32).reshape(1)

    kv_one = lax.ppermute(image, "serve", [(i, (i + 1) % ring) for i in range(ring)])

    params = pltpu.CompilerParams(vmem_limit_bytes=40 * MIB)
    plan_size = 3 * count + 2 * NEED + 8

    def cost(micros):
        return pl.CostEstimate(flops=int(micros * 0.3e9), bytes_accessed=image.size, transcendentals=0)

    scratch = [
        pltpu.VMEM((dim, tokens), BF16),
        pltpu.VMEM((tokens, 2 * dim), BF16),
        pltpu.VMEM((half, col_count), BF16),
    ]
    plan, head_up, head_low = pl.pallas_call(
        first_kernel,
        out_shape=(
            jax.ShapeDtypeStruct((plan_size,), jnp.int32),
            jax.ShapeDtypeStruct((half // 2, col_count), BF16),
            jax.ShapeDtypeStruct((half // 2, col_count), BF16),
        ),
        in_specs=[SMEM, SMEM, VMEM, VMEM],
        out_specs=(SMEM, VMEM, VMEM),
        scratch_shapes=[pltpu.SMEM((2 * NEED,), jnp.int32)] + scratch + [pltpu.VMEM((half, col_count), BF16)],
        compiler_params=params,
        cost_estimate=cost(5),
        name="first_head",
    )(question_slot, question_len, queries, image)

    def resident(*arrays):
        return [pl.BlockSpec(a.shape, lambda n: (0, 0)) for a in arrays]

    def head(seg, key_value):
        return pl.pallas_call(
            functools.partial(head_kernel, seg),
            out_shape=jax.ShapeDtypeStruct((half, col_count), BF16),
            in_specs=[SMEM, VMEM, VMEM],
            out_specs=VMEM,
            scratch_shapes=scratch,
            compiler_params=params,
            cost_estimate=cost(3),
            name="head",
        )(plan, queries, key_value)

    def tails(rows, *key_values):
        return pl.pallas_call(
            tails_kernel,
            out_shape=jax.ShapeDtypeStruct((rows, col_count), BF16),
            grid=(NEED,),
            in_specs=[SMEM] + resident(queries, *key_values),
            out_specs=pl.BlockSpec((rows, col_count), lambda n: (0, 0)),
            scratch_shapes=[pltpu.VMEM((NEED * half, col_count), BF16)] + scratch,
            compiler_params=params,
            cost_estimate=cost(8),
            name="tails",
        )(plan, queries, *key_values)

    def paired(chunk):
        return chunk, lax.ppermute(chunk, "tensor", [(i, i ^ 1) for i in range(line)])

    def crossed(chunk):
        both = jnp.concatenate(chunk, axis=0)
        return *chunk, lax.ppermute(both, "tensor", [(1, 2), (2, 1)])

    def ended(chunk):
        return *chunk, lax.ppermute(chunk[2], "tensor", [(1, 0), (2, 3)])

    tile = min(512, out_cols)
    steps = (out_cols // tile,)
    w_spec = pl.BlockSpec((out_weight.shape[0], tile), lambda n: (0, n))

    def tiled(rows):
        return pl.BlockSpec((rows, tile), lambda n: (0, n))

    def project(*chunks):
        arrays = [a for c in chunks for a in c]
        rows = sum(c[0].shape[0] for c in chunks)
        return pl.pallas_call(
            project_kernel,
            out_shape=jax.ShapeDtypeStruct((rows, out_cols), BF16),
            grid=steps,
            in_specs=[SMEM] + resident(*arrays) + [w_spec],
            out_specs=tiled(rows),
            compiler_params=params,
            cost_estimate=cost(10),
            name="project",
        )(info, *arrays, out_weight)

    def half_weight(far, tile):
        def index(n, info_ref):
            upper = info_ref[0] // (line // 2)
            return 1 - upper if far else upper, n

        return pl.BlockSpec((out_weight.shape[0] // 2, tile), index)

    def with_info(tile, in_specs, out_specs, scratch_shapes=()):
        return pltpu.PrefetchScalarGridSpec(
            num_scalar_prefetch=1, grid=(out_cols // tile,), in_specs=in_specs, out_specs=out_specs, scratch_shapes=scratch_shapes)

    def fixed(*arrays):
        return [pl.BlockSpec(a.shape, lambda n, info_ref: (0, 0)) for a in arrays]

    def strip(rows, tile):
        return pl.BlockSpec((rows, tile), lambda n, info_ref: (0, n))

    def place(segs, *compact):
        return pl.pallas_call(
            functools.partial(place_kernel, segs),
            out_shape=jax.ShapeDtypeStruct((row_count, out_cols), BF16),
            grid=steps,
            in_specs=[SMEM] + [tiled(c.shape[0]) for c in compact],
            out_specs=tiled(row_count),
            scratch_shapes=[pltpu.VMEM((row_count, sum(c.shape[0] for c in compact)), BF16)],
            compiler_params=params,
            cost_estimate=cost(5),
            name="place",
        )(plan, *compact)

    def begin(segs, own3, other3, own, other):
        rows = own3.shape[0] + own.shape[0]
        width = len(segs) * half + own.shape[0]
        return pl.pallas_call(
            functools.partial(begin_kernel, segs),
            out_shape=(
                jax.ShapeDtypeStruct((rows, out_cols), F32),
                jax.ShapeDtypeStruct((row_count, width), BF16),
            ),
            grid_spec=with_info(
                tile,
                [SMEM] + fixed(own3, other3, own, other) + [half_weight(False, tile)],
                (strip(rows, tile), pl.BlockSpec((row_count, width), lambda n, info_ref: (0, 0))),
            ),
            compiler_params=params,
            cost_estimate=cost(5),
            name="begin",
        )(info, plan, own3, other3, own, other, out_weight)

    def finish(middle3, ends3, middle, ends, pick, begun, placed):
        rows = begun.shape[0]
        return pl.pallas_call(
            finish_kernel,
            out_shape=jax.ShapeDtypeStruct((row_count, out_cols), BF16),
            grid_spec=with_info(
                tile,
                fixed(middle3, ends3, middle, ends, pick)
                + [strip(rows, tile), strip(row_count, tile), half_weight(True, tile)],
                strip(row_count, tile),
                [pltpu.VMEM((2, rows, col_count), BF16)],
            ),
            compiler_params=params,
            cost_estimate=cost(7),
            name="finish",
        )(info, middle3, ends3, middle, ends, pick, begun, placed, out_weight)

    def after(value, other):
        return lax.optimization_barrier((value, other))[0]

    up, low = paired(head_up), paired(head_low)
    kv_one, up = lax.optimization_barrier((kv_one, up))
    kv_two = lax.ppermute(after(image, kv_one), "serve", [(i, (i + 2) % ring) for i in range(ring)])
    up, low = ended(crossed(up)), crossed(low)
    chunk1 = paired(head(1, kv_one))
    kv_two = after(kv_two, (chunk1[1], up[3], low[2]))
    odd = lax.axis_index("serve") % 2 == 1
    kv_three = lax.ppermute(
        jnp.where(odd, image, kv_two), "serve",
        [(i, i + 1) if i % 2 == 0 else (i, (i + 3) % ring) for i in range(ring)])
    low = ended(low)
    chunk1 = crossed((chunk1[0], after(chunk1[1], up[3])))
    chunk2 = paired(head(2, kv_two))
    head3 = head(3, kv_three)
    chunk1 = ended((*chunk1[:2], after(chunk1[2], head3)))
    chunk2 = crossed((chunk2[0], after(chunk2[1], (low[3], head3))))
    chunk3 = crossed(paired(head3))
    rest = tails(NEED * half, image, kv_one, kv_two, after(kv_three, chunk3[1]))
    early = half * 15 // 8
    rest_pair = paired(rest[:early])
    chunk2 = ended((*chunk2[:2], after(chunk2[2], rest)))
    live_rest = plan[3 * count + 2 * NEED]
    sizes = [int(half * k) // 4 for k in (5, 6.25, 7.5, 9, 16)]

    def branch(size, rest, rest_pair, up, low, chunk1, chunk2, chunk3):
        own, other = rest_pair
        if size > early:
            own, other = [
                jnp.concatenate(pieces, axis=0) for pieces in zip(rest_pair, paired(rest[early:size]))]
        own, other, middle = crossed((own[:size], other[:size]))
        own3, other3, middle3, ends3 = ended(chunk3)
        done = project(up, low, chunk1, chunk2)
        middle = after(middle, (ends3, done))
        own, other, middle, ends = ended((own, other, middle))
        begun, pick = begin((3,), own3, other3, own, other)
        return finish(middle3, ends3, middle, ends, pick, begun, place((0, 1, 2), done))

    index = sum([(live_rest > s).astype(jnp.int32) for s in sizes[:-1]])
    branches = [functools.partial(branch, s) for s in sizes]
    return lax.switch(index, branches, rest, rest_pair, up, low, chunk1, chunk2, chunk3)


def solution(mesh):
    plain = mesh.shape["tensor"] == KVH == 4 and mesh.shape["serve"] % 2 == 0 and NEED == 4
    return jax.shard_map(
        on_device_line if plain else on_device_general,
        mesh=mesh,
        in_specs=(
            P("serve", "tensor"),
            P("serve", "tensor", None),
            P("serve"),
            P("serve"),
            P(None, "tensor"),
        ),
        out_specs=P("serve", "tensor"),
        check_vma=False,
    )
```

```python
import functools

import jax
import jax.numpy as jnp
from jax import lax
from jax.experimental import pallas as pl
from jax.experimental.pallas import tpu as pltpu
from jax.sharding import PartitionSpec as P

KVH = 4
P_SIZE = 1600
QLEN = 32
NEED = 4
LOG2E = 1.4426950408889634
MIB = 1 << 20
F32 = jnp.float32
BF16 = jnp.bfloat16


def swapped(shard, axis, bit):
    return lax.ppermute(shard, axis, [(i, i ^ 1 << bit) for i in range(lax.axis_size(axis))])


def shifted(value, axis, steps):
    count = lax.axis_size(axis)
    pairs = [(source, (source + steps) % count) for source in range(count)]
    return lax.ppermute(value, axis, pairs)


def attend(query_rows, key_value):
    row_count = query_rows.shape[0]
    head_count = key_value.shape[0]
    head_dim = key_value.shape[2] // 2
    grouped = query_rows.reshape(row_count, head_count, -1, head_dim)
    key_part = key_value[:, :, :head_dim]
    value_part = key_value[:, :, head_dim:]
    scores = jnp.einsum(
        "rkgd,kpd->kgrp", grouped, key_part, preferred_element_type=jnp.float32
    ) * head_dim ** (-0.5)
    row_max = jnp.max(scores, axis=3, keepdims=True)
    exp_scores = jnp.exp(scores - row_max)
    sum_exp = jnp.sum(exp_scores, axis=3, keepdims=True)
    weights = (exp_scores / sum_exp).astype(jnp.bfloat16)
    blended = jnp.einsum("kgrp,kpd->rkgd", weights, value_part, preferred_element_type=jnp.float32)
    return blended.reshape(row_count, -1)


def on_device_general(queries, kv_cache, question_slot, question_len, out_weight):
    row_count, col_count = queries.shape
    head_dim = kv_cache.shape[2] // 2
    question_count = row_count // QLEN
    per_slot = question_count // NEED
    head_piece = kv_cache[0]
    sharing = lax.axis_size("tensor") // KVH
    if sharing > 1:
        for bit_number in range(sharing.bit_length() - 1):
            partner_piece = swapped(head_piece, "tensor", bit_number)
            upper_member = lax.axis_index("tensor") // 2**bit_number % 2 == 1
            head_piece = jnp.where(
                upper_member,
                jnp.concatenate([partner_piece, head_piece], axis=0),
                jnp.concatenate([head_piece, partner_piece], axis=0),
            )
    key_value = head_piece.reshape(-1, P_SIZE, 2 * head_dim)
    ordering = jnp.argsort(question_slot, stable=True)
    inverse_order = jnp.argsort(ordering, stable=True)
    sorted_rows = queries.reshape(question_count, QLEN, col_count)[ordering]
    sorted_rows = sorted_rows.reshape(NEED, per_slot * QLEN, col_count)
    results = []
    for offset_back in range(NEED):
        if offset_back == 0:
            remote = key_value
        else:
            remote = shifted(key_value, "serve", offset_back)
        results.append(attend(sorted_rows[offset_back], remote))
    sorted_out = jnp.stack(results).reshape(question_count, QLEN, col_count)
    blended = sorted_out[inverse_order].reshape(row_count, col_count)
    token_pos = jnp.arange(row_count, dtype=jnp.int32) % QLEN
    live_rows = token_pos < jnp.repeat(question_len, QLEN, total_repeat_length=row_count)
    attended = jnp.where(live_rows[:, None], blended, 0.0).astype(jnp.bfloat16)
    zero_sum = jnp.zeros((row_count, out_weight.shape[1]), jnp.float32)
    gathered_cols = lax.all_gather(attended, "tensor", axis=1, tiled=True)
    weight_rows = lax.slice_in_dim(out_weight, 0, gathered_cols.shape[1], axis=0)
    answers = zero_sum + jnp.dot(gathered_cols, weight_rows, preferred_element_type=jnp.float32)
    return answers.astype(jnp.bfloat16)


def make_plan(info_ref, slot_ref, len_ref, plan_ref, work_ref):
    count = slot_ref.shape[0]
    per = count // NEED
    half = per * QLEN // 2
    odd = info_ref[1]
    for g in range(NEED):
        work_ref[g] = g * per
        work_ref[NEED + g] = 0

    def step(q, carry):
        slot = slot_ref[q]
        length = len_ref[q]
        last = jnp.where(slot == 1, 3 - odd, 2 + odd)
        seg = jnp.where(slot == 0, 0, jnp.where(slot == 2, 1, last))
        at = work_ref[seg]
        first = work_ref[NEED + seg]
        plan_ref[at] = q
        plan_ref[count + at] = first
        plan_ref[2 * count + at] = length
        work_ref[seg] = at + 1
        work_ref[NEED + seg] = first + length
        return carry

    lax.fori_loop(0, count, step, 0)
    begin = jnp.int32(0)
    for g in range(NEED):
        live = work_ref[NEED + g]
        plan_ref[3 * count + g] = live
        plan_ref[3 * count + NEED + g] = begin
        begin = begin + jnp.maximum(live - half, 0)
    plan_ref[3 * count + 2 * NEED] = begin


def segment_rows(q_ref, plan_ref, seg, low, rows):
    count = q_ref.shape[0] // QLEN
    per = count // NEED
    width = per * QLEN
    lane = lax.broadcasted_iota(jnp.int32, (1, width), 1)
    owner = lane // QLEN
    inner = lane % QLEN
    first = jnp.zeros((1, width), jnp.int32)
    length = jnp.zeros((1, width), jnp.int32)
    blocks = []
    for k in range(per):
        q = plan_ref[seg * per + k]
        blocks.append(q_ref[pl.ds(pl.multiple_of(q * QLEN, QLEN), QLEN), :])
        first = jnp.where(owner == k, plan_ref[count + seg * per + k], first)
        length = jnp.where(owner == k, plan_ref[2 * count + seg * per + k], length)
    target = jnp.where(inner < length, first + inner, -1)
    row = lax.broadcasted_iota(jnp.int32, (rows, width), 0) + low
    pick = jnp.where(row == target, 1.0, 0.0).astype(BF16)
    return jnp.dot(pick, jnp.concatenate(blocks, axis=0), preferred_element_type=F32).astype(BF16)


def load_image(kv_ref, keys_ref, ones_ref):
    dim = kv_ref.shape[1] // 2
    keys_ref[...] = kv_ref[:, :dim].T
    ones_ref[:, :dim] = kv_ref[:, dim:]
    ones_ref[:, dim:] = jnp.ones((kv_ref.shape[0], dim), BF16)


def attend_rows(rows_ref, rows, keys_ref, ones_ref, out_ref, base):
    dim = keys_ref.shape[0]
    heads = rows_ref.shape[1] // dim
    group = max(1, min(heads, 256 // rows))

    def step(n, carry):
        places = [pl.ds(pl.multiple_of((n * group + i) * dim, dim), dim) for i in range(group)]
        q = [rows_ref[:rows, cols] for cols in places]
        q = q[0] if len(q) == 1 else jnp.concatenate(q, axis=0)
        s = jnp.dot(q, keys_ref[...], preferred_element_type=F32)
        top = jnp.max(s, axis=1, keepdims=True)
        e = jnp.exp2((s - top) * (LOG2E * dim ** (-0.5))).astype(BF16)
        o = jnp.dot(e, ones_ref[...], preferred_element_type=F32)
        o = (o[:, :dim] / o[:, dim:]).astype(BF16)
        for i, cols in enumerate(places):
            out_ref[pl.ds(base, rows), cols] = o[i * rows:(i + 1) * rows, :]
        return carry

    steps = heads // group
    lax.fori_loop(0, steps, step, 0, unroll=min(steps, 2))


def first_kernel(info_ref, slot_ref, len_ref, q_ref, kv_ref, plan_ref, up_ref, low_ref, work_ref, keys_ref, ones_ref,
                 rows_ref, both_ref):
    make_plan(info_ref, slot_ref, len_ref, plan_ref, work_ref)
    load_image(kv_ref, keys_ref, ones_ref)
    rows = up_ref.shape[0]
    rows_ref[...] = segment_rows(q_ref, plan_ref, 0, 0, 2 * rows)
    attend_rows(rows_ref, 2 * rows, keys_ref, ones_ref, both_ref, 0)
    up_ref[...] = both_ref[:rows, :]
    low_ref[...] = both_ref[rows:, :]


def head_kernel(seg, plan_ref, q_ref, kv_ref, out_ref, keys_ref, ones_ref, rows_ref):
    load_image(kv_ref, keys_ref, ones_ref)
    rows_ref[...] = segment_rows(q_ref, plan_ref, seg, 0, out_ref.shape[0])
    attend_rows(rows_ref, out_ref.shape[0], keys_ref, ones_ref, out_ref, 0)


def tails_kernel(plan_ref, q_ref, kv0_ref, kv1_ref, kv2_ref, kv3_ref, out_ref, tails_ref, keys_ref, ones_ref,
                 rows_ref):
    count = q_ref.shape[0] // QLEN
    width = tails_ref.shape[0]
    half = width // NEED
    seg = pl.program_id(0)
    live = plan_ref[3 * count + seg] - half

    @pl.when(seg == 0)
    def _():
        tails_ref[...] = jnp.zeros(tails_ref.shape, tails_ref.dtype)

    for g, kv_ref in enumerate((kv0_ref, kv1_ref, kv2_ref, kv3_ref)):
        @pl.when((seg == g) & (live > 0))
        def _():
            load_image(kv_ref, keys_ref, ones_ref)

    @pl.when(live > 0)
    def _():
        rows_ref[...] = segment_rows(q_ref, plan_ref, seg, half, half)

    for low, high in ((0, half // 4), (half // 4, half // 2), (half // 2, half)):
        @pl.when((live > low) & (live <= high))
        def _():
            attend_rows(rows_ref, high, keys_ref, ones_ref, tails_ref, pl.multiple_of(seg * half, half))

    @pl.when(seg == NEED - 1)
    def _():
        lane = lax.broadcasted_iota(jnp.int32, (1, width), 1)
        target = jnp.full((1, width), -1, jnp.int32)
        for g in range(NEED):
            inner = lane - g * half
            here = (inner >= 0) & (inner < plan_ref[3 * count + g] - half)
            target = jnp.where(here, plan_ref[3 * count + NEED + g] + inner, target)

        def pack(n, carry):
            low = pl.multiple_of(n * half, half)
            row = lax.broadcasted_iota(jnp.int32, (half, width), 0) + low
            pick = jnp.where(row == target, 1.0, 0.0).astype(BF16)
            out_ref[pl.ds(low, half), :] = jnp.dot(pick, tails_ref[...], preferred_element_type=F32).astype(BF16)
            return carry

        lax.fori_loop(0, out_ref.shape[0] // half, pack, 0)


def columns(info_ref, line):
    me = info_ref[0]
    upper = me >= line // 2
    pair = jnp.where(upper, 5 - me, 1 - me)
    return me, pair, jnp.where(upper, 1, 2), jnp.where(upper, 0, 3)


def from_afar(info_ref, line, middle_ref, ends_ref, k):
    me = info_ref[0]
    rows = middle_ref.shape[0] // 2
    part = pl.ds(k * rows, rows)
    return jnp.where((me == 0) | (me == line - 1), ends_ref[part, :], middle_ref[part, :])


def project_kernel(info_ref, *refs):
    *chunks, w_ref, out_ref = refs
    depth = chunks[0].shape[1]
    line = w_ref.shape[0] // depth
    total = None
    for k, at in enumerate(columns(info_ref, line)):
        if k < 2:
            pieces = [c[...] for c in chunks[k::4]]
        else:
            pieces = [from_afar(info_ref, line, m, e, k - 2) for m, e in zip(chunks[2::4], chunks[3::4])]
        x = pieces[0] if len(pieces) == 1 else jnp.concatenate(pieces, axis=0)
        w = w_ref[pl.ds(pl.multiple_of(at * depth, depth), depth), :]
        y = jnp.dot(x, w, preferred_element_type=F32)
        total = y if total is None else total + y
    out_ref[...] = total.astype(out_ref.dtype)


def pick_rows(plan_ref, pick_ref, segs, tails):
    rows, width = pick_ref.shape
    count = rows // QLEN
    per = count // NEED
    half = per * QLEN // 2
    sub = lax.broadcasted_iota(jnp.int32, (QLEN, 1), 0)
    lane = lax.broadcasted_iota(jnp.int32, (QLEN, width), 1)
    first = segs[0] if segs else 0

    def step(p, carry):
        seg = p // per
        at = plan_ref[count + p] + sub
        head = jnp.where((seg >= first) & (seg < first + len(segs)), at + (seg - first) * half, -1)
        tail = at + (len(segs) - 1) * half + plan_ref[3 * count + NEED + seg] if tails else jnp.full_like(at, -1)
        at = jnp.where(at < half, head, tail)
        at = jnp.where(sub < plan_ref[2 * count + p], at, -1)
        block = pl.ds(pl.multiple_of(plan_ref[p] * QLEN, QLEN), QLEN)
        pick_ref[block, :] = jnp.where(lane == at, 1.0, 0.0).astype(BF16)
        return carry

    lax.fori_loop(0, count, step, 0, unroll=2)


def over_rows(out_ref, body):
    tall = out_ref.shape[0] // 2

    def step(n, carry):
        rows = pl.ds(pl.multiple_of(n * tall, tall), tall)
        out_ref[rows, :] = body(rows).astype(out_ref.dtype)
        return carry

    lax.fori_loop(0, 2, step, 0)


def place_kernel(segs, plan_ref, *refs):
    *compact, out_ref, pick_ref = refs

    @pl.when(pl.program_id(0) == 0)
    def _():
        pick_rows(plan_ref, pick_ref, segs, False)

    y = jnp.concatenate([c[...] for c in compact], axis=0)
    over_rows(out_ref, lambda rows: jnp.dot(pick_ref[rows, :], y, preferred_element_type=F32))


def begin_kernel(segs, info_ref, plan_ref, own3_ref, other3_ref, own_ref, other_ref, w_ref, out_ref, pick_ref):
    @pl.when(pl.program_id(0) == 0)
    def _():
        pick_rows(plan_ref, pick_ref, segs, True)

    depth = own_ref.shape[1]
    upper = info_ref[0] % 2
    total = None
    for x_refs, at in (((own3_ref, own_ref), upper), ((other3_ref, other_ref), 1 - upper)):
        x = jnp.concatenate([r[...] for r in x_refs], axis=0)
        w = w_ref[pl.ds(pl.multiple_of(at * depth, depth), depth), :]
        y = jnp.dot(x, w, preferred_element_type=F32)
        total = y if total is None else total + y
    out_ref[...] = total


def finish_kernel(info_ref, middle3_ref, ends3_ref, middle_ref, ends_ref, pick_ref, begun_ref, placed_ref, w_ref,
                  out_ref, x_ref):
    depth = middle_ref.shape[1]
    line = 2 * (w_ref.shape[0] // depth)
    places = columns(info_ref, line)[2:]

    @pl.when(pl.program_id(0) == 0)
    def _():
        low = middle3_ref.shape[0] // 2
        for k in range(2):
            x_ref[k, :low, :] = from_afar(info_ref, line, middle3_ref, ends3_ref, k)
            x_ref[k, low:, :] = from_afar(info_ref, line, middle_ref, ends_ref, k)

    y = begun_ref[...]
    for k, at in enumerate(places):
        w = w_ref[pl.ds(pl.multiple_of(at % 2 * depth, depth), depth), :]
        y = y + jnp.dot(x_ref[k], w, preferred_element_type=F32)
    y = y.astype(BF16)

    def body(rows):
        return placed_ref[rows, :].astype(F32) + jnp.dot(pick_ref[rows, :], y, preferred_element_type=F32)

    over_rows(out_ref, body)


SMEM = pl.BlockSpec(memory_space=pltpu.SMEM)
VMEM = pl.BlockSpec(memory_space=pltpu.VMEM)


def on_device_line(queries, kv_cache, question_slot, question_len, out_weight):
    row_count, col_count = queries.shape
    count = row_count // QLEN
    seg_rows = row_count // NEED
    half = seg_rows // 2
    image = kv_cache[0]
    tokens, dim = image.shape[0], image.shape[1] // 2
    heads = col_count // dim
    out_cols = out_weight.shape[1]
    line = lax.axis_size("tensor")
    ring = lax.axis_size("serve")
    info = jnp.stack([lax.axis_index("tensor"), lax.axis_index("serve") % 2]).astype(jnp.int32)

    kv_two = lax.ppermute(image, "serve", [(i, (i + 2) % ring) for i in range(ring)])
    kv_mix = lax.ppermute(image, "serve", [(i, i + 1) if i % 2 == 0 else (i, (i + 3) % ring) for i in range(ring)])
    params = pltpu.CompilerParams(vmem_limit_bytes=40 * MIB)
    plan_size = 3 * count + 2 * NEED + 8

    def cost(micros):
        return pl.CostEstimate(flops=int(micros * 0.3e9), bytes_accessed=image.size, transcendentals=0)

    scratch = [
        pltpu.VMEM((dim, tokens), BF16),
        pltpu.VMEM((tokens, 2 * dim), BF16),
        pltpu.VMEM((half, col_count), BF16),
    ]
    plan, head_up, head_low = pl.pallas_call(
        first_kernel,
        out_shape=(
            jax.ShapeDtypeStruct((plan_size,), jnp.int32),
            jax.ShapeDtypeStruct((half // 2, col_count), BF16),
            jax.ShapeDtypeStruct((half // 2, col_count), BF16),
        ),
        in_specs=[SMEM, SMEM, SMEM, VMEM, VMEM],
        out_specs=(SMEM, VMEM, VMEM),
        scratch_shapes=[pltpu.SMEM((2 * NEED,), jnp.int32)] + scratch + [pltpu.VMEM((half, col_count), BF16)],
        compiler_params=params,
        cost_estimate=cost(5),
        name="first_head",
    )(info, question_slot, question_len, queries, image)

    def resident(*arrays):
        return [pl.BlockSpec(a.shape, lambda n: (0, 0)) for a in arrays]

    def head(seg, key_value):
        return pl.pallas_call(
            functools.partial(head_kernel, seg),
            out_shape=jax.ShapeDtypeStruct((half, col_count), BF16),
            in_specs=[SMEM, VMEM, VMEM],
            out_specs=VMEM,
            scratch_shapes=scratch,
            compiler_params=params,
            cost_estimate=cost(3),
            name="head",
        )(plan, queries, key_value)

    def tails(rows, *key_values):
        return pl.pallas_call(
            tails_kernel,
            out_shape=jax.ShapeDtypeStruct((rows, col_count), BF16),
            grid=(NEED,),
            in_specs=[SMEM] + resident(queries, *key_values),
            out_specs=pl.BlockSpec((rows, col_count), lambda n: (0, 0)),
            scratch_shapes=[pltpu.VMEM((NEED * half, col_count), BF16)] + scratch,
            compiler_params=params,
            cost_estimate=cost(8),
            name="tails",
        )(plan, queries, *key_values)

    def paired(chunk):
        return chunk, lax.ppermute(chunk, "tensor", [(i, i ^ 1) for i in range(line)])

    def crossed(chunk):
        both = jnp.concatenate(chunk, axis=0)
        return *chunk, lax.ppermute(both, "tensor", [(1, 2), (2, 1)])

    def ended(chunk):
        return *chunk, lax.ppermute(chunk[2], "tensor", [(1, 0), (2, 3)])

    tile = min(512, out_cols)
    steps = (out_cols // tile,)
    w_spec = pl.BlockSpec((out_weight.shape[0], tile), lambda n: (0, n))

    def tiled(rows):
        return pl.BlockSpec((rows, tile), lambda n: (0, n))

    def project(*chunks):
        arrays = [a for c in chunks for a in c]
        rows = sum(c[0].shape[0] for c in chunks)
        return pl.pallas_call(
            project_kernel,
            out_shape=jax.ShapeDtypeStruct((rows, out_cols), BF16),
            grid=steps,
            in_specs=[SMEM] + resident(*arrays) + [w_spec],
            out_specs=tiled(rows),
            compiler_params=params,
            cost_estimate=cost(10),
            name="project",
        )(info, *arrays, out_weight)

    def half_weight(far, tile):
        def index(n, info_ref):
            upper = info_ref[0] // (line // 2)
            return 1 - upper if far else upper, n

        return pl.BlockSpec((out_weight.shape[0] // 2, tile), index)

    def with_info(tile, in_specs, out_specs, scratch_shapes=()):
        return pltpu.PrefetchScalarGridSpec(
            num_scalar_prefetch=1, grid=(out_cols // tile,), in_specs=in_specs, out_specs=out_specs, scratch_shapes=scratch_shapes)

    def fixed(*arrays):
        return [pl.BlockSpec(a.shape, lambda n, info_ref: (0, 0)) for a in arrays]

    def strip(rows, tile):
        return pl.BlockSpec((rows, tile), lambda n, info_ref: (0, n))

    def place(segs, *compact):
        return pl.pallas_call(
            functools.partial(place_kernel, segs),
            out_shape=jax.ShapeDtypeStruct((row_count, out_cols), BF16),
            grid=steps,
            in_specs=[SMEM] + [tiled(c.shape[0]) for c in compact],
            out_specs=tiled(row_count),
            scratch_shapes=[pltpu.VMEM((row_count, sum(c.shape[0] for c in compact)), BF16)],
            compiler_params=params,
            cost_estimate=cost(5),
            name="place",
        )(plan, *compact)

    def begin(segs, own3, other3, own, other):
        rows = own3.shape[0] + own.shape[0]
        width = len(segs) * half + own.shape[0]
        return pl.pallas_call(
            functools.partial(begin_kernel, segs),
            out_shape=(
                jax.ShapeDtypeStruct((rows, out_cols), F32),
                jax.ShapeDtypeStruct((row_count, width), BF16),
            ),
            grid_spec=with_info(
                tile,
                [SMEM] + fixed(own3, other3, own, other) + [half_weight(False, tile)],
                (strip(rows, tile), pl.BlockSpec((row_count, width), lambda n, info_ref: (0, 0))),
            ),
            compiler_params=params,
            cost_estimate=cost(5),
            name="begin",
        )(info, plan, own3, other3, own, other, out_weight)

    def finish(middle3, ends3, middle, ends, pick, begun, placed):
        rows = begun.shape[0]
        return pl.pallas_call(
            finish_kernel,
            out_shape=jax.ShapeDtypeStruct((row_count, out_cols), BF16),
            grid_spec=with_info(
                tile,
                fixed(middle3, ends3, middle, ends, pick)
                + [strip(rows, tile), strip(row_count, tile), half_weight(True, tile)],
                strip(row_count, tile),
                [pltpu.VMEM((2, rows, col_count), BF16)],
            ),
            compiler_params=params,
            cost_estimate=cost(7),
            name="finish",
        )(info, middle3, ends3, middle, ends, pick, begun, placed, out_weight)

    def after(value, other):
        return lax.optimization_barrier((value, other))[0]

    up, low = crossed(paired(head_up)), paired(head_low)
    kv_two, low, _ = lax.optimization_barrier((kv_two, low, up[2]))
    kv_swap = lax.ppermute(kv_two, "serve", [(i, i ^ 1) for i in range(ring)])
    low = crossed(low)
    up = ended(up)
    chunk1 = paired(head(1, kv_two))
    kv_mix = after(kv_mix, (chunk1[1], low[2]))
    low = ended(low)
    chunk1 = crossed((chunk1[0], after(chunk1[1], up[3])))
    chunk2 = paired(head(2, kv_mix))
    head3 = head(3, kv_swap)
    chunk1 = ended((*chunk1[:2], after(chunk1[2], head3)))
    chunk2 = crossed((chunk2[0], after(chunk2[1], (low[3], head3))))
    chunk3 = crossed(paired(head3))
    rest = tails(NEED * half, image, kv_two, after(kv_mix, chunk3[1]), kv_swap)
    early = half * 15 // 8
    rest_pair = paired(rest[:early])
    chunk2 = ended((*chunk2[:2], after(chunk2[2], rest)))
    live_rest = plan[3 * count + 2 * NEED]
    sizes = [int(half * k) // 4 for k in (5, 6.5, 7.5, 9, 16)]

    def branch(size, rest, rest_pair, up, low, chunk1, chunk2, chunk3):
        own, other = rest_pair
        if size > early:
            own, other = [
                jnp.concatenate(pieces, axis=0) for pieces in zip(rest_pair, paired(rest[early:size]))]
        own, other, middle = crossed((own[:size], other[:size]))
        own3, other3, middle3, ends3 = ended(chunk3)
        done = project(up, low, chunk1, chunk2)
        middle = after(middle, (ends3, done))
        own, other, middle, ends = ended((own, other, middle))
        begun, pick = begin((3,), own3, other3, own, other)
        return finish(middle3, ends3, middle, ends, pick, begun, place((0, 1, 2), done))

    index = sum([(live_rest > s).astype(jnp.int32) for s in sizes[:-1]])
    branches = [functools.partial(branch, s) for s in sizes]
    return lax.switch(index, branches, rest, rest_pair, up, low, chunk1, chunk2, chunk3)


def solution(mesh):
    plain = mesh.shape["tensor"] == KVH == 4 and mesh.shape["serve"] % 2 == 0 and NEED == 4
    return jax.shard_map(
        on_device_line if plain else on_device_general,
        mesh=mesh,
        in_specs=(
            P("serve", "tensor"),
            P("serve", "tensor", None),
            P("serve"),
            P("serve"),
            P(None, "tensor"),
        ),
        out_specs=P("serve", "tensor"),
        check_vma=False,
    )
```

```python
import functools

import jax
import jax.numpy as jnp
from jax import lax
from jax.experimental import pallas as pl
from jax.experimental.pallas import tpu as pltpu
from jax.sharding import PartitionSpec as P

KVH = 4
P_SIZE = 1600
QLEN = 32
NEED = 4
LOG2E = 1.4426950408889634
MIB = 1 << 20
F32 = jnp.float32
BF16 = jnp.bfloat16


def swapped(shard, axis, bit):
    return lax.ppermute(shard, axis, [(i, i ^ 1 << bit) for i in range(lax.axis_size(axis))])


def shifted(value, axis, steps):
    count = lax.axis_size(axis)
    pairs = [(source, (source + steps) % count) for source in range(count)]
    return lax.ppermute(value, axis, pairs)


def attend(query_rows, key_value):
    row_count = query_rows.shape[0]
    head_count = key_value.shape[0]
    head_dim = key_value.shape[2] // 2
    grouped = query_rows.reshape(row_count, head_count, -1, head_dim)
    key_part = key_value[:, :, :head_dim]
    value_part = key_value[:, :, head_dim:]
    scores = jnp.einsum(
        "rkgd,kpd->kgrp", grouped, key_part, preferred_element_type=jnp.float32
    ) * head_dim ** (-0.5)
    row_max = jnp.max(scores, axis=3, keepdims=True)
    exp_scores = jnp.exp(scores - row_max)
    sum_exp = jnp.sum(exp_scores, axis=3, keepdims=True)
    weights = (exp_scores / sum_exp).astype(jnp.bfloat16)
    blended = jnp.einsum("kgrp,kpd->rkgd", weights, value_part, preferred_element_type=jnp.float32)
    return blended.reshape(row_count, -1)


def on_device_general(queries, kv_cache, question_slot, question_len, out_weight):
    row_count, col_count = queries.shape
    head_dim = kv_cache.shape[2] // 2
    question_count = row_count // QLEN
    per_slot = question_count // NEED
    head_piece = kv_cache[0]
    sharing = lax.axis_size("tensor") // KVH
    if sharing > 1:
        for bit_number in range(sharing.bit_length() - 1):
            partner_piece = swapped(head_piece, "tensor", bit_number)
            upper_member = lax.axis_index("tensor") // 2**bit_number % 2 == 1
            head_piece = jnp.where(
                upper_member,
                jnp.concatenate([partner_piece, head_piece], axis=0),
                jnp.concatenate([head_piece, partner_piece], axis=0),
            )
    key_value = head_piece.reshape(-1, P_SIZE, 2 * head_dim)
    ordering = jnp.argsort(question_slot, stable=True)
    inverse_order = jnp.argsort(ordering, stable=True)
    sorted_rows = queries.reshape(question_count, QLEN, col_count)[ordering]
    sorted_rows = sorted_rows.reshape(NEED, per_slot * QLEN, col_count)
    results = []
    for offset_back in range(NEED):
        if offset_back == 0:
            remote = key_value
        else:
            remote = shifted(key_value, "serve", offset_back)
        results.append(attend(sorted_rows[offset_back], remote))
    sorted_out = jnp.stack(results).reshape(question_count, QLEN, col_count)
    blended = sorted_out[inverse_order].reshape(row_count, col_count)
    token_pos = jnp.arange(row_count, dtype=jnp.int32) % QLEN
    live_rows = token_pos < jnp.repeat(question_len, QLEN, total_repeat_length=row_count)
    attended = jnp.where(live_rows[:, None], blended, 0.0).astype(jnp.bfloat16)
    zero_sum = jnp.zeros((row_count, out_weight.shape[1]), jnp.float32)
    gathered_cols = lax.all_gather(attended, "tensor", axis=1, tiled=True)
    weight_rows = lax.slice_in_dim(out_weight, 0, gathered_cols.shape[1], axis=0)
    answers = zero_sum + jnp.dot(gathered_cols, weight_rows, preferred_element_type=jnp.float32)
    return answers.astype(jnp.bfloat16)


def make_plan(info_ref, slot_ref, len_ref, plan_ref, work_ref):
    count = slot_ref.shape[0]
    per = count // NEED
    half = per * QLEN // 2
    odd = info_ref[1]
    for g in range(NEED):
        work_ref[g] = g * per
        work_ref[NEED + g] = 0

    def step(q, carry):
        slot = slot_ref[q]
        length = len_ref[q]
        last = jnp.where(slot == 1, 3 - odd, 2 + odd)
        seg = jnp.where(slot == 0, 0, jnp.where(slot == 2, 1, last))
        at = work_ref[seg]
        first = work_ref[NEED + seg]
        plan_ref[at] = q
        plan_ref[count + at] = first
        plan_ref[2 * count + at] = length
        work_ref[seg] = at + 1
        work_ref[NEED + seg] = first + length
        return carry

    lax.fori_loop(0, count, step, 0)
    begin = jnp.int32(0)
    for g in range(NEED):
        live = work_ref[NEED + g]
        plan_ref[3 * count + g] = live
        plan_ref[3 * count + NEED + g] = begin
        begin = begin + jnp.maximum(live - half, 0)
    plan_ref[3 * count + 2 * NEED] = begin


def segment_rows(q_ref, plan_ref, seg, low, rows):
    count = q_ref.shape[0] // QLEN
    per = count // NEED
    width = per * QLEN
    lane = lax.broadcasted_iota(jnp.int32, (1, width), 1)
    owner = lane // QLEN
    inner = lane % QLEN
    first = jnp.zeros((1, width), jnp.int32)
    length = jnp.zeros((1, width), jnp.int32)
    blocks = []
    for k in range(per):
        q = plan_ref[seg * per + k]
        blocks.append(q_ref[pl.ds(pl.multiple_of(q * QLEN, QLEN), QLEN), :])
        first = jnp.where(owner == k, plan_ref[count + seg * per + k], first)
        length = jnp.where(owner == k, plan_ref[2 * count + seg * per + k], length)
    target = jnp.where(inner < length, first + inner, -1)
    row = lax.broadcasted_iota(jnp.int32, (rows, width), 0) + low
    pick = jnp.where(row == target, 1.0, 0.0).astype(BF16)
    return jnp.dot(pick, jnp.concatenate(blocks, axis=0), preferred_element_type=F32).astype(BF16)


def load_image(kv_ref, keys_ref, ones_ref):
    dim = kv_ref.shape[1] // 2
    keys_ref[...] = kv_ref[:, :dim].T
    ones_ref[:, :dim] = kv_ref[:, dim:]
    ones_ref[:, dim:] = jnp.ones((kv_ref.shape[0], dim), BF16)


def attend_rows(rows_ref, rows, keys_ref, ones_ref, out_ref, base):
    dim = keys_ref.shape[0]
    heads = rows_ref.shape[1] // dim
    group = max(1, min(heads, 256 // rows))

    def step(n, carry):
        places = [pl.ds(pl.multiple_of((n * group + i) * dim, dim), dim) for i in range(group)]
        q = [rows_ref[:rows, cols] for cols in places]
        q = q[0] if len(q) == 1 else jnp.concatenate(q, axis=0)
        s = jnp.dot(q, keys_ref[...], preferred_element_type=F32)
        top = jnp.max(s, axis=1, keepdims=True)
        e = jnp.exp2((s - top) * (LOG2E * dim ** (-0.5))).astype(BF16)
        o = jnp.dot(e, ones_ref[...], preferred_element_type=F32)
        o = (o[:, :dim] / o[:, dim:]).astype(BF16)
        for i, cols in enumerate(places):
            out_ref[pl.ds(base, rows), cols] = o[i * rows:(i + 1) * rows, :]
        return carry

    steps = heads // group
    lax.fori_loop(0, steps, step, 0, unroll=min(steps, 2))


def first_kernel(info_ref, slot_ref, len_ref, q_ref, kv_ref, plan_ref, up_ref, low_ref, work_ref, keys_ref, ones_ref,
                 rows_ref, both_ref):
    make_plan(info_ref, slot_ref, len_ref, plan_ref, work_ref)
    load_image(kv_ref, keys_ref, ones_ref)
    rows = up_ref.shape[0]
    rows_ref[...] = segment_rows(q_ref, plan_ref, 0, 0, 2 * rows)
    attend_rows(rows_ref, 2 * rows, keys_ref, ones_ref, both_ref, 0)
    up_ref[...] = both_ref[:rows, :]
    low_ref[...] = both_ref[rows:, :]


def head_kernel(seg, plan_ref, q_ref, kv_ref, out_ref, keys_ref, ones_ref, rows_ref):
    load_image(kv_ref, keys_ref, ones_ref)
    rows_ref[...] = segment_rows(q_ref, plan_ref, seg, 0, out_ref.shape[0])
    attend_rows(rows_ref, out_ref.shape[0], keys_ref, ones_ref, out_ref, 0)


def tails_kernel(plan_ref, q_ref, kv0_ref, kv1_ref, kv2_ref, kv3_ref, out_ref, tails_ref, keys_ref, ones_ref,
                 rows_ref):
    count = q_ref.shape[0] // QLEN
    width = tails_ref.shape[0]
    half = width // NEED
    seg = pl.program_id(0)
    live = plan_ref[3 * count + seg] - half

    @pl.when(seg == 0)
    def _():
        tails_ref[...] = jnp.zeros(tails_ref.shape, tails_ref.dtype)

    for g, kv_ref in enumerate((kv0_ref, kv1_ref, kv2_ref, kv3_ref)):
        @pl.when((seg == g) & (live > 0))
        def _():
            load_image(kv_ref, keys_ref, ones_ref)

    @pl.when(live > 0)
    def _():
        rows_ref[...] = segment_rows(q_ref, plan_ref, seg, half, half)

    for low, high in ((0, half // 4), (half // 4, half // 2), (half // 2, half)):
        @pl.when((live > low) & (live <= high))
        def _():
            attend_rows(rows_ref, high, keys_ref, ones_ref, tails_ref, pl.multiple_of(seg * half, half))

    @pl.when(seg == NEED - 1)
    def _():
        lane = lax.broadcasted_iota(jnp.int32, (1, width), 1)
        target = jnp.full((1, width), -1, jnp.int32)
        for g in range(NEED):
            inner = lane - g * half
            here = (inner >= 0) & (inner < plan_ref[3 * count + g] - half)
            target = jnp.where(here, plan_ref[3 * count + NEED + g] + inner, target)

        def pack(n, carry):
            low = pl.multiple_of(n * half, half)
            row = lax.broadcasted_iota(jnp.int32, (half, width), 0) + low
            pick = jnp.where(row == target, 1.0, 0.0).astype(BF16)
            out_ref[pl.ds(low, half), :] = jnp.dot(pick, tails_ref[...], preferred_element_type=F32).astype(BF16)
            return carry

        lax.fori_loop(0, out_ref.shape[0] // half, pack, 0)


def columns(info_ref, line):
    me = info_ref[0]
    upper = me >= line // 2
    pair = jnp.where(upper, 5 - me, 1 - me)
    return me, pair, jnp.where(upper, 1, 2), jnp.where(upper, 0, 3)


def from_afar(info_ref, line, middle_ref, ends_ref, k):
    me = info_ref[0]
    rows = middle_ref.shape[0] // 2
    part = pl.ds(k * rows, rows)
    return jnp.where((me == 0) | (me == line - 1), ends_ref[part, :], middle_ref[part, :])


def project_kernel(info_ref, *refs):
    *chunks, w_ref, out_ref = refs
    depth = chunks[0].shape[1]
    line = w_ref.shape[0] // depth
    total = None
    for k, at in enumerate(columns(info_ref, line)):
        if k < 2:
            pieces = [c[...] for c in chunks[k::4]]
        else:
            pieces = [from_afar(info_ref, line, m, e, k - 2) for m, e in zip(chunks[2::4], chunks[3::4])]
        x = pieces[0] if len(pieces) == 1 else jnp.concatenate(pieces, axis=0)
        w = w_ref[pl.ds(pl.multiple_of(at * depth, depth), depth), :]
        y = jnp.dot(x, w, preferred_element_type=F32)
        total = y if total is None else total + y
    out_ref[...] = total.astype(out_ref.dtype)


def pick_rows(plan_ref, pick_ref, segs, tails):
    rows, width = pick_ref.shape
    count = rows // QLEN
    per = count // NEED
    half = per * QLEN // 2
    sub = lax.broadcasted_iota(jnp.int32, (QLEN, 1), 0)
    lane = lax.broadcasted_iota(jnp.int32, (QLEN, width), 1)
    first = segs[0] if segs else 0

    def step(p, carry):
        seg = p // per
        at = plan_ref[count + p] + sub
        head = jnp.where((seg >= first) & (seg < first + len(segs)), at + (seg - first) * half, -1)
        tail = at + (len(segs) - 1) * half + plan_ref[3 * count + NEED + seg] if tails else jnp.full_like(at, -1)
        at = jnp.where(at < half, head, tail)
        at = jnp.where(sub < plan_ref[2 * count + p], at, -1)
        block = pl.ds(pl.multiple_of(plan_ref[p] * QLEN, QLEN), QLEN)
        pick_ref[block, :] = jnp.where(lane == at, 1.0, 0.0).astype(BF16)
        return carry

    lax.fori_loop(0, count, step, 0, unroll=2)


def over_rows(out_ref, body):
    tall = out_ref.shape[0] // 2

    def step(n, carry):
        rows = pl.ds(pl.multiple_of(n * tall, tall), tall)
        out_ref[rows, :] = body(rows).astype(out_ref.dtype)
        return carry

    lax.fori_loop(0, 2, step, 0)


def place_kernel(segs, plan_ref, *refs):
    *compact, out_ref, pick_ref = refs

    @pl.when(pl.program_id(0) == 0)
    def _():
        pick_rows(plan_ref, pick_ref, segs, False)

    y = jnp.concatenate([c[...] for c in compact], axis=0)
    over_rows(out_ref, lambda rows: jnp.dot(pick_ref[rows, :], y, preferred_element_type=F32))


def begin_kernel(segs, info_ref, plan_ref, own3_ref, other3_ref, own_ref, other_ref, w_ref, out_ref, pick_ref):
    @pl.when(pl.program_id(0) == 0)
    def _():
        pick_rows(plan_ref, pick_ref, segs, True)

    depth = own_ref.shape[1]
    upper = info_ref[0] % 2
    total = None
    for x_refs, at in (((own3_ref, own_ref), upper), ((other3_ref, other_ref), 1 - upper)):
        x = jnp.concatenate([r[...] for r in x_refs], axis=0)
        w = w_ref[pl.ds(pl.multiple_of(at * depth, depth), depth), :]
        y = jnp.dot(x, w, preferred_element_type=F32)
        total = y if total is None else total + y
    out_ref[...] = total


def finish_kernel(info_ref, *refs):
    *far, pick_ref, begun_ref, placed_ref, w_ref, out_ref, x_ref = refs
    depth = far[0].shape[1]
    line = 2 * (w_ref.shape[0] // depth)
    places = columns(info_ref, line)[2:]

    @pl.when(pl.program_id(0) == 0)
    def _():
        low = 0
        for middle_ref, ends_ref in zip(far[0::2], far[1::2]):
            high = low + middle_ref.shape[0] // 2
            for k in range(2):
                x_ref[k, low:high, :] = from_afar(info_ref, line, middle_ref, ends_ref, k)
            low = high

    y = begun_ref[...]
    for k, at in enumerate(places):
        w = w_ref[pl.ds(pl.multiple_of(at % 2 * depth, depth), depth), :]
        y = y + jnp.dot(x_ref[k], w, preferred_element_type=F32)
    y = y.astype(BF16)

    def body(rows):
        return placed_ref[rows, :].astype(F32) + jnp.dot(pick_ref[rows, :], y, preferred_element_type=F32)

    over_rows(out_ref, body)


SMEM = pl.BlockSpec(memory_space=pltpu.SMEM)
VMEM = pl.BlockSpec(memory_space=pltpu.VMEM)


def on_device_line(queries, kv_cache, question_slot, question_len, out_weight):
    row_count, col_count = queries.shape
    count = row_count // QLEN
    seg_rows = row_count // NEED
    half = seg_rows // 2
    image = kv_cache[0]
    tokens, dim = image.shape[0], image.shape[1] // 2
    heads = col_count // dim
    out_cols = out_weight.shape[1]
    line = lax.axis_size("tensor")
    ring = lax.axis_size("serve")
    info = jnp.stack([lax.axis_index("tensor"), lax.axis_index("serve") % 2]).astype(jnp.int32)

    kv_two = lax.ppermute(image, "serve", [(i, (i + 2) % ring) for i in range(ring)])
    kv_mix = lax.ppermute(image, "serve", [(i, i + 1) if i % 2 == 0 else (i, (i + 3) % ring) for i in range(ring)])
    params = pltpu.CompilerParams(vmem_limit_bytes=40 * MIB)
    plan_size = 3 * count + 2 * NEED + 8

    def cost(micros):
        return pl.CostEstimate(flops=int(micros * 0.3e9), bytes_accessed=image.size, transcendentals=0)

    scratch = [
        pltpu.VMEM((dim, tokens), BF16),
        pltpu.VMEM((tokens, 2 * dim), BF16),
        pltpu.VMEM((half, col_count), BF16),
    ]
    plan, head_up, head_low = pl.pallas_call(
        first_kernel,
        out_shape=(
            jax.ShapeDtypeStruct((plan_size,), jnp.int32),
            jax.ShapeDtypeStruct((half // 2, col_count), BF16),
            jax.ShapeDtypeStruct((half // 2, col_count), BF16),
        ),
        in_specs=[SMEM, SMEM, SMEM, VMEM, VMEM],
        out_specs=(SMEM, VMEM, VMEM),
        scratch_shapes=[pltpu.SMEM((2 * NEED,), jnp.int32)] + scratch + [pltpu.VMEM((half, col_count), BF16)],
        compiler_params=params,
        cost_estimate=cost(5),
        name="first_head",
    )(info, question_slot, question_len, queries, image)

    def resident(*arrays):
        return [pl.BlockSpec(a.shape, lambda n: (0, 0)) for a in arrays]

    def head(seg, key_value):
        return pl.pallas_call(
            functools.partial(head_kernel, seg),
            out_shape=jax.ShapeDtypeStruct((half, col_count), BF16),
            in_specs=[SMEM, VMEM, VMEM],
            out_specs=VMEM,
            scratch_shapes=scratch,
            compiler_params=params,
            cost_estimate=cost(3),
            name="head",
        )(plan, queries, key_value)

    def tails(rows, *key_values):
        return pl.pallas_call(
            tails_kernel,
            out_shape=jax.ShapeDtypeStruct((rows, col_count), BF16),
            grid=(NEED,),
            in_specs=[SMEM] + resident(queries, *key_values),
            out_specs=pl.BlockSpec((rows, col_count), lambda n: (0, 0)),
            scratch_shapes=[pltpu.VMEM((NEED * half, col_count), BF16)] + scratch,
            compiler_params=params,
            cost_estimate=cost(8),
            name="tails",
        )(plan, queries, *key_values)

    def paired(chunk):
        return chunk, lax.ppermute(chunk, "tensor", [(i, i ^ 1) for i in range(line)])

    def crossed(chunk):
        both = jnp.concatenate(chunk, axis=0)
        return *chunk, lax.ppermute(both, "tensor", [(1, 2), (2, 1)])

    def ended(chunk):
        return *chunk, lax.ppermute(chunk[2], "tensor", [(1, 0), (2, 3)])

    tile = min(512, out_cols)
    steps = (out_cols // tile,)
    w_spec = pl.BlockSpec((out_weight.shape[0], tile), lambda n: (0, n))

    def tiled(rows):
        return pl.BlockSpec((rows, tile), lambda n: (0, n))

    def project(*chunks):
        arrays = [a for c in chunks for a in c]
        rows = sum(c[0].shape[0] for c in chunks)
        return pl.pallas_call(
            project_kernel,
            out_shape=jax.ShapeDtypeStruct((rows, out_cols), BF16),
            grid=steps,
            in_specs=[SMEM] + resident(*arrays) + [w_spec],
            out_specs=tiled(rows),
            compiler_params=params,
            cost_estimate=cost(10),
            name="project",
        )(info, *arrays, out_weight)

    def half_weight(far, tile):
        def index(n, info_ref):
            upper = info_ref[0] // (line // 2)
            return 1 - upper if far else upper, n

        return pl.BlockSpec((out_weight.shape[0] // 2, tile), index)

    def with_info(tile, in_specs, out_specs, scratch_shapes=()):
        return pltpu.PrefetchScalarGridSpec(
            num_scalar_prefetch=1, grid=(out_cols // tile,), in_specs=in_specs, out_specs=out_specs, scratch_shapes=scratch_shapes)

    def fixed(*arrays):
        return [pl.BlockSpec(a.shape, lambda n, info_ref: (0, 0)) for a in arrays]

    def strip(rows, tile):
        return pl.BlockSpec((rows, tile), lambda n, info_ref: (0, n))

    def place(segs, *compact):
        return pl.pallas_call(
            functools.partial(place_kernel, segs),
            out_shape=jax.ShapeDtypeStruct((row_count, out_cols), BF16),
            grid=steps,
            in_specs=[SMEM] + [tiled(c.shape[0]) for c in compact],
            out_specs=tiled(row_count),
            scratch_shapes=[pltpu.VMEM((row_count, sum(c.shape[0] for c in compact)), BF16)],
            compiler_params=params,
            cost_estimate=cost(5),
            name="place",
        )(plan, *compact)

    def begin(segs, own3, other3, own, other):
        rows = own3.shape[0] + own.shape[0]
        width = len(segs) * half + own.shape[0]
        return pl.pallas_call(
            functools.partial(begin_kernel, segs),
            out_shape=(
                jax.ShapeDtypeStruct((rows, out_cols), F32),
                jax.ShapeDtypeStruct((row_count, width), BF16),
            ),
            grid_spec=with_info(
                tile,
                [SMEM] + fixed(own3, other3, own, other) + [half_weight(False, tile)],
                (strip(rows, tile), pl.BlockSpec((row_count, width), lambda n, info_ref: (0, 0))),
            ),
            compiler_params=params,
            cost_estimate=cost(5),
            name="begin",
        )(info, plan, own3, other3, own, other, out_weight)

    def finish(far, pick, begun, placed):
        rows = begun.shape[0]
        return pl.pallas_call(
            finish_kernel,
            out_shape=jax.ShapeDtypeStruct((row_count, out_cols), BF16),
            grid_spec=with_info(
                tile,
                fixed(*far, pick)
                + [strip(rows, tile), strip(row_count, tile), half_weight(True, tile)],
                strip(row_count, tile),
                [pltpu.VMEM((2, rows, col_count), BF16)],
            ),
            compiler_params=params,
            cost_estimate=cost(7),
            name="finish",
        )(info, *far, pick, begun, placed, out_weight)

    def after(value, other):
        return lax.optimization_barrier((value, other))[0]

    up, low = crossed(paired(head_up)), paired(head_low)
    kv_two, low, _ = lax.optimization_barrier((kv_two, low, up[2]))
    kv_swap = lax.ppermute(kv_two, "serve", [(i, i ^ 1) for i in range(ring)])
    low = crossed(low)
    up = ended(up)
    chunk1 = paired(head(1, kv_two))
    kv_mix = after(kv_mix, (chunk1[1], low[2]))
    low = ended(low)
    chunk1 = crossed((chunk1[0], after(chunk1[1], up[3])))
    chunk2 = paired(head(2, kv_mix))
    head3 = head(3, kv_swap)
    chunk1 = ended((*chunk1[:2], after(chunk1[2], head3)))
    chunk2 = crossed((chunk2[0], after(chunk2[1], (low[3], head3))))
    chunk3 = crossed(paired(head3))
    rest = tails(NEED * half, image, kv_two, after(kv_mix, chunk3[1]), kv_swap)
    early = half * 7 // 4
    rest_pair = paired(rest[:early])
    chunk2 = ended((*chunk2[:2], after(chunk2[2], rest)))
    live_rest = plan[3 * count + 2 * NEED]
    sizes = [int(half * k) // 4 for k in (5.5, 7, 9, 16)]

    def branch(size, rest, rest_pair, up, low, chunk1, chunk2, chunk3):
        own, other = rest_pair
        if size > early:
            own, other = [
                jnp.concatenate(pieces, axis=0) for pieces in zip(rest_pair, paired(rest[early:size]))]
        own, other = own[:size], other[:size]
        cut = size // 32 * 16
        first = crossed((own[:cut], other[:cut]))[2]
        last = crossed((own[cut:], other[cut:]))[2]
        chunk3 = ended(chunk3)
        begun, pick = begin((3,), *chunk3[:2], own, other)
        first = after(first, (begun, chunk3[3]))
        done = project((after(up[0], first), *up[1:]), low, chunk1, chunk2)
        first = ended((own, other, first))
        last = ended((own, other, after(last, (first[3], done))))
        far = [*chunk3[2:], *first[2:], *last[2:]]
        return finish(far, pick, begun, place((0, 1, 2), done))

    index = sum([(live_rest > s).astype(jnp.int32) for s in sizes[:-1]])
    branches = [functools.partial(branch, s) for s in sizes]
    return lax.switch(index, branches, rest, rest_pair, up, low, chunk1, chunk2, chunk3)


def solution(mesh):
    plain = mesh.shape["tensor"] == KVH == 4 and mesh.shape["serve"] % 2 == 0 and NEED == 4
    return jax.shard_map(
        on_device_line if plain else on_device_general,
        mesh=mesh,
        in_specs=(
            P("serve", "tensor"),
            P("serve", "tensor", None),
            P("serve"),
            P("serve"),
            P(None, "tensor"),
        ),
        out_specs=P("serve", "tensor"),
        check_vma=False,
    )
```

```python
import functools

import jax
import jax.numpy as jnp
from jax import lax
from jax.experimental import pallas as pl
from jax.experimental.pallas import tpu as pltpu
from jax.sharding import PartitionSpec as P

KVH = 4
P_SIZE = 1600
QLEN = 32
NEED = 4
LOG2E = 1.4426950408889634
MIB = 1 << 20
F32 = jnp.float32
BF16 = jnp.bfloat16


def swapped(shard, axis, bit):
    return lax.ppermute(shard, axis, [(i, i ^ 1 << bit) for i in range(lax.axis_size(axis))])


def shifted(value, axis, steps):
    count = lax.axis_size(axis)
    pairs = [(source, (source + steps) % count) for source in range(count)]
    return lax.ppermute(value, axis, pairs)


def attend(query_rows, key_value):
    row_count = query_rows.shape[0]
    head_count = key_value.shape[0]
    head_dim = key_value.shape[2] // 2
    grouped = query_rows.reshape(row_count, head_count, -1, head_dim)
    key_part = key_value[:, :, :head_dim]
    value_part = key_value[:, :, head_dim:]
    scores = jnp.einsum(
        "rkgd,kpd->kgrp", grouped, key_part, preferred_element_type=jnp.float32
    ) * head_dim ** (-0.5)
    row_max = jnp.max(scores, axis=3, keepdims=True)
    exp_scores = jnp.exp(scores - row_max)
    sum_exp = jnp.sum(exp_scores, axis=3, keepdims=True)
    weights = (exp_scores / sum_exp).astype(jnp.bfloat16)
    blended = jnp.einsum("kgrp,kpd->rkgd", weights, value_part, preferred_element_type=jnp.float32)
    return blended.reshape(row_count, -1)


def on_device_general(queries, kv_cache, question_slot, question_len, out_weight):
    row_count, col_count = queries.shape
    head_dim = kv_cache.shape[2] // 2
    question_count = row_count // QLEN
    per_slot = question_count // NEED
    head_piece = kv_cache[0]
    sharing = lax.axis_size("tensor") // KVH
    if sharing > 1:
        for bit_number in range(sharing.bit_length() - 1):
            partner_piece = swapped(head_piece, "tensor", bit_number)
            upper_member = lax.axis_index("tensor") // 2**bit_number % 2 == 1
            head_piece = jnp.where(
                upper_member,
                jnp.concatenate([partner_piece, head_piece], axis=0),
                jnp.concatenate([head_piece, partner_piece], axis=0),
            )
    key_value = head_piece.reshape(-1, P_SIZE, 2 * head_dim)
    ordering = jnp.argsort(question_slot, stable=True)
    inverse_order = jnp.argsort(ordering, stable=True)
    sorted_rows = queries.reshape(question_count, QLEN, col_count)[ordering]
    sorted_rows = sorted_rows.reshape(NEED, per_slot * QLEN, col_count)
    results = []
    for offset_back in range(NEED):
        if offset_back == 0:
            remote = key_value
        else:
            remote = shifted(key_value, "serve", offset_back)
        results.append(attend(sorted_rows[offset_back], remote))
    sorted_out = jnp.stack(results).reshape(question_count, QLEN, col_count)
    blended = sorted_out[inverse_order].reshape(row_count, col_count)
    token_pos = jnp.arange(row_count, dtype=jnp.int32) % QLEN
    live_rows = token_pos < jnp.repeat(question_len, QLEN, total_repeat_length=row_count)
    attended = jnp.where(live_rows[:, None], blended, 0.0).astype(jnp.bfloat16)
    zero_sum = jnp.zeros((row_count, out_weight.shape[1]), jnp.float32)
    gathered_cols = lax.all_gather(attended, "tensor", axis=1, tiled=True)
    weight_rows = lax.slice_in_dim(out_weight, 0, gathered_cols.shape[1], axis=0)
    answers = zero_sum + jnp.dot(gathered_cols, weight_rows, preferred_element_type=jnp.float32)
    return answers.astype(jnp.bfloat16)


def make_plan(info_ref, slot_ref, len_ref, plan_ref, work_ref):
    count = slot_ref.shape[0]
    per = count // NEED
    half = per * QLEN // 2
    odd = info_ref[1]
    for g in range(NEED):
        work_ref[g] = g * per
        work_ref[NEED + g] = 0

    def step(q, carry):
        slot = slot_ref[q]
        length = len_ref[q]
        last = jnp.where(slot == 1, 3 - odd, 2 + odd)
        seg = jnp.where(slot == 0, 0, jnp.where(slot == 2, 1, last))
        at = work_ref[seg]
        first = work_ref[NEED + seg]
        plan_ref[at] = q
        plan_ref[count + at] = first
        plan_ref[2 * count + at] = length
        work_ref[seg] = at + 1
        work_ref[NEED + seg] = first + length
        return carry

    lax.fori_loop(0, count, step, 0)
    begin = jnp.int32(0)
    for g in range(NEED):
        live = work_ref[NEED + g]
        plan_ref[3 * count + g] = live
        plan_ref[3 * count + NEED + g] = begin
        begin = begin + jnp.maximum(live - half, 0)
    plan_ref[3 * count + 2 * NEED] = begin


def segment_rows(q_ref, plan_ref, seg, low, rows):
    count = q_ref.shape[0] // QLEN
    per = count // NEED
    width = per * QLEN
    lane = lax.broadcasted_iota(jnp.int32, (1, width), 1)
    owner = lane // QLEN
    inner = lane % QLEN
    first = jnp.zeros((1, width), jnp.int32)
    length = jnp.zeros((1, width), jnp.int32)
    blocks = []
    for k in range(per):
        q = plan_ref[seg * per + k]
        blocks.append(q_ref[pl.ds(pl.multiple_of(q * QLEN, QLEN), QLEN), :])
        first = jnp.where(owner == k, plan_ref[count + seg * per + k], first)
        length = jnp.where(owner == k, plan_ref[2 * count + seg * per + k], length)
    target = jnp.where(inner < length, first + inner, -1)
    row = lax.broadcasted_iota(jnp.int32, (rows, width), 0) + low
    pick = jnp.where(row == target, 1.0, 0.0).astype(BF16)
    return jnp.dot(pick, jnp.concatenate(blocks, axis=0), preferred_element_type=F32).astype(BF16)


def load_image(kv_ref, keys_ref, ones_ref):
    dim = kv_ref.shape[1] // 2
    keys_ref[...] = kv_ref[:, :dim].T
    ones_ref[:, :dim] = kv_ref[:, dim:]
    ones_ref[:, dim:] = jnp.ones((kv_ref.shape[0], dim), BF16)


def attend_rows(rows_ref, rows, keys_ref, ones_ref, out_ref, base):
    dim = keys_ref.shape[0]
    heads = rows_ref.shape[1] // dim
    group = max(1, min(heads, 256 // rows))

    def step(n, carry):
        places = [pl.ds(pl.multiple_of((n * group + i) * dim, dim), dim) for i in range(group)]
        q = [rows_ref[:rows, cols] for cols in places]
        q = q[0] if len(q) == 1 else jnp.concatenate(q, axis=0)
        s = jnp.dot(q, keys_ref[...], preferred_element_type=F32)
        top = jnp.max(s, axis=1, keepdims=True)
        e = jnp.exp2((s - top) * (LOG2E * dim ** (-0.5))).astype(BF16)
        o = jnp.dot(e, ones_ref[...], preferred_element_type=F32)
        o = (o[:, :dim] / o[:, dim:]).astype(BF16)
        for i, cols in enumerate(places):
            out_ref[pl.ds(base, rows), cols] = o[i * rows:(i + 1) * rows, :]
        return carry

    steps = heads // group
    lax.fori_loop(0, steps, step, 0, unroll=min(steps, 2))


def first_kernel(info_ref, slot_ref, len_ref, q_ref, kv_ref, plan_ref, up_ref, low_ref, work_ref, keys_ref, ones_ref,
                 rows_ref, both_ref):
    make_plan(info_ref, slot_ref, len_ref, plan_ref, work_ref)
    load_image(kv_ref, keys_ref, ones_ref)
    rows = up_ref.shape[0]
    rows_ref[...] = segment_rows(q_ref, plan_ref, 0, 0, 2 * rows)
    attend_rows(rows_ref, 2 * rows, keys_ref, ones_ref, both_ref, 0)
    up_ref[...] = both_ref[:rows, :]
    low_ref[...] = both_ref[rows:, :]


def head_kernel(seg, plan_ref, q_ref, kv_ref, out_ref, keys_ref, ones_ref, rows_ref):
    load_image(kv_ref, keys_ref, ones_ref)
    rows_ref[...] = segment_rows(q_ref, plan_ref, seg, 0, out_ref.shape[0])
    attend_rows(rows_ref, out_ref.shape[0], keys_ref, ones_ref, out_ref, 0)


def tails_kernel(plan_ref, q_ref, kv0_ref, kv1_ref, kv2_ref, kv3_ref, out_ref, tails_ref, keys_ref, ones_ref,
                 rows_ref):
    count = q_ref.shape[0] // QLEN
    width = tails_ref.shape[0]
    half = width // NEED
    seg = pl.program_id(0)
    live = plan_ref[3 * count + seg] - half

    @pl.when(seg == 0)
    def _():
        tails_ref[...] = jnp.zeros(tails_ref.shape, tails_ref.dtype)

    for g, kv_ref in enumerate((kv0_ref, kv1_ref, kv2_ref, kv3_ref)):
        @pl.when((seg == g) & (live > 0))
        def _():
            load_image(kv_ref, keys_ref, ones_ref)

    @pl.when(live > 0)
    def _():
        rows_ref[...] = segment_rows(q_ref, plan_ref, seg, half, half)

    for low, high in ((0, half // 4), (half // 4, half // 2), (half // 2, half)):
        @pl.when((live > low) & (live <= high))
        def _():
            attend_rows(rows_ref, high, keys_ref, ones_ref, tails_ref, pl.multiple_of(seg * half, half))

    @pl.when(seg == NEED - 1)
    def _():
        lane = lax.broadcasted_iota(jnp.int32, (1, width), 1)
        target = jnp.full((1, width), -1, jnp.int32)
        for g in range(NEED):
            inner = lane - g * half
            here = (inner >= 0) & (inner < plan_ref[3 * count + g] - half)
            target = jnp.where(here, plan_ref[3 * count + NEED + g] + inner, target)

        def pack(n, carry):
            low = pl.multiple_of(n * half, half)
            row = lax.broadcasted_iota(jnp.int32, (half, width), 0) + low
            pick = jnp.where(row == target, 1.0, 0.0).astype(BF16)
            out_ref[pl.ds(low, half), :] = jnp.dot(pick, tails_ref[...], preferred_element_type=F32).astype(BF16)
            return carry

        lax.fori_loop(0, out_ref.shape[0] // half, pack, 0)


def columns(info_ref, line):
    me = info_ref[0]
    upper = me >= line // 2
    pair = jnp.where(upper, 5 - me, 1 - me)
    return me, pair, jnp.where(upper, 1, 2), jnp.where(upper, 0, 3)


def from_afar(info_ref, line, middle_ref, ends_ref, k):
    me = info_ref[0]
    rows = middle_ref.shape[0] // 2
    part = pl.ds(k * rows, rows)
    return jnp.where((me == 0) | (me == line - 1), ends_ref[part, :], middle_ref[part, :])


def project_kernel(info_ref, *refs):
    *chunks, w_ref, out_ref = refs
    depth = chunks[0].shape[1]
    line = w_ref.shape[0] // depth
    total = None
    for k, at in enumerate(columns(info_ref, line)):
        if k < 2:
            pieces = [c[...] for c in chunks[k::4]]
        else:
            pieces = [from_afar(info_ref, line, m, e, k - 2) for m, e in zip(chunks[2::4], chunks[3::4])]
        x = pieces[0] if len(pieces) == 1 else jnp.concatenate(pieces, axis=0)
        w = w_ref[pl.ds(pl.multiple_of(at * depth, depth), depth), :]
        y = jnp.dot(x, w, preferred_element_type=F32)
        total = y if total is None else total + y
    out_ref[...] = total.astype(out_ref.dtype)


def pick_rows(plan_ref, pick_ref, segs, tails):
    rows, width = pick_ref.shape
    count = rows // QLEN
    per = count // NEED
    half = per * QLEN // 2
    sub = lax.broadcasted_iota(jnp.int32, (QLEN, 1), 0)
    lane = lax.broadcasted_iota(jnp.int32, (QLEN, width), 1)
    first = segs[0] if segs else 0

    def step(p, carry):
        seg = p // per
        at = plan_ref[count + p] + sub
        head = jnp.where((seg >= first) & (seg < first + len(segs)), at + (seg - first) * half, -1)
        tail = at + (len(segs) - 1) * half + plan_ref[3 * count + NEED + seg] if tails else jnp.full_like(at, -1)
        at = jnp.where(at < half, head, tail)
        at = jnp.where(sub < plan_ref[2 * count + p], at, -1)
        block = pl.ds(pl.multiple_of(plan_ref[p] * QLEN, QLEN), QLEN)
        pick_ref[block, :] = jnp.where(lane == at, 1.0, 0.0).astype(BF16)
        return carry

    lax.fori_loop(0, count, step, 0, unroll=2)


def over_rows(out_ref, body):
    tall = out_ref.shape[0] // 2

    def step(n, carry):
        rows = pl.ds(pl.multiple_of(n * tall, tall), tall)
        out_ref[rows, :] = body(rows).astype(out_ref.dtype)
        return carry

    lax.fori_loop(0, 2, step, 0)


def place_kernel(segs, plan_ref, *refs):
    *compact, out_ref, pick_ref = refs

    @pl.when(pl.program_id(0) == 0)
    def _():
        pick_rows(plan_ref, pick_ref, segs, False)

    y = jnp.concatenate([c[...] for c in compact], axis=0)
    over_rows(out_ref, lambda rows: jnp.dot(pick_ref[rows, :], y, preferred_element_type=F32))


def begin_kernel(segs, info_ref, plan_ref, own3_ref, other3_ref, own_ref, other_ref, w_ref, out_ref, pick_ref):
    @pl.when(pl.program_id(0) == 0)
    def _():
        pick_rows(plan_ref, pick_ref, segs, True)

    depth = own_ref.shape[1]
    upper = info_ref[0] % 2
    total = None
    for x_refs, at in (((own3_ref, own_ref), upper), ((other3_ref, other_ref), 1 - upper)):
        x = jnp.concatenate([r[...] for r in x_refs], axis=0)
        w = w_ref[pl.ds(pl.multiple_of(at * depth, depth), depth), :]
        y = jnp.dot(x, w, preferred_element_type=F32)
        total = y if total is None else total + y
    out_ref[...] = total


def finish_kernel(info_ref, middle3_ref, ends3_ref, middle_ref, ends_ref, pick_ref, begun_ref, placed_ref, w_ref,
                  out_ref, x_ref):
    depth = middle_ref.shape[1]
    line = 2 * (w_ref.shape[0] // depth)
    places = columns(info_ref, line)[2:]

    @pl.when(pl.program_id(0) == 0)
    def _():
        low = middle3_ref.shape[0] // 2
        for k in range(2):
            x_ref[k, :low, :] = from_afar(info_ref, line, middle3_ref, ends3_ref, k)
            x_ref[k, low:, :] = from_afar(info_ref, line, middle_ref, ends_ref, k)

    y = begun_ref[...]
    for k, at in enumerate(places):
        w = w_ref[pl.ds(pl.multiple_of(at % 2 * depth, depth), depth), :]
        y = y + jnp.dot(x_ref[k], w, preferred_element_type=F32)
    y = y.astype(BF16)

    def body(rows):
        return placed_ref[rows, :].astype(F32) + jnp.dot(pick_ref[rows, :], y, preferred_element_type=F32)

    over_rows(out_ref, body)


SMEM = pl.BlockSpec(memory_space=pltpu.SMEM)
VMEM = pl.BlockSpec(memory_space=pltpu.VMEM)


def on_device_line(queries, kv_cache, question_slot, question_len, out_weight):
    row_count, col_count = queries.shape
    count = row_count // QLEN
    seg_rows = row_count // NEED
    half = seg_rows // 2
    image = kv_cache[0]
    tokens, dim = image.shape[0], image.shape[1] // 2
    heads = col_count // dim
    out_cols = out_weight.shape[1]
    line = lax.axis_size("tensor")
    ring = lax.axis_size("serve")
    info = jnp.stack([lax.axis_index("tensor"), lax.axis_index("serve") % 2]).astype(jnp.int32)

    kv_two = lax.ppermute(image, "serve", [(i, (i + 2) % ring) for i in range(ring)])
    kv_mix = lax.ppermute(image, "serve", [(i, i + 1) if i % 2 == 0 else (i, (i + 3) % ring) for i in range(ring)])
    params = pltpu.CompilerParams(vmem_limit_bytes=40 * MIB)
    plan_size = 3 * count + 2 * NEED + 8

    def cost(micros):
        return pl.CostEstimate(flops=int(micros * 0.3e9), bytes_accessed=image.size, transcendentals=0)

    scratch = [
        pltpu.VMEM((dim, tokens), BF16),
        pltpu.VMEM((tokens, 2 * dim), BF16),
        pltpu.VMEM((half, col_count), BF16),
    ]
    plan, head_up, head_low = pl.pallas_call(
        first_kernel,
        out_shape=(
            jax.ShapeDtypeStruct((plan_size,), jnp.int32),
            jax.ShapeDtypeStruct((half // 2, col_count), BF16),
            jax.ShapeDtypeStruct((half // 2, col_count), BF16),
        ),
        in_specs=[SMEM, SMEM, SMEM, VMEM, VMEM],
        out_specs=(SMEM, VMEM, VMEM),
        scratch_shapes=[pltpu.SMEM((2 * NEED,), jnp.int32)] + scratch + [pltpu.VMEM((half, col_count), BF16)],
        compiler_params=params,
        cost_estimate=cost(5),
        name="first_head",
    )(info, question_slot, question_len, queries, image)

    def resident(*arrays):
        return [pl.BlockSpec(a.shape, lambda n: (0, 0)) for a in arrays]

    def head(seg, key_value):
        return pl.pallas_call(
            functools.partial(head_kernel, seg),
            out_shape=jax.ShapeDtypeStruct((half, col_count), BF16),
            in_specs=[SMEM, VMEM, VMEM],
            out_specs=VMEM,
            scratch_shapes=scratch,
            compiler_params=params,
            cost_estimate=cost(3),
            name="head",
        )(plan, queries, key_value)

    def tails(rows, *key_values):
        return pl.pallas_call(
            tails_kernel,
            out_shape=jax.ShapeDtypeStruct((rows, col_count), BF16),
            grid=(NEED,),
            in_specs=[SMEM] + resident(queries, *key_values),
            out_specs=pl.BlockSpec((rows, col_count), lambda n: (0, 0)),
            scratch_shapes=[pltpu.VMEM((NEED * half, col_count), BF16)] + scratch,
            compiler_params=params,
            cost_estimate=cost(8),
            name="tails",
        )(plan, queries, *key_values)

    def paired(chunk):
        return chunk, lax.ppermute(chunk, "tensor", [(i, i ^ 1) for i in range(line)])

    def crossed(chunk):
        both = jnp.concatenate(chunk, axis=0)
        return *chunk, lax.ppermute(both, "tensor", [(1, 2), (2, 1)])

    def ended(chunk):
        return *chunk, lax.ppermute(chunk[2], "tensor", [(1, 0), (2, 3)])

    tile = min(512, out_cols)
    steps = (out_cols // tile,)
    w_spec = pl.BlockSpec((out_weight.shape[0], tile), lambda n: (0, n))

    def tiled(rows):
        return pl.BlockSpec((rows, tile), lambda n: (0, n))

    def project(*chunks):
        arrays = [a for c in chunks for a in c]
        rows = sum(c[0].shape[0] for c in chunks)
        return pl.pallas_call(
            project_kernel,
            out_shape=jax.ShapeDtypeStruct((rows, out_cols), BF16),
            grid=steps,
            in_specs=[SMEM] + resident(*arrays) + [w_spec],
            out_specs=tiled(rows),
            compiler_params=params,
            cost_estimate=cost(10),
            name="project",
        )(info, *arrays, out_weight)

    def half_weight(far, tile):
        def index(n, info_ref):
            upper = info_ref[0] // (line // 2)
            return 1 - upper if far else upper, n

        return pl.BlockSpec((out_weight.shape[0] // 2, tile), index)

    def with_info(tile, in_specs, out_specs, scratch_shapes=()):
        return pltpu.PrefetchScalarGridSpec(
            num_scalar_prefetch=1, grid=(out_cols // tile,), in_specs=in_specs, out_specs=out_specs, scratch_shapes=scratch_shapes)

    def fixed(*arrays):
        return [pl.BlockSpec(a.shape, lambda n, info_ref: (0, 0)) for a in arrays]

    def strip(rows, tile):
        return pl.BlockSpec((rows, tile), lambda n, info_ref: (0, n))

    def place(segs, *compact):
        return pl.pallas_call(
            functools.partial(place_kernel, segs),
            out_shape=jax.ShapeDtypeStruct((row_count, out_cols), BF16),
            grid=steps,
            in_specs=[SMEM] + [tiled(c.shape[0]) for c in compact],
            out_specs=tiled(row_count),
            scratch_shapes=[pltpu.VMEM((row_count, sum(c.shape[0] for c in compact)), BF16)],
            compiler_params=params,
            cost_estimate=cost(5),
            name="place",
        )(plan, *compact)

    def begin(segs, own3, other3, own, other):
        rows = own3.shape[0] + own.shape[0]
        width = len(segs) * half + own.shape[0]
        return pl.pallas_call(
            functools.partial(begin_kernel, segs),
            out_shape=(
                jax.ShapeDtypeStruct((rows, out_cols), F32),
                jax.ShapeDtypeStruct((row_count, width), BF16),
            ),
            grid_spec=with_info(
                tile,
                [SMEM] + fixed(own3, other3, own, other) + [half_weight(False, tile)],
                (strip(rows, tile), pl.BlockSpec((row_count, width), lambda n, info_ref: (0, 0))),
            ),
            compiler_params=params,
            cost_estimate=cost(5),
            name="begin",
        )(info, plan, own3, other3, own, other, out_weight)

    def finish(middle3, ends3, middle, ends, pick, begun, placed):
        rows = begun.shape[0]
        return pl.pallas_call(
            finish_kernel,
            out_shape=jax.ShapeDtypeStruct((row_count, out_cols), BF16),
            grid_spec=with_info(
                tile,
                fixed(middle3, ends3, middle, ends, pick)
                + [strip(rows, tile), strip(row_count, tile), half_weight(True, tile)],
                strip(row_count, tile),
                [pltpu.VMEM((2, rows, col_count), BF16)],
            ),
            compiler_params=params,
            cost_estimate=cost(7),
            name="finish",
        )(info, middle3, ends3, middle, ends, pick, begun, placed, out_weight)

    def after(value, other):
        return lax.optimization_barrier((value, other))[0]

    up, low = crossed(paired(head_up)), paired(head_low)
    kv_two, low, _ = lax.optimization_barrier((kv_two, low, up[2]))
    kv_swap = lax.ppermute(kv_two, "serve", [(i, i ^ 1) for i in range(ring)])
    low = crossed(low)
    up = ended(up)
    chunk1 = paired(head(1, kv_two))
    kv_mix = after(kv_mix, (chunk1[1], low[2]))
    low = ended(low)
    chunk1 = crossed((chunk1[0], after(chunk1[1], up[3])))
    chunk2 = paired(head(2, kv_mix))
    head3 = head(3, kv_swap)
    chunk1 = ended((*chunk1[:2], after(chunk1[2], head3)))
    chunk2 = crossed((chunk2[0], after(chunk2[1], (low[3], head3))))
    chunk3 = crossed(paired(head3))
    rest = tails(NEED * half, image, kv_two, after(kv_mix, chunk3[1]), kv_swap)
    early = half * 2
    rest_pair = paired(rest[:early])
    chunk2 = ended((*chunk2[:2], after(chunk2[2], rest)))
    live_rest = plan[3 * count + 2 * NEED]
    sizes = [int(half * k) // 4 for k in (5, 6.5, 8, 9.5, 16)]

    def branch(size, rest, rest_pair, up, low, chunk1, chunk2, chunk3):
        own, other = rest_pair
        if size > early:
            own, other = [
                jnp.concatenate(pieces, axis=0) for pieces in zip(rest_pair, paired(rest[early:size]))]
        own, other, middle = crossed((own[:size], other[:size]))
        own3, other3, middle3, ends3 = ended(chunk3)
        done = project(up, low, chunk1, chunk2)
        middle = after(middle, (ends3, done))
        own, other, middle, ends = ended((own, other, middle))
        begun, pick = begin((3,), own3, other3, own, other)
        return finish(middle3, ends3, middle, ends, pick, begun, place((0, 1, 2), done))

    index = sum([(live_rest > s).astype(jnp.int32) for s in sizes[:-1]])
    branches = [functools.partial(branch, s) for s in sizes]
    return lax.switch(index, branches, rest, rest_pair, up, low, chunk1, chunk2, chunk3)


def solution(mesh):
    plain = mesh.shape["tensor"] == KVH == 4 and mesh.shape["serve"] % 2 == 0 and NEED == 4
    return jax.shard_map(
        on_device_line if plain else on_device_general,
        mesh=mesh,
        in_specs=(
            P("serve", "tensor"),
            P("serve", "tensor", None),
            P("serve"),
            P("serve"),
            P(None, "tensor"),
        ),
        out_specs=P("serve", "tensor"),
        check_vma=False,
    )
```
